32 devices in a mesh: view: 8 (over z, y), tok: 4 (over x, core).
Axes of the slice: x: 2, y: 2, z: 4, core: 2. Of those that a mesh axis runs over, the one named last changes fastest.
Arguments:
- queries: bfloat16 [8, 2, 512, 1024], P('view', None, 'tok'), may hold values from -6 to 6
- keys: bfloat16 [8, 2, 512, 1024], P('view', None, 'tok'), may hold values from -6 to 6
- values: bfloat16 [8, 2, 512, 1024], P('view', None, 'tok'), may hold values from -6 to 6
- tile_mask: int32 [8, 2, 4, 4], P('view'), may hold values from 0 to 1, as said below
- offsets: int32 [8, 2], P('view'), may hold values from -2 to 2, as said below
- branch_slots: int32 [8, 2], replicated, may hold values from 0 to 1, each once within a row
Outputs:
- attended: bfloat16 [8, 2, 512, 1024], P('view', None, 'tok')
The draws below stay inside these ranges and needn't reach their ends.
Inputs may be any that keep to these rules, and one draw needn't show every extreme that they name: Each row tile_mask[v, j, t, :] holds 1 to 4 ones at consecutive tiles modulo 4; for every v and j some row holds exactly 4. `offsets`: each row holds two different values of -2, -1, 1, 2. `branch_slots`: each row is 0, 1 or 1, 0.
All inputs are finite; a program needn't handle non-finite values.
Results may differ from the reference program's by a relative error of at most 0.0049.
Values may be sent and summed in bfloat16 or wider, within the bound.
No kernel may reach another device: no remote copies, remote signals or barrier semaphores. Data moves between devices by JAX's collectives and lax.ppermute only.
A program may use at most 128 MiB of HBM per device.

```python
import jax
import jax.numpy as jnp
from jax import lax

HD = 64
HEADS = 16
TILE = 128
NB = 2
VIEWS = 8
VIEW_TOK = 512
W = 1024
KT = 4
MOST = 4


def draw_queries(key, part):
    key = jax.random.fold_in(key, 11)
    shape = (VIEWS, 2, VIEW_TOK, W)
    base = jnp.clip(jax.random.normal(key, shape), -6.0, 6.0)
    return base.astype(jnp.bfloat16)


def draw_keys(key, part):
    key = jax.random.fold_in(key, 23)
    shape = (VIEWS, 2, VIEW_TOK, W)
    base = jnp.clip(jax.random.normal(key, shape), -6.0, 6.0)
    return base.astype(jnp.bfloat16)


def draw_tile_mask(key, part):
    key = jax.random.fold_in(key, 37)
    first, second, third = jax.random.split(key, 3)
    counts = jax.random.randint(first, (VIEWS, NB, KT), 1, MOST + 1)
    full_at = jax.random.randint(second, (VIEWS, NB), 0, KT)
    counts = jnp.where(jnp.arange(KT)[None, None, :] == full_at[..., None], MOST, counts)
    start = jax.random.randint(third, (VIEWS, NB, KT), 0, KT)
    position = (jnp.arange(KT)[None, None, None, :] - start[..., None]) % KT
    return (position < counts[..., None]).astype(jnp.int32)


def draw_offsets(key, part):
    key = jax.random.fold_in(key, 51)
    view_keys = jax.random.split(key, VIEWS)
    orders = jax.vmap(lambda single: jax.random.permutation(single, 4))(view_keys)
    table = jnp.array([-2, -1, 1, 2], jnp.int32)
    return table[orders[:, :NB]]


def block_levels(own_key, dims, cuts, least, top_value):
    level = 1.0
    for axis_at, parts in cuts:
        heights = jax.random.uniform(jax.random.fold_in(jax.random.fold_in(own_key, 6), axis_at), (parts,), jnp.float32, least / len(cuts), top_value / len(cuts))
        level = level * jnp.repeat(jnp.exp(heights), dims[axis_at] // parts).reshape((-1,) + (1,) * (len(dims) - 1 - axis_at))
    return level


def scatter_about(key, extent, spread, bound, pieces=(), kind=jnp.bfloat16):
    values = spread * jax.random.normal(key, extent, jnp.float32)
    if pieces:
        values = values * block_levels(key, extent, pieces, -0.22, 0.18)
    return jnp.clip(values, -bound, bound).astype(kind)


def setup_inputs(seed: int = 0) -> dict:
    seeds = jax.random.split(jax.random.key(seed), 7)
    queries = draw_queries(jax.random.fold_in(seeds[6], 71), 0)
    keys = draw_keys(jax.random.fold_in(seeds[6], 71), 0)
    values = scatter_about(seeds[2], (VIEWS, 2, VIEW_TOK, W), 1.0, 6.0, ((0, 8), (2, 4)))
    tile_mask = draw_tile_mask(jax.random.fold_in(seeds[6], 71), 0)
    offsets = draw_offsets(jax.random.fold_in(seeds[6], 71), 0)
    branch_slots = jax.vmap(lambda own: jax.random.permutation(own, 2))(jax.random.split(seeds[5], VIEWS)).reshape((VIEWS, 2)).astype(jnp.int32)
    return dict(queries=queries, keys=keys, values=values, tile_mask=tile_mask, offsets=offsets, branch_slots=branch_slots)


NEG_SCORE = -1e30


def attend_tile(query_tile, key_block, value_block, keep_mask):
    scores = jnp.einsum("bqhd,bkhd->bhqk", query_tile, key_block) * (HD ** -0.5)
    scores = jnp.where(keep_mask[None, None, None, :], scores, NEG_SCORE)
    row_max = jnp.max(scores, axis=-1, keepdims=True)
    expo = jnp.exp(scores - row_max)
    row_total = jnp.sum(expo, axis=-1, keepdims=True)
    weights = lax.optimization_barrier((expo / row_total).astype(jnp.bfloat16)).astype(jnp.float32)
    result = jnp.einsum("bhqk,bkhd->bqhd", weights, value_block)
    return result.astype(jnp.bfloat16)


def reference(queries, keys, values, tile_mask, offsets, branch_slots):
    tile_count = jnp.sum(tile_mask, axis=-1)
    chosen = jnp.argsort(1 - tile_mask, axis=-1, stable=True)[..., :MOST].astype(jnp.int32)
    valid = jnp.arange(MOST, dtype=jnp.int32)[None, None, None, :] < tile_count[..., None]

    def view_result(view_index):
        shape5 = (2, KT, TILE, HEADS, HD)
        query_all = queries[view_index].astype(jnp.float32).reshape(shape5)
        own_keys = keys[view_index].astype(jnp.float32).reshape(shape5)
        own_values = values[view_index].astype(jnp.float32).reshape(shape5)
        other_keys = []
        other_values = []
        for member in range(NB):
            other_view = (view_index + offsets[view_index, member]) % VIEWS
            flipped = branch_slots[other_view, 0] != branch_slots[view_index, 0]
            key_other = keys[other_view]
            value_other = values[other_view]
            key_other = jnp.where(flipped, key_other[::-1], key_other)
            value_other = jnp.where(flipped, value_other[::-1], value_other)
            other_keys.append(key_other.astype(jnp.float32).reshape(shape5))
            other_values.append(value_other.astype(jnp.float32).reshape(shape5))

        def tile_result(tile_index):
            key_parts = [own_keys[:, tile_index]]
            value_parts = [own_values[:, tile_index]]
            keep_parts = [jnp.ones((TILE,), bool)]
            for member in range(NB):
                picked = chosen[view_index, member, tile_index]
                key_parts.append(other_keys[member][:, picked].reshape(2, MOST * TILE, HEADS, HD))
                value_parts.append(other_values[member][:, picked].reshape(2, MOST * TILE, HEADS, HD))
                keep_parts.append(jnp.repeat(valid[view_index, member, tile_index], TILE))
            return attend_tile(query_all[:, tile_index], jnp.concatenate(key_parts, 1),
                               jnp.concatenate(value_parts, 1), jnp.concatenate(keep_parts))

        tiles_out = lax.map(tile_result, jnp.arange(KT, dtype=jnp.int32))
        return jnp.moveaxis(tiles_out, 0, 1).reshape(2, VIEW_TOK, W)

    return lax.map(view_result, jnp.arange(VIEWS, dtype=jnp.int32))
```

```python
import functools
import math

import jax
import jax.numpy as jnp
from jax import lax
from jax.experimental import pallas as pl
from jax.experimental.pallas import tpu as pltpu
from jax.sharding import Mesh, PartitionSpec as P

HD = 64
TILE = 128
NB = 2
REACH = 2
MARK_FLOPS = (4 * 10 ** 9, 10 ** 10)
GROUP = ("sub", "tok")

NEG_SCORE = -1e30

SMEM = pl.BlockSpec(memory_space=pltpu.SMEM)
VMEM = pl.BlockSpec(memory_space=pltpu.VMEM)
ANY = pl.BlockSpec(memory_space=pl.ANY)


def after(x, *others):
    return lax.optimization_barrier((x, others))[0]


def from_plane(x, by):
    size = lax.axis_size("plane")
    return lax.ppermute(x, "plane", [((i + by) % size, i) for i in range(size)])


def exchange(x):
    return lax.all_to_all(x, GROUP, split_axis=0, concat_axis=0, tiled=True)


class Move:
    def __init__(self, array, branch, piece, planes=0, row=0, rows=TILE, pitch=TILE, to=0):
        self.array, self.branch, self.piece, self.planes = array, branch, piece, planes
        self.row, self.rows, self.pitch, self.to = row, rows, pitch, to


def slot_of(plan, slots_ref, planes, branch):
    views = slots_ref.shape[1]
    view = (lax.axis_index("plane") + planes) * plan.sub + lax.axis_index("sub") + views
    return slots_ref[branch, lax.rem(view, views)]


def pack_kernel(plan, moves, staged, slots_ref, mark_ref, *refs):
    if staged:
        *ins, out, sem, stage, stage_sem = refs
    else:
        *ins, out, sem = refs
    ways, tiles, _, _, share = out.shape
    sources = []
    for i, move in enumerate(moves):
        slot = slot_of(plan, slots_ref, move.planes, move.branch)
        for m in range(tiles):
            rows = pl.ds(m * move.pitch + move.row, move.rows)
            source = ins[move.array].at[0, slot, rows]
            if staged:
                there = stage.at[i, m, pl.ds(0, move.rows)]
                copy = pltpu.make_async_copy(source, there, stage_sem.at[i, m])
                copy.start()
                sources.append((move, m, there, copy))
            else:
                sources.append((move, m, source, None))
    for move, m, source, copy in sources:
        if copy is not None:
            copy.wait()
        for w in range(ways):
            to, lanes = pl.ds(move.to, move.rows), pl.ds(w * share, share)
            if plan.whole_lanes:
                pltpu.make_async_copy(
                    source.at[:, lanes], out.at[w, m, move.piece, to], sem
                ).start()
            else:
                out[w, m, move.piece, to] = source[:, lanes]
    if plan.whole_lanes:
        pltpu.make_async_copy(out, out, sem).wait()


def last_kernel(plan, slots_ref, x0, x1, out, sem):
    ways, tiles, _, _, share = x0.shape
    for b, x in enumerate((x0, x1)):
        slot = slot_of(plan, slots_ref, 0, b)
        for m in range(tiles):
            for w in range(ways):
                rows, lanes = pl.ds(m * TILE, TILE), pl.ds(w * share, share)
                if plan.whole_lanes:
                    pltpu.make_async_copy(x.at[w, m, 0], out.at[0, slot, rows, lanes], sem).start()
                else:
                    out[0, slot, rows, lanes] = x[w, m, 0]
    if plan.whole_lanes:
        pltpu.make_async_copy(out, out, sem).wait()


class Plan:
    def __init__(self, sub, kt, hops, share):
        self.sub, self.kt, self.hops, self.share = sub, kt, hops, share
        self.planes = 2 * hops + 1
        self.heads = share // HD
        self.rows = self.heads * TILE
        self.cols = (1 + NB * kt) * TILE
        self.pairs = sub * kt * self.rows * self.cols
        self.whole_lanes = share % 128 == 0


def fact(plan, facts, g, i):
    own_ref, other_ref = facts
    if plan.sub == 1:
        return own_ref[i]
    return jnp.where(lax.axis_index("sub") == g, own_ref[i], other_ref[i])


def start_far(plan, facts, copies_of):
    for g in range(plan.sub):
        for j in range(NB):
            at = fact(plan, facts, g, NB * plan.kt * plan.kt + j) + (plan.hops * plan.sub + g)
            tiles_at = lax.rem(at, plan.sub) * plan.kt
            for d in range(plan.planes):
                @pl.when(lax.div(at, plan.sub) == d)
                def _():
                    for copy in copies_of(g, j, d, tiles_at):
                        copy.start()


def mark_kernel(*refs):
    refs[-1][...] = jnp.zeros_like(refs[-1])


def head_of_lane(plan):
    return lax.broadcasted_iota(jnp.int32, (TILE, plan.share), 1) // HD


def split_heads(plan, q):
    if plan.heads == 1:
        return q
    block = head_of_lane(plan)
    return jnp.concatenate([jnp.where(block == h, q, 0) for h in range(plan.heads)], axis=0)


def scores_of(q, k):
    return lax.dot_general(q, k, (((1,), (1,)), ((), ())), preferred_element_type=jnp.float32)


def numerators(plan, facts, g, t, own, far):
    factor = HD ** -0.5 * math.log2(math.e)
    parts = [own]
    for j in range(NB):
        for k in range(plan.kt):
            keep = fact(plan, facts, g, (j * plan.kt + t) * plan.kt + k) == 1
            bias = jnp.where(keep, 0.0, NEG_SCORE)
            parts.append(far[j][:, k * TILE:(k + 1) * TILE] + bias)
    top = functools.reduce(jnp.maximum, parts)
    top = jnp.max(top, axis=1, keepdims=True)
    return [jnp.exp2((part - top) * factor).astype(jnp.bfloat16) for part in parts]


def weigh(p, v):
    v = jnp.concatenate([v, jnp.ones_like(v)], axis=1)
    return jnp.dot(p, v, preferred_element_type=jnp.float32)


def finish(plan, total):
    result = total[:TILE]
    block = head_of_lane(plan)
    both = jnp.concatenate([block, block], axis=1)
    for h in range(1, plan.heads):
        result = jnp.where(both == h, total[h * TILE:(h + 1) * TILE], result)
    return (result[:, :plan.share] / result[:, plan.share:]).astype(jnp.bfloat16)


def far_rows(plan, buffer, g, j):
    return buffer[g, j].reshape(plan.kt * TILE, plan.share)


def attend_kernel(plan, branch, weighs, n_early, n_late, own, other, *refs):
    scores = n_early > 0
    h = plan.hops
    facts = (own, other)
    given, refs = refs[0], refs[1:]
    planes, late = refs[:n_early], refs[n_early:n_early + n_late]
    out, result, k_far, v_far, far_sem, out_sem = refs[-6:]
    mixed = given
    half = TILE // 2
    mine, low, high = pl.ds(branch * half, half), pl.ds(0, half), pl.ds(half, half)

    def values_at(d, tiles):
        return late[d].at[tiles, 0] if late else planes[d].at[tiles, 1]

    def far_copies(g, j, d, tiles_at):
        tiles = pl.ds(tiles_at, plan.kt)
        found = []
        if scores:
            found.append((mixed.at[tiles, 2 + d, mine], k_far.at[g, j, :, low]))
            found.append((planes[d].at[tiles, 0, mine], k_far.at[g, j, :, high]))
        if weighs:
            found.append((values_at(d, tiles), v_far.at[g, j]))
        return [
            pltpu.make_async_copy(src, to, far_sem.at[i, g, j]) for i, (src, to) in enumerate(found)
        ]

    start_far(plan, facts, far_copies)
    count = math.gcd(plan.kt, 4)
    rows, wide = plan.rows, plan.kt * TILE

    def some_tiles(g, t0):
        tiles = [(g * plan.kt + t0 + i, t0 + i) for i in range(count)]
        if scores:
            q = [split_heads(plan, mixed[at, branch]) for at, _ in tiles]
            k_own = [
                jnp.concatenate([mixed[at, 2 + h, mine], planes[h][at, 0, mine]], axis=0)
                for at, _ in tiles
            ]
            own_scores = [scores_of(a, b) for a, b in zip(q, k_own)]
            q = jnp.concatenate(q, axis=0)
            far = [scores_of(q, far_rows(plan, k_far, g, j)) for j in range(NB)]
            expo = [
                numerators(
                    plan, facts, g, t, own_scores[i],
                    [far[j][i * rows:(i + 1) * rows] for j in range(NB)],
                )
                for i, (_, t) in enumerate(tiles)
            ]
            if not weighs:
                for (at, _), parts in zip(tiles, expo):
                    for i, part in enumerate(parts):
                        out[at, :, i * TILE:(i + 1) * TILE] = part
                return
            expo_own = [parts[0] for parts in expo]
            expo_far = [
                jnp.concatenate([
                    jnp.concatenate(parts[1 + j * plan.kt:1 + (j + 1) * plan.kt], axis=1)
                    for parts in expo
                ], axis=0)
                for j in range(NB)
            ]
        else:
            expo_own = [given[at, :, :TILE] for at, _ in tiles]
            expo_far = [
                jnp.concatenate([
                    given[at, :, TILE + j * wide:TILE + (j + 1) * wide] for at, _ in tiles
                ], axis=0)
                for j in range(NB)
            ]
        total = sum(weigh(expo_far[j], far_rows(plan, v_far, g, j)) for j in range(NB))
        for i, (at, _) in enumerate(tiles):
            v_own = late[h][at, 0] if late else planes[h][at, 1]
            mine_too = total[i * rows:(i + 1) * rows] + weigh(expo_own[i], v_own)
            result[at, 0] = finish(plan, mine_too)

    def one_view(g, carry):
        for j in range(NB):
            for copy in far_copies(g, j, plan.hops, 0):
                copy.wait()
        if count == plan.kt:
            some_tiles(g, 0)
        else:
            def some(i, c):
                some_tiles(g, i * count)
                return c
            lax.fori_loop(0, plan.kt // count, some, 0)
        if weighs:
            tiles = pl.ds(g * plan.kt, plan.kt)
            pltpu.make_async_copy(result.at[tiles], out.at[tiles], out_sem).start()
        return carry

    lax.fori_loop(0, plan.sub, one_view, 0)
    if weighs:
        pltpu.make_async_copy(result, out, out_sem).wait()


def call(kernel, name, out_shape, in_specs, out_specs, scratch, args, flops=0, exps=0, moved=0,
         mib=8):
    return pl.pallas_call(
        kernel,
        out_shape=out_shape,
        in_specs=in_specs,
        out_specs=out_specs,
        scratch_shapes=scratch,
        compiler_params=pltpu.CompilerParams(vmem_limit_bytes=mib * 2 ** 20),
        cost_estimate=pl.CostEstimate(flops=flops, bytes_accessed=moved, transcendentals=exps),
        name=name,
    )(*args)


def local(queries, keys, values, tile_mask, offsets, branch_slots):
    sub, toks = lax.axis_size("sub"), lax.axis_size("tok")
    ways = sub * toks
    dtype = queries.dtype
    _, _, tokens, width = queries.shape
    tiles, share = tokens // TILE, width // ways
    kt = toks * tiles
    hops = -(-REACH // sub)
    plan = Plan(sub, kt, hops, share)
    shifts = [d for d in range(-hops, hops + 1) if d]
    order = range(-hops, hops + 1)
    half = TILE // 2
    size = queries.size * 2

    slots = branch_slots.T
    own = jnp.concatenate([tile_mask.reshape(-1), offsets.reshape(-1)])
    other = own
    if sub == 2:
        other = lax.ppermute(own, "sub", [(0, 1), (1, 0)])
    facts = (own, other)

    place = ANY if plan.whole_lanes else VMEM
    sem = pltpu.SemaphoreType.DMA(())

    def pack(name, arrays, moves, pieces, staged=False, mark=None):
        staged = staged and plan.whole_lanes
        scratch = [sem]
        if staged:
            scratch.append(pltpu.VMEM((len(moves), tiles, TILE, width), dtype))
            scratch.append(pltpu.SemaphoreType.DMA((len(moves), tiles)))
        return call(
            functools.partial(pack_kernel, plan, moves, staged), name,
            jax.ShapeDtypeStruct((ways, tiles, pieces, TILE, share), dtype),
            [SMEM, ANY] + [ANY if staged else VMEM] * len(arrays), place, scratch,
            (slots, slots if mark is None else mark, *arrays), moved=pieces * size,
            mib=62 if staged else 16,
        )

    def spread(x):
        return exchange(x).reshape(ways * tiles, x.shape[2], TILE, share)

    def around(x, chain=False):
        found, last = {0: x}, ()
        for d in shifts:
            found[d] = from_plane(after(x, last), d)
            last = found[d] if chain else ()
        return found

    def mark(arrays, flops):
        return call(
            mark_kernel, "mark", jax.ShapeDtypeStruct((8, 128), jnp.float32),
            [ANY] * len(arrays), VMEM, [], arrays, flops=flops,
        )

    raw = keys.reshape(1, 2, tiles, TILE, width)[:, :, :, :half].reshape(1, 2, tiles * half, width)
    raw = around(raw, chain=True)
    packed = pack(
        "first", [keys, values],
        [Move(0, b, 0, row=half, rows=half, to=b * half) for b in range(2)]
        + [Move(1, b, 1 + b) for b in range(2)], 3, staged=True,
    )
    early = spread(packed)
    arrived = mark([raw[d] for d in shifts], MARK_FLOPS[0])
    early, arrived, facts = lax.optimization_barrier((early, arrived, facts))

    planes = around(early[:, :2])
    brought = mark([planes[d] for d in shifts], MARK_FLOPS[1])
    last_values, brought = lax.optimization_barrier((early[:, 2:], brought))
    late = around(last_values)
    moves = [Move(0, 0, 0), Move(0, 1, 1)]
    for d in order:
        for b in range(2):
            moves.append(Move(
                1 + d + hops, b, 2 + d + hops, planes=d, rows=half, pitch=half, to=b * half
            ))
    packed = pack(
        "second", [queries, *[raw[d] for d in order]], moves, 2 + plan.planes, mark=arrived
    )
    mixed = spread(packed)
    planes[0] = early
    planes = [planes[d] for d in order]
    late = [late[d] for d in order]

    result = (ways * tiles, 1, TILE, share)

    def attend(name, branch, given, planes, late, weighs, out_shape):
        far = pltpu.VMEM((sub, NB, kt, TILE, share), dtype)
        ins = [given] + planes + late
        parts = (1 if planes else 0) + (1 if weighs else 0)
        return call(
            functools.partial(attend_kernel, plan, branch, weighs, len(planes), len(late)), name,
            jax.ShapeDtypeStruct(out_shape, dtype),
            [SMEM] * 2 + [VMEM] * len(ins) + [ANY], ANY if weighs else VMEM,
            [pltpu.VMEM(result, dtype), far, far, pltpu.SemaphoreType.DMA((3, sub, NB)), sem],
            (*facts, *ins, brought), flops=plan.pairs * HD * 2 * parts,
            exps=plan.pairs if planes else 0, moved=2 * size, mib=24,
        )

    def back(x):
        return exchange(x.reshape(ways, tiles, 1, TILE, share))

    x0 = back(attend("attend", 0, mixed, planes, [], True, result))
    expo = attend(
        "scores", 1, mixed, planes, [], False, (sub * kt, plan.rows, plan.cols)
    )
    x1 = back(attend("weigh", 1, expo, [], late, True, result))
    return call(
        functools.partial(last_kernel, plan), "last",
        jax.ShapeDtypeStruct(queries.shape, dtype), [SMEM, place, place], place, [sem],
        (slots, x0, x1), moved=2 * size,
    )


def solution(mesh):
    views, toks = mesh.shape["view"], mesh.shape["tok"]

    def run(queries, keys, values, tile_mask, offsets, branch_slots):
        heads = queries.shape[-1] // HD
        sub = 2 if views % 2 == 0 and heads % (2 * toks) == 0 else 1
        fine = Mesh(mesh.devices.reshape(views // sub, sub, toks), ("plane", "sub", "tok"))
        view = ("plane", "sub")
        shard = P(view, None, "tok", None)
        in_specs = (shard, shard, shard, P(view, None, None, None), P(view, None), P())
        return jax.shard_map(
            local, mesh=fine, in_specs=in_specs, out_specs=shard, check_vma=False
        )(queries, keys, values, tile_mask, offsets, branch_slots)

    return run
```

```python
import functools
import math

import jax
import jax.numpy as jnp
from jax import lax
from jax.experimental import pallas as pl
from jax.experimental.pallas import tpu as pltpu
from jax.sharding import Mesh, PartitionSpec as P

HD = 64
TILE = 128
NB = 2
REACH = 2
GROUP = ("sub", "tok")
MARK_FLOPS = 4 * 10 ** 9
EXPO_MOST = 16 * 2 ** 20

NEG_SCORE = -1e30

SMEM = pl.BlockSpec(memory_space=pltpu.SMEM)
VMEM = pl.BlockSpec(memory_space=pltpu.VMEM)
ANY = pl.BlockSpec(memory_space=pl.ANY)


def from_plane(x, by):
    size = lax.axis_size("plane")
    return lax.ppermute(x, "plane", [((i + by) % size, i) for i in range(size)])


def exchange(x):
    return lax.all_to_all(x, GROUP, split_axis=0, concat_axis=0, tiled=True)


def pack_kernel(whole_lanes, staged, moves, mark_ref, *refs):
    if staged:
        *ins, out, sem, stage, stage_sem = refs
    else:
        *ins, out, sem = refs
    ways, tiles, _, _, share = out.shape
    sources = []
    for i, (array, slot) in enumerate(moves):
        for m in range(tiles):
            source = ins[array].at[0, slot, pl.ds(m * TILE, TILE)]
            copy = None
            if staged:
                there = stage.at[i, m]
                copy = pltpu.make_async_copy(source, there, stage_sem.at[i, m])
                copy.start()
                source = there
            sources.append((i, m, source, copy))
    for i, m, source, copy in sources:
        if copy is not None:
            copy.wait()
        for w in range(ways):
            lanes = pl.ds(w * share, share)
            if whole_lanes:
                pltpu.make_async_copy(source.at[:, lanes], out.at[w, m, i], sem).start()
            else:
                out[w, m, i] = source[:, lanes]
    if whole_lanes:
        pltpu.make_async_copy(out, out, sem).wait()


def last_kernel(whole_lanes, x, out, sem):
    ways, tiles, slots, _, share = x.shape
    for s in range(slots):
        for m in range(tiles):
            for w in range(ways):
                rows, lanes = pl.ds(m * TILE, TILE), pl.ds(w * share, share)
                if whole_lanes:
                    pltpu.make_async_copy(x.at[w, m, s], out.at[0, s, rows, lanes], sem).start()
                else:
                    out[0, s, rows, lanes] = x[w, m, s]
    if whole_lanes:
        pltpu.make_async_copy(out, out, sem).wait()


def mark_kernel(*refs):
    refs[-1][...] = jnp.zeros_like(refs[-1])


class Plan:
    def __init__(self, sub, kt, hops, share):
        self.sub, self.kt, self.hops, self.share = sub, kt, hops, share
        self.planes = 2 * hops + 1
        self.heads = share // HD
        self.rows = self.heads * TILE
        self.cols = (1 + NB * kt) * TILE
        self.pairs = 2 * sub * kt * self.rows * self.cols
        self.whole_lanes = share % 128 == 0


def fact(plan, facts, g, i):
    own_ref, other_ref, _ = facts
    if plan.sub == 1:
        return own_ref[i]
    return jnp.where(lax.axis_index("sub") == g, own_ref[i], other_ref[i])


def start_far(plan, facts, copies_of):
    slots_ref = facts[2]
    views = slots_ref.shape[1]
    for g in range(plan.sub):
        view = lax.axis_index("plane") * plan.sub + g
        for j in range(NB):
            step = fact(plan, facts, g, NB * plan.kt * plan.kt + j)
            other = lax.rem(view + step + views, views)
            swap = jnp.where(slots_ref[0, other] == slots_ref[0, view], 0, 1)
            at = step + (plan.hops * plan.sub + g)
            tiles_at = lax.rem(at, plan.sub) * plan.kt
            for d in range(plan.planes):
                @pl.when(lax.div(at, plan.sub) == d)
                def _():
                    for copy in copies_of(g, j, d, tiles_at, swap):
                        copy.start()


def head_of_lane(plan):
    return lax.broadcasted_iota(jnp.int32, (TILE, plan.share), 1) // HD


def split_heads(plan, q):
    if plan.heads == 1:
        return q
    block = head_of_lane(plan)
    return jnp.concatenate([jnp.where(block == h, q, 0) for h in range(plan.heads)], axis=0)


def scores_of(q, k):
    return lax.dot_general(q, k, (((1,), (1,)), ((), ())), preferred_element_type=jnp.float32)


def numerators(plan, facts, g, t, own, far):
    factor = HD ** -0.5 * math.log2(math.e)
    parts = [own]
    for j in range(NB):
        for k in range(plan.kt):
            keep = fact(plan, facts, g, (j * plan.kt + t) * plan.kt + k) == 1
            bias = jnp.where(keep, 0.0, NEG_SCORE)
            parts.append(far[j][:, k * TILE:(k + 1) * TILE] + bias)
    top = functools.reduce(jnp.maximum, parts)
    top = jnp.max(top, axis=1, keepdims=True)
    return [jnp.exp2((part - top) * factor).astype(jnp.bfloat16) for part in parts]


def with_ones(v):
    return jnp.concatenate([v, jnp.ones_like(v)], axis=1)


def weigh(p, v):
    return jnp.dot(p, v, preferred_element_type=jnp.float32)


def finish(plan, total):
    result = total[:TILE]
    block = head_of_lane(plan)
    both = jnp.concatenate([block, block], axis=1)
    for h in range(1, plan.heads):
        result = jnp.where(both == h, total[h * TILE:(h + 1) * TILE], result)
    return (result[:, :plan.share] / result[:, plan.share:]).astype(jnp.bfloat16)


def attend_kernel(plan, scores, weighs, own, other, slots, *refs):
    n, h = plan.planes, plan.hops
    facts = (own, other, slots)
    refs = list(refs)
    if scores:
        q, ks = refs[0], refs[1:1 + n]
        refs = refs[1 + n:]
    if weighs:
        v0s, v1 = refs[:n], refs[n]
        refs = refs[1 + n:]
    if not scores:
        expo_ref = refs[0]
    out, result, k_far, v_far, far_sem, out_sem = refs[-6:]

    def far_copies(g, j, d, tiles_at, swap):
        tiles = pl.ds(tiles_at, plan.kt)
        found = []
        for s in range(2):
            here = swap if s == 0 else 1 - swap
            if scores:
                found.append((ks[d].at[tiles, s], k_far.at[g, j, here], 0, here))
            if weighs:
                src = v0s[d].at[tiles, 0] if s == 0 else v1.at[tiles, d]
                found.append((src, v_far.at[g, j, here], 1, here))
        return [
            pltpu.make_async_copy(src, to, far_sem.at[i, g, j, here]) for src, to, i, here in found
        ]

    start_far(plan, facts, far_copies)
    count = math.gcd(plan.kt, 4)
    wide = plan.kt * TILE

    def one_tile(s, g, t, k, v):
        at = g * plan.kt + t
        if scores:
            expo = split_heads(plan, q[at, s])
            expo = numerators(
                plan, facts, g, t, scores_of(expo, ks[h][at, s]),
                [scores_of(expo, k[j]) for j in range(NB)],
            )
            if not weighs:
                for i, part in enumerate(expo):
                    out[s, at, :, i * TILE:(i + 1) * TILE] = part
                return
            expo_own = expo[0]
            expo_far = [
                jnp.concatenate(expo[1 + j * plan.kt:1 + (j + 1) * plan.kt], axis=1)
                for j in range(NB)
            ]
        else:
            expo_own = expo_ref[s, at, :, :TILE]
            expo_far = [
                expo_ref[s, at, :, TILE + j * wide:TILE + (j + 1) * wide] for j in range(NB)
            ]
        total = weigh(expo_own, with_ones(jnp.where(s == 0, v0s[h][at, 0], v1[at, h])))
        for j in range(NB):
            total += weigh(expo_far[j], v[j])
        result[at, s] = finish(plan, total)

    def some_tiles(s, g, t0):
        def rows(buffer, j):
            return buffer[g, j, s].reshape(wide, plan.share)

        k = [rows(k_far, j) for j in range(NB)] if scores else None
        v = [with_ones(rows(v_far, j)) for j in range(NB)] if weighs else None
        for i in range(count):
            one_tile(s, g, t0 + i, k, v)

    def one_view(i, carry):
        s, g = lax.div(i, plan.sub), lax.rem(i, plan.sub)
        for j in range(NB):
            kinds = ([(0, k_far)] if scores else []) + ([(1, v_far)] if weighs else [])
            for kind, buffer in kinds:
                there = buffer.at[g, j, s]
                pltpu.make_async_copy(there, there, far_sem.at[kind, g, j, s]).wait()
        if count == plan.kt:
            some_tiles(s, g, 0)
        else:
            def some(t, c):
                some_tiles(s, g, t * count)
                return c
            lax.fori_loop(0, plan.kt // count, some, 0)
        if weighs:
            tiles = pl.ds(g * plan.kt, plan.kt)
            pltpu.make_async_copy(result.at[tiles, s], out.at[tiles, s], out_sem).start()
        return carry

    lax.fori_loop(0, 2 * plan.sub, one_view, 0)
    if weighs:
        pltpu.make_async_copy(result, out, out_sem).wait()


def call(kernel, name, out_shape, in_specs, out_specs, scratch, args, flops=0, exps=0, moved=0,
         mib=8):
    return pl.pallas_call(
        kernel,
        out_shape=out_shape,
        in_specs=in_specs,
        out_specs=out_specs,
        scratch_shapes=scratch,
        compiler_params=pltpu.CompilerParams(vmem_limit_bytes=mib * 2 ** 20),
        cost_estimate=pl.CostEstimate(flops=flops, bytes_accessed=moved, transcendentals=exps),
        name=name,
    )(*args)


def local(queries, keys, values, tile_mask, offsets, branch_slots):
    sub, toks = lax.axis_size("sub"), lax.axis_size("tok")
    ways = sub * toks
    dtype = queries.dtype
    _, _, tokens, width = queries.shape
    tiles, share = tokens // TILE, width // ways
    kt = toks * tiles
    hops = -(-REACH // sub)
    plan = Plan(sub, kt, hops, share)
    order = list(range(-hops, hops + 1))
    shifts = [d for d in order if d]
    size = queries.size * 2

    slots = branch_slots.T
    own = jnp.concatenate([tile_mask.reshape(-1), offsets.reshape(-1)])
    other = own
    if sub == 2:
        other = lax.ppermute(own, "sub", [(0, 1), (1, 0)])
    facts = (own, other, slots)

    place = ANY if plan.whole_lanes else VMEM
    sem = pltpu.SemaphoreType.DMA(())

    def pack(name, arrays, moves, mark, staged=False):
        staged = staged and plan.whole_lanes
        scratch = [sem]
        if staged:
            scratch.append(pltpu.VMEM((len(moves), tiles, TILE, width), dtype))
            scratch.append(pltpu.SemaphoreType.DMA((len(moves), tiles)))
        return call(
            functools.partial(pack_kernel, plan.whole_lanes, staged, moves), name,
            jax.ShapeDtypeStruct((ways, tiles, len(moves), TILE, share), dtype),
            [ANY] + [ANY if staged else VMEM] * len(arrays), place, scratch, (mark, *arrays),
            moved=len(moves) * size, mib=62 if staged else 16,
        )

    def spread(x):
        return exchange(x).reshape(ways * tiles, x.shape[2], TILE, share)

    def around(x, chain=False):
        found, last = {0: x}, ()
        for d in shifts:
            found[d] = from_plane(lax.optimization_barrier((x, last))[0], d)
            last = found[d] if chain else ()
        return [found[d] for d in order]

    raw = around(values[:, 1:], chain=True)
    keys = spread(pack("first", [keys], [(0, 0), (0, 1)], slots, staged=True))
    keys, raw = lax.optimization_barrier((keys, raw))

    planes = around(keys)
    arrived = call(
        mark_kernel, "mark", jax.ShapeDtypeStruct((8, 128), jnp.float32),
        [ANY] * plan.planes, VMEM, [], planes, flops=MARK_FLOPS,
    )
    mixed = spread(pack("second", [queries, values], [(0, 0), (0, 1), (1, 0)], keys))

    packed = pack("third", raw, [(i, 0) for i in range(plan.planes)], slots)
    packed, mixed = lax.optimization_barrier((packed, mixed))
    late = spread(packed)
    v_planes = around(mixed[:, 2:])

    result = (ways * tiles, 2, TILE, share)
    far = pltpu.VMEM((sub, NB, 2, kt, TILE, share), dtype)

    def attend(name, scores, weighs, ins, out_shape, rest=()):
        return call(
            functools.partial(attend_kernel, plan, scores, weighs), name,
            jax.ShapeDtypeStruct(out_shape, dtype),
            [SMEM] * 3 + [VMEM] * len(ins) + [ANY] * len(rest), ANY if weighs else VMEM,
            [pltpu.VMEM(result, dtype), far, far, pltpu.SemaphoreType.DMA((2, sub, NB, 2)), sem],
            (*facts, *ins, *rest), exps=plan.pairs if weighs else 0, moved=size, mib=28,
        )

    ins_k, ins_v = [mixed, *planes], [*v_planes, late]
    if plan.pairs * 2 <= EXPO_MOST:
        shape = (2, sub * kt, plan.rows, plan.cols)
        expo = attend("scores", True, False, ins_k, shape, rest=(arrived,))
        x = attend("weigh", False, True, [*ins_v, expo], result)
    else:
        x = attend("attend", True, True, [*ins_k, *ins_v], result, rest=(arrived,))
    x = exchange(x.reshape(ways, tiles, 2, TILE, share))
    return call(
        functools.partial(last_kernel, plan.whole_lanes), "last",
        jax.ShapeDtypeStruct(queries.shape, dtype), [place], place, [sem], (x,), moved=2 * size,
    )


def solution(mesh):
    views, toks = mesh.shape["view"], mesh.shape["tok"]

    def run(queries, keys, values, tile_mask, offsets, branch_slots):
        heads = queries.shape[-1] // HD
        sub = 2 if views % 2 == 0 and heads % (2 * toks) == 0 else 1
        fine = Mesh(mesh.devices.reshape(views // sub, sub, toks), ("plane", "sub", "tok"))
        view = ("plane", "sub")
        shard = P(view, None, "tok", None)
        in_specs = (shard, shard, shard, P(view, None, None, None), P(view, None), P())
        return jax.shard_map(
            local, mesh=fine, in_specs=in_specs, out_specs=shard, check_vma=False
        )(queries, keys, values, tile_mask, offsets, branch_slots)

    return run
```

```python
import functools
import math

import jax
import jax.numpy as jnp
from jax import lax
from jax.experimental import pallas as pl
from jax.experimental.pallas import tpu as pltpu
from jax.sharding import Mesh, PartitionSpec as P

HD = 64
TILE = 128
NB = 2
REACH = 2
MARK_FLOPS = (4 * 10 ** 9, 10 ** 10)
GROUP = ("sub", "tok")

NEG_SCORE = -1e30

SMEM = pl.BlockSpec(memory_space=pltpu.SMEM)
VMEM = pl.BlockSpec(memory_space=pltpu.VMEM)
ANY = pl.BlockSpec(memory_space=pl.ANY)


def after(x, *others):
    return lax.optimization_barrier((x, others))[0]


def from_plane(x, by):
    size = lax.axis_size("plane")
    return lax.ppermute(x, "plane", [((i + by) % size, i) for i in range(size)])


def exchange(x):
    return lax.all_to_all(x, GROUP, split_axis=0, concat_axis=0, tiled=True)


class Move:
    def __init__(self, array, branch, piece, planes=0, row=0, rows=TILE, pitch=TILE, to=0):
        self.array, self.branch, self.piece, self.planes = array, branch, piece, planes
        self.row, self.rows, self.pitch, self.to = row, rows, pitch, to


def slot_of(plan, slots_ref, planes, branch):
    views = slots_ref.shape[1]
    view = (lax.axis_index("plane") + planes) * plan.sub + lax.axis_index("sub") + views
    return slots_ref[branch, lax.rem(view, views)]


def pack_kernel(plan, moves, staged, slots_ref, mark_ref, *refs):
    if staged:
        *ins, out, sem, stage, stage_sem = refs
    else:
        *ins, out, sem = refs
    ways, tiles, _, _, share = out.shape
    sources = []
    for i, move in enumerate(moves):
        slot = slot_of(plan, slots_ref, move.planes, move.branch)
        for m in range(tiles):
            rows = pl.ds(m * move.pitch + move.row, move.rows)
            source = ins[move.array].at[0, slot, rows]
            if staged:
                there = stage.at[i, m, pl.ds(0, move.rows)]
                copy = pltpu.make_async_copy(source, there, stage_sem.at[i, m])
                copy.start()
                sources.append((move, m, there, copy))
            else:
                sources.append((move, m, source, None))
    for move, m, source, copy in sources:
        if copy is not None:
            copy.wait()
        for w in range(ways):
            to, lanes = pl.ds(move.to, move.rows), pl.ds(w * share, share)
            if plan.whole_lanes:
                pltpu.make_async_copy(
                    source.at[:, lanes], out.at[w, m, move.piece, to], sem
                ).start()
            else:
                out[w, m, move.piece, to] = source[:, lanes]
    if plan.whole_lanes:
        pltpu.make_async_copy(out, out, sem).wait()


def last_kernel(plan, x, out, sem):
    ways, tiles, slots, _, share = x.shape
    for s in range(slots):
        for m in range(tiles):
            for w in range(ways):
                rows, lanes = pl.ds(m * TILE, TILE), pl.ds(w * share, share)
                if plan.whole_lanes:
                    pltpu.make_async_copy(x.at[w, m, s], out.at[0, s, rows, lanes], sem).start()
                else:
                    out[0, s, rows, lanes] = x[w, m, s]
    if plan.whole_lanes:
        pltpu.make_async_copy(out, out, sem).wait()


class Plan:
    def __init__(self, sub, kt, hops, share):
        self.sub, self.kt, self.hops, self.share = sub, kt, hops, share
        self.planes = 2 * hops + 1
        self.heads = share // HD
        self.rows = self.heads * TILE
        self.cols = (1 + NB * kt) * TILE
        self.pairs = sub * kt * self.rows * self.cols
        self.whole_lanes = share % 128 == 0


def fact(plan, facts, g, i):
    own_ref, other_ref = facts
    if plan.sub == 1:
        return own_ref[i]
    return jnp.where(lax.axis_index("sub") == g, own_ref[i], other_ref[i])


def start_far(plan, facts, copies_of):
    for g in range(plan.sub):
        for j in range(NB):
            at = fact(plan, facts, g, NB * plan.kt * plan.kt + j) + (plan.hops * plan.sub + g)
            tiles_at = lax.rem(at, plan.sub) * plan.kt
            for d in range(plan.planes):
                @pl.when(lax.div(at, plan.sub) == d)
                def _():
                    for copy in copies_of(g, j, d, tiles_at):
                        copy.start()


def mark_kernel(*refs):
    refs[-1][...] = jnp.zeros_like(refs[-1])


def head_of_lane(plan):
    return lax.broadcasted_iota(jnp.int32, (TILE, plan.share), 1) // HD


def split_heads(plan, q):
    if plan.heads == 1:
        return q
    block = head_of_lane(plan)
    return jnp.concatenate([jnp.where(block == h, q, 0) for h in range(plan.heads)], axis=0)


def scores_of(q, k):
    return lax.dot_general(q, k, (((1,), (1,)), ((), ())), preferred_element_type=jnp.float32)


def numerators(plan, facts, g, t, own, far):
    factor = HD ** -0.5 * math.log2(math.e)
    parts = [own]
    for j in range(NB):
        for k in range(plan.kt):
            keep = fact(plan, facts, g, (j * plan.kt + t) * plan.kt + k) == 1
            bias = jnp.where(keep, 0.0, NEG_SCORE)
            parts.append(far[j][:, k * TILE:(k + 1) * TILE] + bias)
    top = functools.reduce(jnp.maximum, parts)
    top = jnp.max(top, axis=1, keepdims=True)
    return [jnp.exp2((part - top) * factor).astype(jnp.bfloat16) for part in parts]


def with_ones(v):
    return jnp.concatenate([v, jnp.ones_like(v)], axis=1)


def weigh(p, v):
    return jnp.dot(p, v, preferred_element_type=jnp.float32)


def finish(plan, total):
    result = total[:TILE]
    block = head_of_lane(plan)
    both = jnp.concatenate([block, block], axis=1)
    for h in range(1, plan.heads):
        result = jnp.where(both == h, total[h * TILE:(h + 1) * TILE], result)
    return (result[:, :plan.share] / result[:, plan.share:]).astype(jnp.bfloat16)


def far_rows(plan, buffer, g, j):
    return buffer[g, j].reshape(plan.kt * TILE, plan.share)


def each_view(plan, wait, one_tile, prepare):
    count = math.gcd(plan.kt, 4)

    def some_tiles(g, t0):
        ready = prepare(g)
        for i in range(count):
            one_tile(g, t0 + i, ready)

    def one_view(g, carry):
        wait(g)
        if count == plan.kt:
            some_tiles(g, 0)
        else:
            def some(i, c):
                some_tiles(g, i * count)
                return c
            lax.fori_loop(0, plan.kt // count, some, 0)
        return carry

    lax.fori_loop(0, plan.sub, one_view, 0)


def core_kernel(plan, own, other, mixed, *refs):
    n, h = plan.planes, plan.hops
    planes = refs[:n]
    out, expo_ref, k_far, v_far, k_sem, v_sem = refs[-6:]
    facts = (own, other)
    half = TILE // 2
    low, high = pl.ds(0, half), pl.ds(half, half)
    mine = [pl.ds(b * half, half) for b in range(2)]

    def far_copies(g, j, d, tiles_at):
        tiles = pl.ds(tiles_at, plan.kt)
        found = []
        for b in range(2):
            found.append((mixed.at[tiles, 2 + d, mine[b]], k_far.at[b, g, j, :, low], k_sem.at[0, b, g, j]))
            found.append((planes[d].at[tiles, 0, mine[b]], k_far.at[b, g, j, :, high], k_sem.at[1, b, g, j]))
            if b == 0:
                found.append((planes[d].at[tiles, 1], v_far.at[g, j], v_sem.at[g, j]))
        return [pltpu.make_async_copy(*copy) for copy in found]

    start_far(plan, facts, far_copies)

    def wait(b, g):
        for j in range(NB):
            for part, rows in enumerate((low, high)):
                there = k_far.at[b, g, j, :, rows]
                pltpu.make_async_copy(there, there, k_sem.at[part, b, g, j]).wait()
            if b == 0:
                there = v_far.at[g, j]
                pltpu.make_async_copy(there, there, v_sem.at[g, j]).wait()

    def expo_of(b, g, t, k):
        at = g * plan.kt + t
        q = split_heads(plan, mixed[at, b])
        k_own = jnp.concatenate([mixed[at, 2 + h, mine[b]], planes[h][at, 0, mine[b]]], axis=0)
        return numerators(
            plan, facts, g, t, scores_of(q, k_own), [scores_of(q, k[j]) for j in range(NB)]
        )

    def keys(b, g):
        return [far_rows(plan, k_far.at[b], g, j) for j in range(NB)]

    def attended(g, t, ready):
        k, v = ready
        at = g * plan.kt + t
        expo = expo_of(0, g, t, k)
        total = weigh(expo[0], with_ones(planes[h][at, 1]))
        for j in range(NB):
            p = jnp.concatenate(expo[1 + j * plan.kt:1 + (j + 1) * plan.kt], axis=1)
            total += weigh(p, v[j])
        out[at, 0] = finish(plan, total)

    def scored(g, t, k):
        for i, part in enumerate(expo_of(1, g, t, k)):
            expo_ref[g * plan.kt + t, :, i * TILE:(i + 1) * TILE] = part

    each_view(
        plan, functools.partial(wait, 0), attended,
        lambda g: (keys(0, g), [with_ones(far_rows(plan, v_far, g, j)) for j in range(NB)]),
    )
    each_view(plan, functools.partial(wait, 1), scored, functools.partial(keys, 1))


def weigh_kernel(plan, own, other, slots, expo, done, *refs):
    n, h = plan.planes, plan.hops
    late = refs[:n]
    out, v_far, far_sem = refs[-3:]

    def stored(g, b):
        return slots[b, lax.axis_index("plane") * plan.sub + g]

    def far_copies(g, j, d, tiles_at):
        src = late[d].at[pl.ds(tiles_at, plan.kt), 0]
        return [pltpu.make_async_copy(src, v_far.at[g, j], far_sem.at[g, j])]

    start_far(plan, (own, other), far_copies)
    for g in range(plan.sub):
        for t in range(plan.kt):
            out[g * plan.kt + t, stored(g, 0)] = done[g * plan.kt + t, 0]

    def wait(g):
        for j in range(NB):
            there = v_far.at[g, j]
            pltpu.make_async_copy(there, there, far_sem.at[g, j]).wait()

    def one_tile(g, t, v):
        at = g * plan.kt + t
        wide = plan.kt * TILE
        total = weigh(expo[at, :, :TILE], with_ones(late[h][at, 0]))
        for j in range(NB):
            total += weigh(expo[at, :, TILE + j * wide:TILE + (j + 1) * wide], v[j])
        out[at, stored(g, 1)] = finish(plan, total)

    each_view(
        plan, wait, one_tile,
        lambda g: [with_ones(far_rows(plan, v_far, g, j)) for j in range(NB)],
    )


def call(kernel, name, out_shape, in_specs, out_specs, scratch, args, flops=0, exps=0, moved=0,
         mib=8):
    return pl.pallas_call(
        kernel,
        out_shape=out_shape,
        in_specs=in_specs,
        out_specs=out_specs,
        scratch_shapes=scratch,
        compiler_params=pltpu.CompilerParams(vmem_limit_bytes=mib * 2 ** 20),
        cost_estimate=pl.CostEstimate(flops=flops, bytes_accessed=moved, transcendentals=exps),
        name=name,
    )(*args)


def local(queries, keys, values, tile_mask, offsets, branch_slots):
    sub, toks = lax.axis_size("sub"), lax.axis_size("tok")
    ways = sub * toks
    dtype = queries.dtype
    _, _, tokens, width = queries.shape
    tiles, share = tokens // TILE, width // ways
    kt = toks * tiles
    hops = -(-REACH // sub)
    plan = Plan(sub, kt, hops, share)
    shifts = [d for d in range(-hops, hops + 1) if d]
    order = range(-hops, hops + 1)
    half = TILE // 2
    size = queries.size * 2

    slots = branch_slots.T
    own = jnp.concatenate([tile_mask.reshape(-1), offsets.reshape(-1)])
    other = own
    if sub == 2:
        other = lax.ppermute(own, "sub", [(0, 1), (1, 0)])
    facts = (own, other)

    place = ANY if plan.whole_lanes else VMEM
    sem = pltpu.SemaphoreType.DMA(())

    def pack(name, arrays, moves, pieces, staged=False, mark=None):
        staged = staged and plan.whole_lanes
        scratch = [sem]
        if staged:
            scratch.append(pltpu.VMEM((len(moves), tiles, TILE, width), dtype))
            scratch.append(pltpu.SemaphoreType.DMA((len(moves), tiles)))
        return call(
            functools.partial(pack_kernel, plan, moves, staged), name,
            jax.ShapeDtypeStruct((ways, tiles, pieces, TILE, share), dtype),
            [SMEM, ANY] + [ANY if staged else VMEM] * len(arrays), place, scratch,
            (slots, slots if mark is None else mark, *arrays), moved=pieces * size,
            mib=62 if staged else 16,
        )

    def spread(x):
        return exchange(x).reshape(ways * tiles, x.shape[2], TILE, share)

    def around(x, chain=False):
        found, last = {0: x}, ()
        for d in shifts:
            found[d] = from_plane(after(x, last), d)
            last = found[d] if chain else ()
        return found

    def mark(arrays, flops):
        return call(
            mark_kernel, "mark", jax.ShapeDtypeStruct((8, 128), jnp.float32),
            [ANY] * len(arrays), VMEM, [], arrays, flops=flops,
        )

    raw = keys.reshape(1, 2, tiles, TILE, width)[:, :, :, :half].reshape(1, 2, tiles * half, width)
    raw = around(raw, chain=True)
    packed = pack(
        "first", [keys, values],
        [Move(0, b, 0, row=half, rows=half, to=b * half) for b in range(2)]
        + [Move(1, b, 1 + b) for b in range(2)], 3, staged=True,
    )
    early = spread(packed)
    arrived = mark([raw[d] for d in shifts], MARK_FLOPS[0])
    early, arrived, facts = lax.optimization_barrier((early, arrived, facts))

    planes = around(early[:, :2])
    brought = mark([planes[d] for d in shifts], MARK_FLOPS[1])
    last_values, brought = lax.optimization_barrier((early[:, 2:], brought))
    late = around(last_values)
    moves = [Move(0, 0, 0), Move(0, 1, 1)]
    for d in order:
        for b in range(2):
            moves.append(Move(
                1 + d + hops, b, 2 + d + hops, planes=d, rows=half, pitch=half, to=b * half
            ))
    packed = pack(
        "second", [queries, *[raw[d] for d in order]], moves, 2 + plan.planes, mark=arrived
    )
    mixed = spread(packed)
    planes[0] = early
    planes = [planes[d] for d in order]
    late = [late[d] for d in order]

    def result(n):
        return jax.ShapeDtypeStruct((ways * tiles, n, TILE, share), dtype)

    sems = pltpu.SemaphoreType.DMA
    far = (sub, NB, kt, TILE, share)
    expo = jax.ShapeDtypeStruct((sub * kt, plan.rows, plan.cols), dtype)
    out0, expo = call(
        functools.partial(core_kernel, plan), "core", (result(1), expo),
        [SMEM] * 2 + [VMEM] * (1 + plan.planes) + [ANY], (VMEM, VMEM),
        [pltpu.VMEM((2, *far), dtype), pltpu.VMEM(far, dtype), sems((2, 2, sub, NB)),
         sems((sub, NB))],
        (*facts, mixed, *planes, brought), flops=plan.pairs * HD * 6, exps=2 * plan.pairs,
        moved=2 * size, mib=24,
    )
    x = call(
        functools.partial(weigh_kernel, plan), "weigh", result(2),
        [SMEM] * 3 + [VMEM] * (2 + plan.planes), VMEM,
        [pltpu.VMEM(far, dtype), sems((sub, NB))], (*facts, slots, expo, out0, *late),
        flops=plan.pairs * HD * 2, moved=2 * size, mib=24,
    )
    x = exchange(x.reshape(ways, tiles, 2, TILE, share))
    return call(
        functools.partial(last_kernel, plan), "last",
        jax.ShapeDtypeStruct(queries.shape, dtype), [place], place, [sem], (x,),
        moved=2 * size,
    )


def solution(mesh):
    views, toks = mesh.shape["view"], mesh.shape["tok"]

    def run(queries, keys, values, tile_mask, offsets, branch_slots):
        heads = queries.shape[-1] // HD
        sub = 2 if views % 2 == 0 and heads % (2 * toks) == 0 else 1
        fine = Mesh(mesh.devices.reshape(views // sub, sub, toks), ("plane", "sub", "tok"))
        view = ("plane", "sub")
        shard = P(view, None, "tok", None)
        in_specs = (shard, shard, shard, P(view, None, None, None), P(view, None), P())
        return jax.shard_map(
            local, mesh=fine, in_specs=in_specs, out_specs=shard, check_vma=False
        )(queries, keys, values, tile_mask, offsets, branch_slots)

    return run
```

```python
import functools
import math

import jax
import jax.numpy as jnp
from jax import lax
from jax.experimental import pallas as pl
from jax.experimental.pallas import tpu as pltpu
from jax.sharding import Mesh, PartitionSpec as P

HD = 64
TILE = 128
NB = 2
REACH = 2
MARK_FLOPS = (4 * 10 ** 9, 10 ** 10)
GROUP = ("sub", "tok")

NEG_SCORE = -1e30

SMEM = pl.BlockSpec(memory_space=pltpu.SMEM)
VMEM = pl.BlockSpec(memory_space=pltpu.VMEM)
ANY = pl.BlockSpec(memory_space=pl.ANY)


def after(x, *others):
    return lax.optimization_barrier((x, others))[0]


def from_plane(x, by):
    size = lax.axis_size("plane")
    return lax.ppermute(x, "plane", [((i + by) % size, i) for i in range(size)])


def exchange(x):
    return lax.all_to_all(x, GROUP, split_axis=0, concat_axis=0, tiled=True)


class Move:
    def __init__(self, array, branch, piece, planes=0, row=0, rows=TILE, pitch=TILE, to=0):
        self.array, self.branch, self.piece, self.planes = array, branch, piece, planes
        self.row, self.rows, self.pitch, self.to = row, rows, pitch, to


def slot_of(plan, slots_ref, planes, branch):
    views = slots_ref.shape[1]
    view = (lax.axis_index("plane") + planes) * plan.sub + lax.axis_index("sub") + views
    return slots_ref[branch, lax.rem(view, views)]


def pack_kernel(plan, moves, staged, slots_ref, mark_ref, *refs):
    if staged:
        *ins, out, sem, stage, stage_sem = refs
    else:
        *ins, out, sem = refs
    ways, tiles, _, _, share = out.shape
    sources = []
    for i, move in enumerate(moves):
        slot = slot_of(plan, slots_ref, move.planes, move.branch)
        for m in range(tiles):
            rows = pl.ds(m * move.pitch + move.row, move.rows)
            source = ins[move.array].at[0, slot, rows]
            if staged:
                there = stage.at[i, m, pl.ds(0, move.rows)]
                copy = pltpu.make_async_copy(source, there, stage_sem.at[i, m])
                copy.start()
                sources.append((move, m, there, copy))
            else:
                sources.append((move, m, source, None))
    for move, m, source, copy in sources:
        if copy is not None:
            copy.wait()
        for w in range(ways):
            to, lanes = pl.ds(move.to, move.rows), pl.ds(w * share, share)
            if plan.whole_lanes:
                pltpu.make_async_copy(
                    source.at[:, lanes], out.at[w, m, move.piece, to], sem
                ).start()
            else:
                out[w, m, move.piece, to] = source[:, lanes]
    if plan.whole_lanes:
        pltpu.make_async_copy(out, out, sem).wait()


def last_kernel(plan, x, out, sem):
    ways, tiles, slots, _, share = x.shape
    for s in range(slots):
        for m in range(tiles):
            for w in range(ways):
                rows, lanes = pl.ds(m * TILE, TILE), pl.ds(w * share, share)
                if plan.whole_lanes:
                    pltpu.make_async_copy(x.at[w, m, s], out.at[0, s, rows, lanes], sem).start()
                else:
                    out[0, s, rows, lanes] = x[w, m, s]
    if plan.whole_lanes:
        pltpu.make_async_copy(out, out, sem).wait()


class Plan:
    def __init__(self, sub, kt, hops, share):
        self.sub, self.kt, self.hops, self.share = sub, kt, hops, share
        self.planes = 2 * hops + 1
        self.heads = share // HD
        self.rows = self.heads * TILE
        self.cols = (1 + NB * kt) * TILE
        self.pairs = sub * kt * self.rows * self.cols
        self.whole_lanes = share % 128 == 0


def fact(plan, facts, g, i):
    own_ref, other_ref = facts
    if plan.sub == 1:
        return own_ref[i]
    return jnp.where(lax.axis_index("sub") == g, own_ref[i], other_ref[i])


def start_far(plan, facts, copies_of):
    for g in range(plan.sub):
        for j in range(NB):
            at = fact(plan, facts, g, NB * plan.kt * plan.kt + j) + (plan.hops * plan.sub + g)
            tiles_at = lax.rem(at, plan.sub) * plan.kt
            for d in range(plan.planes):
                @pl.when(lax.div(at, plan.sub) == d)
                def _():
                    for copy in copies_of(g, j, d, tiles_at):
                        copy.start()


def mark_kernel(*refs):
    refs[-1][...] = jnp.zeros_like(refs[-1])


def head_of_lane(plan):
    return lax.broadcasted_iota(jnp.int32, (TILE, plan.share), 1) // HD


def split_heads(plan, q):
    if plan.heads == 1:
        return q
    block = head_of_lane(plan)
    return jnp.concatenate([jnp.where(block == h, q, 0) for h in range(plan.heads)], axis=0)


def scores_of(q, k):
    return lax.dot_general(q, k, (((1,), (1,)), ((), ())), preferred_element_type=jnp.float32)


def numerators(plan, facts, g, t, own, far):
    factor = HD ** -0.5 * math.log2(math.e)
    parts = [own]
    for j in range(NB):
        for k in range(plan.kt):
            keep = fact(plan, facts, g, (j * plan.kt + t) * plan.kt + k) == 1
            bias = jnp.where(keep, 0.0, NEG_SCORE)
            parts.append(far[j][:, k * TILE:(k + 1) * TILE] + bias)
    top = functools.reduce(jnp.maximum, parts)
    top = jnp.max(top, axis=1, keepdims=True)
    return [jnp.exp2((part - top) * factor).astype(jnp.bfloat16) for part in parts]


def with_ones(v):
    return jnp.concatenate([v, jnp.ones_like(v)], axis=1)


def weigh(p, v):
    return jnp.dot(p, v, preferred_element_type=jnp.float32)


def finish(plan, total):
    result = total[:TILE]
    block = head_of_lane(plan)
    both = jnp.concatenate([block, block], axis=1)
    for h in range(1, plan.heads):
        result = jnp.where(both == h, total[h * TILE:(h + 1) * TILE], result)
    return (result[:, :plan.share] / result[:, plan.share:]).astype(jnp.bfloat16)


def far_rows(plan, buffer, g, j):
    return buffer[g, j].reshape(plan.kt * TILE, plan.share)


def each_view(plan, wait, one_tile, prepare):
    count = math.gcd(plan.kt, 4)

    def some_tiles(g, t0):
        ready = prepare(g)
        for i in range(count):
            one_tile(g, t0 + i, ready)

    def one_view(g, carry):
        wait(g)
        if count == plan.kt:
            some_tiles(g, 0)
        else:
            def some(i, c):
                some_tiles(g, i * count)
                return c
            lax.fori_loop(0, plan.kt // count, some, 0)
        return carry

    lax.fori_loop(0, plan.sub, one_view, 0)


def core_kernel(plan, own, other, mixed, *refs):
    n, h = plan.planes, plan.hops
    planes = refs[:n]
    out, expo_ref, k_far, v_far, k_sem, v_sem = refs[-6:]
    facts = (own, other)
    half = TILE // 2
    low, high = pl.ds(0, half), pl.ds(half, half)
    mine = [pl.ds(b * half, half) for b in range(2)]

    def far_copies(g, j, d, tiles_at):
        tiles = pl.ds(tiles_at, plan.kt)
        found = []
        for b in range(2):
            found.append((mixed.at[tiles, 2 + d, mine[b]], k_far.at[b, g, j, :, low], k_sem.at[0, b, g, j]))
            found.append((planes[d].at[tiles, 0, mine[b]], k_far.at[b, g, j, :, high], k_sem.at[1, b, g, j]))
            if b == 0:
                found.append((planes[d].at[tiles, 1], v_far.at[g, j], v_sem.at[g, j]))
        return [pltpu.make_async_copy(*copy) for copy in found]

    start_far(plan, facts, far_copies)

    def wait(b, g):
        for j in range(NB):
            for part, rows in enumerate((low, high)):
                there = k_far.at[b, g, j, :, rows]
                pltpu.make_async_copy(there, there, k_sem.at[part, b, g, j]).wait()
            if b == 0:
                there = v_far.at[g, j]
                pltpu.make_async_copy(there, there, v_sem.at[g, j]).wait()

    def expo_of(b, g, t, k):
        at = g * plan.kt + t
        q = split_heads(plan, mixed[at, b])
        k_own = jnp.concatenate([mixed[at, 2 + h, mine[b]], planes[h][at, 0, mine[b]]], axis=0)
        return numerators(
            plan, facts, g, t, scores_of(q, k_own), [scores_of(q, k[j]) for j in range(NB)]
        )

    def keys(b, g):
        return [far_rows(plan, k_far.at[b], g, j) for j in range(NB)]

    def attended(g, t, ready):
        k, v = ready
        at = g * plan.kt + t
        expo = expo_of(0, g, t, k)
        total = weigh(expo[0], with_ones(planes[h][at, 1]))
        for j in range(NB):
            p = jnp.concatenate(expo[1 + j * plan.kt:1 + (j + 1) * plan.kt], axis=1)
            total += weigh(p, v[j])
        out[at, 0] = finish(plan, total)

    def scored(g, t, k):
        for i, part in enumerate(expo_of(1, g, t, k)):
            expo_ref[g * plan.kt + t, :, i * TILE:(i + 1) * TILE] = part

    each_view(
        plan, functools.partial(wait, 0), attended,
        lambda g: (keys(0, g), [with_ones(far_rows(plan, v_far, g, j)) for j in range(NB)]),
    )
    each_view(plan, functools.partial(wait, 1), scored, functools.partial(keys, 1))


def weigh_kernel(plan, own, other, slots, expo, done, *refs):
    n, h = plan.planes, plan.hops
    late = refs[:n]
    out, v_far, far_sem = refs[-3:]

    def stored(g, b):
        return slots[b, lax.axis_index("plane") * plan.sub + g]

    def far_copies(g, j, d, tiles_at):
        src = late[d].at[pl.ds(tiles_at, plan.kt), 0]
        return [pltpu.make_async_copy(src, v_far.at[g, j], far_sem.at[g, j])]

    start_far(plan, (own, other), far_copies)
    for g in range(plan.sub):
        for t in range(plan.kt):
            out[g * plan.kt + t, stored(g, 0)] = done[g * plan.kt + t, 0]

    def wait(g):
        for j in range(NB):
            there = v_far.at[g, j]
            pltpu.make_async_copy(there, there, far_sem.at[g, j]).wait()

    def one_tile(g, t, v):
        at = g * plan.kt + t
        wide = plan.kt * TILE
        total = weigh(expo[at, :, :TILE], with_ones(late[h][at, 0]))
        for j in range(NB):
            total += weigh(expo[at, :, TILE + j * wide:TILE + (j + 1) * wide], v[j])
        out[at, stored(g, 1)] = finish(plan, total)

    each_view(
        plan, wait, one_tile,
        lambda g: [with_ones(far_rows(plan, v_far, g, j)) for j in range(NB)],
    )


def call(kernel, name, out_shape, in_specs, out_specs, scratch, args, flops=0, exps=0, moved=0,
         mib=8):
    return pl.pallas_call(
        kernel,
        out_shape=out_shape,
        in_specs=in_specs,
        out_specs=out_specs,
        scratch_shapes=scratch,
        compiler_params=pltpu.CompilerParams(vmem_limit_bytes=mib * 2 ** 20),
        cost_estimate=pl.CostEstimate(flops=flops, bytes_accessed=moved, transcendentals=exps),
        name=name,
    )(*args)


def local(queries, keys, values, tile_mask, offsets, branch_slots):
    sub, toks = lax.axis_size("sub"), lax.axis_size("tok")
    ways = sub * toks
    dtype = queries.dtype
    _, _, tokens, width = queries.shape
    tiles, share = tokens // TILE, width // ways
    kt = toks * tiles
    hops = -(-REACH // sub)
    plan = Plan(sub, kt, hops, share)
    shifts = [d for d in range(-hops, hops + 1) if d]
    order = range(-hops, hops + 1)
    half = TILE // 2
    size = queries.size * 2

    slots = branch_slots.T
    own = jnp.concatenate([tile_mask.reshape(-1), offsets.reshape(-1)])
    other = own
    if sub == 2:
        other = lax.ppermute(own, "sub", [(0, 1), (1, 0)])
    facts = (own, other)

    place = ANY if plan.whole_lanes else VMEM
    sem = pltpu.SemaphoreType.DMA(())

    def pack(name, arrays, moves, pieces, staged=False, mark=None):
        staged = staged and plan.whole_lanes
        scratch = [sem]
        if staged:
            scratch.append(pltpu.VMEM((len(moves), tiles, TILE, width), dtype))
            scratch.append(pltpu.SemaphoreType.DMA((len(moves), tiles)))
        return call(
            functools.partial(pack_kernel, plan, moves, staged), name,
            jax.ShapeDtypeStruct((ways, tiles, pieces, TILE, share), dtype),
            [SMEM, ANY] + [ANY if staged else VMEM] * len(arrays), place, scratch,
            (slots, slots if mark is None else mark, *arrays), moved=pieces * size,
            mib=62 if staged else 16,
        )

    def spread(x):
        return exchange(x).reshape(ways * tiles, x.shape[2], TILE, share)

    def around(x, chain=False):
        found, last = {0: x}, ()
        for d in shifts:
            found[d] = from_plane(after(x, last), d)
            last = found[d] if chain else ()
        return found

    def mark(arrays, flops):
        return call(
            mark_kernel, "mark", jax.ShapeDtypeStruct((8, 128), jnp.float32),
            [ANY] * len(arrays), VMEM, [], arrays, flops=flops,
        )

    raw = keys.reshape(1, 2, tiles, TILE, width)[:, :, :, :half].reshape(1, 2, tiles * half, width)
    raw = around(raw, chain=True)
    packed = pack(
        "first", [keys, values],
        [Move(0, b, 0, row=half, rows=half, to=b * half) for b in range(2)]
        + [Move(1, b, 1 + b) for b in range(2)], 3, staged=True,
    )
    early = spread(packed)
    arrived = mark([raw[d] for d in shifts], MARK_FLOPS[0])
    early, arrived, facts = lax.optimization_barrier((early, arrived, facts))

    planes = around(early[:, :2])
    last_values, planes = lax.optimization_barrier((early[:, 2:], planes))
    brought = mark([last_values], MARK_FLOPS[1])
    last_values, brought = lax.optimization_barrier((last_values, brought))
    late = around(last_values)
    moves = [Move(0, 0, 0), Move(0, 1, 1)]
    for d in order:
        for b in range(2):
            moves.append(Move(
                1 + d + hops, b, 2 + d + hops, planes=d, rows=half, pitch=half, to=b * half
            ))
    packed = pack(
        "second", [queries, *[raw[d] for d in order]], moves, 2 + plan.planes, mark=arrived
    )
    mixed = spread(packed)
    planes[0] = early
    planes = [planes[d] for d in order]
    late = [late[d] for d in order]

    def result(n):
        return jax.ShapeDtypeStruct((ways * tiles, n, TILE, share), dtype)

    sems = pltpu.SemaphoreType.DMA
    far = (sub, NB, kt, TILE, share)
    expo = jax.ShapeDtypeStruct((sub * kt, plan.rows, plan.cols), dtype)
    out0, expo = call(
        functools.partial(core_kernel, plan), "core", (result(1), expo),
        [SMEM] * 2 + [VMEM] + [ANY if d else VMEM for d in order] + [ANY], (VMEM, VMEM),
        [pltpu.VMEM((2, *far), dtype), pltpu.VMEM(far, dtype), sems((2, 2, sub, NB)),
         sems((sub, NB))],
        (*facts, mixed, *planes, brought), flops=plan.pairs * HD * 6, exps=2 * plan.pairs,
        moved=2 * size, mib=12,
    )
    x = call(
        functools.partial(weigh_kernel, plan), "weigh", result(2),
        [SMEM] * 3 + [VMEM] * (2 + plan.planes), VMEM,
        [pltpu.VMEM(far, dtype), sems((sub, NB))], (*facts, slots, expo, out0, *late),
        flops=plan.pairs * HD * 2, moved=2 * size, mib=12,
    )
    x = exchange(x.reshape(ways, tiles, 2, TILE, share))
    return call(
        functools.partial(last_kernel, plan), "last",
        jax.ShapeDtypeStruct(queries.shape, dtype), [place], place, [sem], (x,),
        moved=2 * size,
    )


def solution(mesh):
    views, toks = mesh.shape["view"], mesh.shape["tok"]

    def run(queries, keys, values, tile_mask, offsets, branch_slots):
        heads = queries.shape[-1] // HD
        sub = 2 if views % 2 == 0 and heads % (2 * toks) == 0 else 1
        fine = Mesh(mesh.devices.reshape(views // sub, sub, toks), ("plane", "sub", "tok"))
        view = ("plane", "sub")
        shard = P(view, None, "tok", None)
        in_specs = (shard, shard, shard, P(view, None, None, None), P(view, None), P())
        return jax.shard_map(
            local, mesh=fine, in_specs=in_specs, out_specs=shard, check_vma=False
        )(queries, keys, values, tile_mask, offsets, branch_slots)

    return run
```

```python
import functools
import math

import jax
import jax.numpy as jnp
from jax import lax
from jax.experimental import pallas as pl
from jax.experimental.pallas import tpu as pltpu
from jax.sharding import Mesh, PartitionSpec as P

HD = 64
TILE = 128
NB = 2
REACH = 2
MARK_FLOPS = (4 * 10 ** 9, 10 ** 10)
GROUP = ("sub", "tok")

NEG_SCORE = -1e30

SMEM = pl.BlockSpec(memory_space=pltpu.SMEM)
VMEM = pl.BlockSpec(memory_space=pltpu.VMEM)
ANY = pl.BlockSpec(memory_space=pl.ANY)


def after(x, *others):
    return lax.optimization_barrier((x, others))[0]


def from_plane(x, by):
    size = lax.axis_size("plane")
    return lax.ppermute(x, "plane", [((i + by) % size, i) for i in range(size)])


def exchange(x):
    return lax.all_to_all(x, GROUP, split_axis=0, concat_axis=0, tiled=True)


class Move:
    def __init__(self, array, branch, piece, planes=0, row=0, rows=TILE, pitch=TILE, to=0):
        self.array, self.branch, self.piece, self.planes = array, branch, piece, planes
        self.row, self.rows, self.pitch, self.to = row, rows, pitch, to


def slot_of(plan, slots_ref, planes, branch):
    views = slots_ref.shape[1]
    view = (lax.axis_index("plane") + planes) * plan.sub + lax.axis_index("sub") + views
    return slots_ref[branch, lax.rem(view, views)]


def pack_kernel(plan, moves, staged, slots_ref, mark_ref, *refs):
    if staged:
        *ins, out, sem, stage, stage_sem = refs
    else:
        *ins, out, sem = refs
    ways, tiles, _, _, share = out.shape
    sources = []
    for i, move in enumerate(moves):
        slot = slot_of(plan, slots_ref, move.planes, move.branch)
        for m in range(tiles):
            rows = pl.ds(m * move.pitch + move.row, move.rows)
            source = ins[move.array].at[0, slot, rows]
            if staged:
                there = stage.at[i, m, pl.ds(0, move.rows)]
                copy = pltpu.make_async_copy(source, there, stage_sem.at[i, m])
                copy.start()
                sources.append((move, m, there, copy))
            else:
                sources.append((move, m, source, None))
    for move, m, source, copy in sources:
        if copy is not None:
            copy.wait()
        for w in range(ways):
            to, lanes = pl.ds(move.to, move.rows), pl.ds(w * share, share)
            if plan.whole_lanes:
                pltpu.make_async_copy(
                    source.at[:, lanes], out.at[w, m, move.piece, to], sem
                ).start()
            else:
                out[w, m, move.piece, to] = source[:, lanes]
    if plan.whole_lanes:
        pltpu.make_async_copy(out, out, sem).wait()


def last_kernel(plan, x, out, sem):
    ways, tiles, slots, _, share = x.shape
    for s in range(slots):
        for m in range(tiles):
            for w in range(ways):
                rows, lanes = pl.ds(m * TILE, TILE), pl.ds(w * share, share)
                if plan.whole_lanes:
                    pltpu.make_async_copy(x.at[w, m, s], out.at[0, s, rows, lanes], sem).start()
                else:
                    out[0, s, rows, lanes] = x[w, m, s]
    if plan.whole_lanes:
        pltpu.make_async_copy(out, out, sem).wait()


class Plan:
    def __init__(self, sub, kt, hops, share):
        self.sub, self.kt, self.hops, self.share = sub, kt, hops, share
        self.planes = 2 * hops + 1
        self.heads = share // HD
        self.rows = self.heads * TILE
        self.cols = (1 + NB * kt) * TILE
        self.pairs = sub * kt * self.rows * self.cols
        self.whole_lanes = share % 128 == 0


def fact(plan, facts, g, i):
    own_ref, other_ref = facts
    if plan.sub == 1:
        return own_ref[i]
    return jnp.where(lax.axis_index("sub") == g, own_ref[i], other_ref[i])


def start_far(plan, facts, copies_of):
    for g in range(plan.sub):
        for j in range(NB):
            at = fact(plan, facts, g, NB * plan.kt * plan.kt + j) + (plan.hops * plan.sub + g)
            tiles_at = lax.rem(at, plan.sub) * plan.kt
            for d in range(plan.planes):
                @pl.when(lax.div(at, plan.sub) == d)
                def _():
                    for copy in copies_of(g, j, d, tiles_at):
                        copy.start()


def mark_kernel(*refs):
    refs[-1][...] = jnp.zeros_like(refs[-1])


def head_of_lane(plan):
    return lax.broadcasted_iota(jnp.int32, (TILE, plan.share), 1) // HD


def split_heads(plan, q):
    if plan.heads == 1:
        return q
    block = head_of_lane(plan)
    return jnp.concatenate([jnp.where(block == h, q, 0) for h in range(plan.heads)], axis=0)


def scores_of(q, k):
    return lax.dot_general(q, k, (((1,), (1,)), ((), ())), preferred_element_type=jnp.float32)


def numerators(plan, facts, g, t, own, far):
    factor = HD ** -0.5 * math.log2(math.e)
    parts = [own]
    for j in range(NB):
        for k in range(plan.kt):
            keep = fact(plan, facts, g, (j * plan.kt + t) * plan.kt + k) == 1
            bias = jnp.where(keep, 0.0, NEG_SCORE)
            parts.append(far[j][:, k * TILE:(k + 1) * TILE] + bias)
    top = functools.reduce(jnp.maximum, parts)
    top = jnp.max(top, axis=1, keepdims=True)
    return [jnp.exp2((part - top) * factor).astype(jnp.bfloat16) for part in parts]


def with_ones(v):
    return jnp.concatenate([v, jnp.ones_like(v)], axis=1)


def weigh(p, v):
    return jnp.dot(p, v, preferred_element_type=jnp.float32)


def finish(plan, total):
    result = total[:TILE]
    block = head_of_lane(plan)
    both = jnp.concatenate([block, block], axis=1)
    for h in range(1, plan.heads):
        result = jnp.where(both == h, total[h * TILE:(h + 1) * TILE], result)
    return (result[:, :plan.share] / result[:, plan.share:]).astype(jnp.bfloat16)


def far_rows(plan, buffer, g, j):
    return buffer[g, j].reshape(plan.kt * TILE, plan.share)


def each_view(plan, wait, one_tile, prepare):
    count = math.gcd(plan.kt, 4)

    def some_tiles(g, t0):
        ready = prepare(g)
        for i in range(count):
            one_tile(g, t0 + i, ready)

    def one_view(g, carry):
        wait(g)
        if count == plan.kt:
            some_tiles(g, 0)
        else:
            def some(i, c):
                some_tiles(g, i * count)
                return c
            lax.fori_loop(0, plan.kt // count, some, 0)
        return carry

    lax.fori_loop(0, plan.sub, one_view, 0)


def first_part_kernel(plan, b, own, other, mixed, *refs):
    n, h = plan.planes, plan.hops
    planes = refs[:n]
    out, k_far, v_far, k_sem, v_sem = refs[-5:]
    facts = (own, other)
    half = TILE // 2
    low, high, mine = pl.ds(0, half), pl.ds(half, half), pl.ds(b * half, half)

    def far_copies(g, j, d, tiles_at):
        tiles = pl.ds(tiles_at, plan.kt)
        found = [
            (mixed.at[tiles, 2 + d, mine], k_far.at[g, j, :, low], k_sem.at[0, g, j]),
            (planes[d].at[tiles, 0, mine], k_far.at[g, j, :, high], k_sem.at[1, g, j]),
        ]
        if b == 0:
            found.append((planes[d].at[tiles, 1], v_far.at[g, j], v_sem.at[g, j]))
        return [pltpu.make_async_copy(*copy) for copy in found]

    start_far(plan, facts, far_copies)

    def wait(g):
        for j in range(NB):
            for part, rows in enumerate((low, high)):
                there = k_far.at[g, j, :, rows]
                pltpu.make_async_copy(there, there, k_sem.at[part, g, j]).wait()
            if b == 0:
                there = v_far.at[g, j]
                pltpu.make_async_copy(there, there, v_sem.at[g, j]).wait()

    def expo_of(g, t, k):
        at = g * plan.kt + t
        q = split_heads(plan, mixed[at, b])
        k_own = jnp.concatenate([mixed[at, 2 + h, mine], planes[h][at, 0, mine]], axis=0)
        return numerators(
            plan, facts, g, t, scores_of(q, k_own), [scores_of(q, k[j]) for j in range(NB)]
        )

    def keys(g):
        return [far_rows(plan, k_far, g, j) for j in range(NB)]

    def attended(g, t, ready):
        k, v = ready
        at = g * plan.kt + t
        expo = expo_of(g, t, k)
        total = weigh(expo[0], with_ones(planes[h][at, 1]))
        for j in range(NB):
            p = jnp.concatenate(expo[1 + j * plan.kt:1 + (j + 1) * plan.kt], axis=1)
            total += weigh(p, v[j])
        out[at, 0] = finish(plan, total)

    def scored(g, t, k):
        for i, part in enumerate(expo_of(g, t, k)):
            out[g * plan.kt + t, :, i * TILE:(i + 1) * TILE] = part

    if b == 0:
        each_view(plan, wait, attended, lambda g: (
            keys(g), [with_ones(far_rows(plan, v_far, g, j)) for j in range(NB)]
        ))
    else:
        each_view(plan, wait, scored, keys)


def weigh_kernel(plan, own, other, slots, expo, done, *refs):
    n, h = plan.planes, plan.hops
    late = refs[:n]
    out, v_far, far_sem = refs[-3:]

    def stored(g, b):
        return slots[b, lax.axis_index("plane") * plan.sub + g]

    def far_copies(g, j, d, tiles_at):
        src = late[d].at[pl.ds(tiles_at, plan.kt), 0]
        return [pltpu.make_async_copy(src, v_far.at[g, j], far_sem.at[g, j])]

    start_far(plan, (own, other), far_copies)
    for g in range(plan.sub):
        for t in range(plan.kt):
            out[g * plan.kt + t, stored(g, 0)] = done[g * plan.kt + t, 0]

    def wait(g):
        for j in range(NB):
            there = v_far.at[g, j]
            pltpu.make_async_copy(there, there, far_sem.at[g, j]).wait()

    def one_tile(g, t, v):
        at = g * plan.kt + t
        wide = plan.kt * TILE
        total = weigh(expo[at, :, :TILE], with_ones(late[h][at, 0]))
        for j in range(NB):
            total += weigh(expo[at, :, TILE + j * wide:TILE + (j + 1) * wide], v[j])
        out[at, stored(g, 1)] = finish(plan, total)

    each_view(
        plan, wait, one_tile,
        lambda g: [with_ones(far_rows(plan, v_far, g, j)) for j in range(NB)],
    )


def call(kernel, name, out_shape, in_specs, out_specs, scratch, args, flops=0, exps=0, moved=0,
         mib=8):
    return pl.pallas_call(
        kernel,
        out_shape=out_shape,
        in_specs=in_specs,
        out_specs=out_specs,
        scratch_shapes=scratch,
        compiler_params=pltpu.CompilerParams(vmem_limit_bytes=mib * 2 ** 20),
        cost_estimate=pl.CostEstimate(flops=flops, bytes_accessed=moved, transcendentals=exps),
        name=name,
    )(*args)


def local(queries, keys, values, tile_mask, offsets, branch_slots):
    sub, toks = lax.axis_size("sub"), lax.axis_size("tok")
    ways = sub * toks
    dtype = queries.dtype
    _, _, tokens, width = queries.shape
    tiles, share = tokens // TILE, width // ways
    kt = toks * tiles
    hops = -(-REACH // sub)
    plan = Plan(sub, kt, hops, share)
    shifts = [d for d in range(-hops, hops + 1) if d]
    order = range(-hops, hops + 1)
    half = TILE // 2
    size = queries.size * 2

    slots = branch_slots.T
    own = jnp.concatenate([tile_mask.reshape(-1), offsets.reshape(-1)])
    other = own
    if sub == 2:
        other = lax.ppermute(own, "sub", [(0, 1), (1, 0)])
    facts = (own, other)

    place = ANY if plan.whole_lanes else VMEM
    sem = pltpu.SemaphoreType.DMA(())

    def pack(name, arrays, moves, pieces, staged=False, mark=None):
        staged = staged and plan.whole_lanes
        scratch = [sem]
        if staged:
            scratch.append(pltpu.VMEM((len(moves), tiles, TILE, width), dtype))
            scratch.append(pltpu.SemaphoreType.DMA((len(moves), tiles)))
        return call(
            functools.partial(pack_kernel, plan, moves, staged), name,
            jax.ShapeDtypeStruct((ways, tiles, pieces, TILE, share), dtype),
            [SMEM, ANY] + [ANY if staged else VMEM] * len(arrays), place, scratch,
            (slots, slots if mark is None else mark, *arrays), moved=pieces * size,
            mib=62 if staged else 8,
        )

    def spread(x):
        return exchange(x).reshape(ways * tiles, x.shape[2], TILE, share)

    def around(x, chain=False):
        found, last = {0: x}, ()
        for d in shifts:
            found[d] = from_plane(after(x, last), d)
            last = found[d] if chain else ()
        return found

    def mark(arrays, flops):
        return call(
            mark_kernel, "mark", jax.ShapeDtypeStruct((8, 128), jnp.float32),
            [ANY] * len(arrays), VMEM, [], arrays, flops=flops, mib=1,
        )

    raw = keys.reshape(1, 2, tiles, TILE, width)[:, :, :, :half].reshape(1, 2, tiles * half, width)
    raw = around(raw, chain=True)
    packed = pack(
        "first", [keys, values],
        [Move(0, b, 0, row=half, rows=half, to=b * half) for b in range(2)]
        + [Move(1, b, 1 + b) for b in range(2)], 3, staged=True,
    )
    early = spread(packed)
    arrived = mark([raw[d] for d in shifts], MARK_FLOPS[0])
    early, arrived, facts = lax.optimization_barrier((early, arrived, facts))

    planes = around(early[:, :2])
    brought = mark([planes[d] for d in shifts], MARK_FLOPS[1])
    last_values, brought = lax.optimization_barrier((early[:, 2:], brought))
    late = around(last_values)
    moves = [Move(0, 0, 0), Move(0, 1, 1)]
    for d in order:
        for b in range(2):
            moves.append(Move(
                1 + d + hops, b, 2 + d + hops, planes=d, rows=half, pitch=half, to=b * half
            ))
    packed = pack(
        "second", [queries, *[raw[d] for d in order]], moves, 2 + plan.planes, mark=arrived
    )
    mixed = spread(packed)
    planes[0] = early
    planes = [planes[d] for d in order]
    late = [late[d] for d in order]

    def result(n):
        return jax.ShapeDtypeStruct((ways * tiles, n, TILE, share), dtype)

    sems = pltpu.SemaphoreType.DMA
    far = (sub, NB, kt, TILE, share)
    shapes = result(1), jax.ShapeDtypeStruct((sub * kt, plan.rows, plan.cols), dtype)
    out0, expo = (
        call(
            functools.partial(first_part_kernel, plan, b), ("attend", "scores")[b], shapes[b],
            [SMEM] * 2 + [VMEM] * (1 + plan.planes) + [ANY], VMEM,
            [pltpu.VMEM(far, dtype), pltpu.VMEM(far, dtype), sems((2, sub, NB)), sems((sub, NB))],
            (*facts, mixed, *planes, brought), flops=plan.pairs * HD * (4 - 2 * b),
            exps=plan.pairs, moved=2 * size, mib=12,
        ) for b in range(2)
    )
    x = call(
        functools.partial(weigh_kernel, plan), "weigh", result(2),
        [SMEM] * 3 + [VMEM] * (2 + plan.planes), VMEM,
        [pltpu.VMEM(far, dtype), sems((sub, NB))], (*facts, slots, expo, out0, *late),
        flops=plan.pairs * HD * 2, moved=2 * size, mib=12,
    )
    x = exchange(x.reshape(ways, tiles, 2, TILE, share))
    return call(
        functools.partial(last_kernel, plan), "last",
        jax.ShapeDtypeStruct(queries.shape, dtype), [place], place, [sem], (x,),
        moved=2 * size,
    )


def solution(mesh):
    views, toks = mesh.shape["view"], mesh.shape["tok"]

    def run(queries, keys, values, tile_mask, offsets, branch_slots):
        heads = queries.shape[-1] // HD
        sub = 2 if views % 2 == 0 and heads % (2 * toks) == 0 else 1
        fine = Mesh(mesh.devices.reshape(views // sub, sub, toks), ("plane", "sub", "tok"))
        view = ("plane", "sub")
        shard = P(view, None, "tok", None)
        in_specs = (shard, shard, shard, P(view, None, None, None), P(view, None), P())
        return jax.shard_map(
            local, mesh=fine, in_specs=in_specs, out_specs=shard, check_vma=False
        )(queries, keys, values, tile_mask, offsets, branch_slots)

    return run
```

```python
import functools
import math

import jax
import jax.numpy as jnp
from jax import lax
from jax.experimental import pallas as pl
from jax.experimental.pallas import tpu as pltpu
from jax.sharding import Mesh, PartitionSpec as P

HD = 64
TILE = 128
NB = 2
REACH = 2
MARK_FLOPS = (4 * 10 ** 9, 2 * 10 ** 9, 10 ** 10)
GROUP = ("sub", "tok")

NEG_SCORE = -1e30

SMEM = pl.BlockSpec(memory_space=pltpu.SMEM)
VMEM = pl.BlockSpec(memory_space=pltpu.VMEM)
ANY = pl.BlockSpec(memory_space=pl.ANY)


def after(x, *others):
    return lax.optimization_barrier((x, others))[0]


def from_plane(x, by):
    size = lax.axis_size("plane")
    return lax.ppermute(x, "plane", [((i + by) % size, i) for i in range(size)])


def exchange(x):
    return lax.all_to_all(x, GROUP, split_axis=0, concat_axis=0, tiled=True)


class Move:
    def __init__(self, array, branch, piece, planes=0, row=0, rows=TILE, pitch=TILE, to=0):
        self.array, self.branch, self.piece, self.planes = array, branch, piece, planes
        self.row, self.rows, self.pitch, self.to = row, rows, pitch, to


def slot_of(plan, slots_ref, planes, branch):
    views = slots_ref.shape[1]
    view = (lax.axis_index("plane") + planes) * plan.sub + lax.axis_index("sub") + views
    return slots_ref[branch, lax.rem(view, views)]


def pack_kernel(plan, moves, staged, slots_ref, mark_ref, *refs):
    if staged:
        *ins, out, sem, stage, stage_sem = refs
    else:
        *ins, out, sem = refs
    ways, tiles, _, _, share = out.shape
    sources = []
    for i, move in enumerate(moves):
        slot = slot_of(plan, slots_ref, move.planes, move.branch)
        for m in range(tiles):
            rows = pl.ds(m * move.pitch + move.row, move.rows)
            source = ins[move.array].at[0, slot, rows]
            if staged:
                there = stage.at[i, m, pl.ds(0, move.rows)]
                copy = pltpu.make_async_copy(source, there, stage_sem.at[i, m])
                copy.start()
                sources.append((move, m, there, copy))
            else:
                sources.append((move, m, source, None))
    for move, m, source, copy in sources:
        if copy is not None:
            copy.wait()
        for w in range(ways):
            to, lanes = pl.ds(move.to, move.rows), pl.ds(w * share, share)
            if plan.whole_lanes:
                pltpu.make_async_copy(
                    source.at[:, lanes], out.at[w, m, move.piece, to], sem
                ).start()
            else:
                out[w, m, move.piece, to] = source[:, lanes]
    if plan.whole_lanes:
        pltpu.make_async_copy(out, out, sem).wait()


def last_kernel(plan, x, out, sem):
    ways, tiles, slots, _, share = x.shape
    for s in range(slots):
        for m in range(tiles):
            for w in range(ways):
                rows, lanes = pl.ds(m * TILE, TILE), pl.ds(w * share, share)
                if plan.whole_lanes:
                    pltpu.make_async_copy(x.at[w, m, s], out.at[0, s, rows, lanes], sem).start()
                else:
                    out[0, s, rows, lanes] = x[w, m, s]
    if plan.whole_lanes:
        pltpu.make_async_copy(out, out, sem).wait()


class Plan:
    def __init__(self, sub, kt, hops, share):
        self.sub, self.kt, self.hops, self.share = sub, kt, hops, share
        self.planes = 2 * hops + 1
        self.heads = share // HD
        self.rows = self.heads * TILE
        self.cols = (1 + NB * kt) * TILE
        self.pairs = sub * kt * self.rows * self.cols
        self.whole_lanes = share % 128 == 0


def fact(plan, facts, g, i):
    own_ref, other_ref = facts
    if plan.sub == 1:
        return own_ref[i]
    return jnp.where(lax.axis_index("sub") == g, own_ref[i], other_ref[i])


def start_far(plan, facts, copies_of):
    for g in range(plan.sub):
        for j in range(NB):
            at = fact(plan, facts, g, NB * plan.kt * plan.kt + j) + (plan.hops * plan.sub + g)
            tiles_at = lax.rem(at, plan.sub) * plan.kt
            for d in range(plan.planes):
                @pl.when(lax.div(at, plan.sub) == d)
                def _():
                    for copy in copies_of(g, j, d, tiles_at):
                        copy.start()


def mark_kernel(*refs):
    refs[-1][...] = jnp.zeros_like(refs[-1])


def head_of_lane(plan):
    return lax.broadcasted_iota(jnp.int32, (TILE, plan.share), 1) // HD


def split_heads(plan, q):
    if plan.heads == 1:
        return q
    block = head_of_lane(plan)
    return jnp.concatenate([jnp.where(block == h, q, 0) for h in range(plan.heads)], axis=0)


def scores_of(q, k):
    return lax.dot_general(q, k, (((1,), (1,)), ((), ())), preferred_element_type=jnp.float32)


def numerators(plan, facts, g, t, own, far):
    factor = HD ** -0.5 * math.log2(math.e)
    parts = [own]
    for j in range(NB):
        for k in range(plan.kt):
            keep = fact(plan, facts, g, (j * plan.kt + t) * plan.kt + k) == 1
            bias = jnp.where(keep, 0.0, NEG_SCORE)
            parts.append(far[j][:, k * TILE:(k + 1) * TILE] + bias)
    top = functools.reduce(jnp.maximum, parts)
    top = jnp.max(top, axis=1, keepdims=True)
    return [jnp.exp2((part - top) * factor).astype(jnp.bfloat16) for part in parts]


def with_ones(v):
    return jnp.concatenate([v, jnp.ones_like(v)], axis=1)


def weigh(p, v):
    return jnp.dot(p, v, preferred_element_type=jnp.float32)


def finish(plan, total):
    result = total[:TILE]
    block = head_of_lane(plan)
    both = jnp.concatenate([block, block], axis=1)
    for h in range(1, plan.heads):
        result = jnp.where(both == h, total[h * TILE:(h + 1) * TILE], result)
    return (result[:, :plan.share] / result[:, plan.share:]).astype(jnp.bfloat16)


def far_rows(plan, buffer, g, j):
    return buffer[g, j].reshape(plan.kt * TILE, plan.share)


def each_view(plan, wait, one_tile, prepare):
    count = math.gcd(plan.kt, 4)

    def some_tiles(g, t0):
        ready = prepare(g)
        for i in range(count):
            one_tile(g, t0 + i, ready)

    def one_view(g, carry):
        wait(g)
        if count == plan.kt:
            some_tiles(g, 0)
        else:
            def some(i, c):
                some_tiles(g, i * count)
                return c
            lax.fori_loop(0, plan.kt // count, some, 0)
        return carry

    lax.fori_loop(0, plan.sub, one_view, 0)


def first_part_kernel(plan, b, own, other, mixed, *refs):
    n, h = plan.planes, plan.hops
    planes = refs[:n]
    out, k_far, v_far, k_sem, v_sem = refs[-5:]
    facts = (own, other)
    half = TILE // 2
    low, high, mine = pl.ds(0, half), pl.ds(half, half), pl.ds(b * half, half)

    def far_copies(g, j, d, tiles_at):
        tiles = pl.ds(tiles_at, plan.kt)
        found = [
            (mixed.at[tiles, 2 + d, mine], k_far.at[g, j, :, low], k_sem.at[0, g, j]),
            (planes[d].at[tiles, 0, mine], k_far.at[g, j, :, high], k_sem.at[1, g, j]),
        ]
        if b == 0:
            found.append((planes[d].at[tiles, 1], v_far.at[g, j], v_sem.at[g, j]))
        return [pltpu.make_async_copy(*copy) for copy in found]

    start_far(plan, facts, far_copies)

    def wait(g):
        for j in range(NB):
            for part, rows in enumerate((low, high)):
                there = k_far.at[g, j, :, rows]
                pltpu.make_async_copy(there, there, k_sem.at[part, g, j]).wait()
            if b == 0:
                there = v_far.at[g, j]
                pltpu.make_async_copy(there, there, v_sem.at[g, j]).wait()

    def expo_of(g, t, k):
        at = g * plan.kt + t
        q = split_heads(plan, mixed[at, b])
        k_own = jnp.concatenate([mixed[at, 2 + h, mine], planes[h][at, 0, mine]], axis=0)
        return numerators(
            plan, facts, g, t, scores_of(q, k_own), [scores_of(q, k[j]) for j in range(NB)]
        )

    def keys(g):
        return [far_rows(plan, k_far, g, j) for j in range(NB)]

    def attended(g, t, ready):
        k, v = ready
        at = g * plan.kt + t
        expo = expo_of(g, t, k)
        total = weigh(expo[0], with_ones(planes[h][at, 1]))
        for j in range(NB):
            p = jnp.concatenate(expo[1 + j * plan.kt:1 + (j + 1) * plan.kt], axis=1)
            total += weigh(p, v[j])
        out[at, 0] = finish(plan, total)

    def scored(g, t, k):
        for i, part in enumerate(expo_of(g, t, k)):
            out[g * plan.kt + t, :, i * TILE:(i + 1) * TILE] = part

    if b == 0:
        each_view(plan, wait, attended, lambda g: (
            keys(g), [with_ones(far_rows(plan, v_far, g, j)) for j in range(NB)]
        ))
    else:
        each_view(plan, wait, scored, keys)


def weigh_kernel(plan, own, other, slots, expo, done, *refs):
    n, h = plan.planes, plan.hops
    late = refs[:n]
    out, v_far, far_sem = refs[-3:]

    def stored(g, b):
        return slots[b, lax.axis_index("plane") * plan.sub + g]

    def far_copies(g, j, d, tiles_at):
        src = late[d].at[pl.ds(tiles_at, plan.kt), 0]
        return [pltpu.make_async_copy(src, v_far.at[g, j], far_sem.at[g, j])]

    start_far(plan, (own, other), far_copies)
    for g in range(plan.sub):
        for t in range(plan.kt):
            out[g * plan.kt + t, stored(g, 0)] = done[g * plan.kt + t, 0]

    def wait(g):
        for j in range(NB):
            there = v_far.at[g, j]
            pltpu.make_async_copy(there, there, far_sem.at[g, j]).wait()

    def one_tile(g, t, v):
        at = g * plan.kt + t
        wide = plan.kt * TILE
        total = weigh(expo[at, :, :TILE], with_ones(late[h][at, 0]))
        for j in range(NB):
            total += weigh(expo[at, :, TILE + j * wide:TILE + (j + 1) * wide], v[j])
        out[at, stored(g, 1)] = finish(plan, total)

    each_view(
        plan, wait, one_tile,
        lambda g: [with_ones(far_rows(plan, v_far, g, j)) for j in range(NB)],
    )


def call(kernel, name, out_shape, in_specs, out_specs, scratch, args, flops=0, exps=0, moved=0,
         mib=8):
    return pl.pallas_call(
        kernel,
        out_shape=out_shape,
        in_specs=in_specs,
        out_specs=out_specs,
        scratch_shapes=scratch,
        compiler_params=pltpu.CompilerParams(vmem_limit_bytes=mib * 2 ** 20),
        cost_estimate=pl.CostEstimate(flops=flops, bytes_accessed=moved, transcendentals=exps),
        name=name,
    )(*args)


def local(queries, keys, values, tile_mask, offsets, branch_slots):
    sub, toks = lax.axis_size("sub"), lax.axis_size("tok")
    ways = sub * toks
    dtype = queries.dtype
    _, _, tokens, width = queries.shape
    tiles, share = tokens // TILE, width // ways
    kt = toks * tiles
    hops = -(-REACH // sub)
    plan = Plan(sub, kt, hops, share)
    shifts = [d for d in range(-hops, hops + 1) if d]
    order = range(-hops, hops + 1)
    half = TILE // 2
    size = queries.size * 2

    slots = branch_slots.T
    own = jnp.concatenate([tile_mask.reshape(-1), offsets.reshape(-1)])
    other = own
    if sub == 2:
        other = lax.ppermute(own, "sub", [(0, 1), (1, 0)])
    facts = (own, other)

    place = ANY if plan.whole_lanes else VMEM
    sem = pltpu.SemaphoreType.DMA(())

    def pack(name, arrays, moves, pieces, staged=False, mark=None):
        staged = staged and plan.whole_lanes
        scratch = [sem]
        if staged:
            scratch.append(pltpu.VMEM((len(moves), tiles, TILE, width), dtype))
            scratch.append(pltpu.SemaphoreType.DMA((len(moves), tiles)))
        return call(
            functools.partial(pack_kernel, plan, moves, staged), name,
            jax.ShapeDtypeStruct((ways, tiles, pieces, TILE, share), dtype),
            [SMEM, ANY] + [ANY if staged else VMEM] * len(arrays), place, scratch,
            (slots, slots if mark is None else mark, *arrays), moved=pieces * size,
            mib=62 if staged else 8,
        )

    def spread(x):
        return exchange(x).reshape(ways * tiles, x.shape[2], TILE, share)

    def around(x, chain=False):
        found, last = {0: x}, ()
        for d in shifts:
            found[d] = from_plane(after(x, last), d)
            last = found[d] if chain else ()
        return found

    def mark(arrays, flops):
        return call(
            mark_kernel, "mark", jax.ShapeDtypeStruct((8, 128), jnp.float32),
            [ANY] * len(arrays), VMEM, [], arrays, flops=flops, mib=1,
        )

    raw = keys.reshape(1, 2, tiles, TILE, width)[:, :, :, :half].reshape(1, 2, tiles * half, width)
    raw = around(raw, chain=True)
    packed = pack(
        "first", [keys, values],
        [Move(0, b, 0, row=half, rows=half, to=b * half) for b in range(2)]
        + [Move(1, b, 1 + b) for b in range(2)], 3, staged=True,
    )
    early = spread(packed)
    arrived = mark([raw[d] for d in shifts], MARK_FLOPS[0])
    early, arrived, facts = lax.optimization_barrier((early, arrived, facts))

    planes = around(early[:, :2])
    leads = mark([planes[shifts[0]]], MARK_FLOPS[1])
    brought = mark([planes[d] for d in shifts[1:]], MARK_FLOPS[2])
    last_values, leads = lax.optimization_barrier((early[:, 2:], leads))
    late = around(last_values)
    moves = [Move(0, 0, 0), Move(0, 1, 1)]
    for d in order:
        for b in range(2):
            moves.append(Move(
                1 + d + hops, b, 2 + d + hops, planes=d, rows=half, pitch=half, to=b * half
            ))
    packed = pack(
        "second", [queries, *[raw[d] for d in order]], moves, 2 + plan.planes, mark=arrived
    )
    mixed = spread(packed)
    planes[0] = early
    planes = [planes[d] for d in order]
    late = [late[d] for d in order]

    def result(n):
        return jax.ShapeDtypeStruct((ways * tiles, n, TILE, share), dtype)

    sems = pltpu.SemaphoreType.DMA
    far = (sub, NB, kt, TILE, share)
    shapes = result(1), jax.ShapeDtypeStruct((sub * kt, plan.rows, plan.cols), dtype)
    out0, expo = (
        call(
            functools.partial(first_part_kernel, plan, b), ("attend", "scores")[b], shapes[b],
            [SMEM] * 2 + [VMEM] * (1 + plan.planes) + [ANY] * 2, VMEM,
            [pltpu.VMEM(far, dtype), pltpu.VMEM(far, dtype), sems((2, sub, NB)), sems((sub, NB))],
            (*facts, mixed, *planes, leads, brought), flops=plan.pairs * HD * (4 - 2 * b),
            exps=plan.pairs, moved=2 * size, mib=12,
        ) for b in range(2)
    )
    x = call(
        functools.partial(weigh_kernel, plan), "weigh", result(2),
        [SMEM] * 3 + [VMEM] * (2 + plan.planes), VMEM,
        [pltpu.VMEM(far, dtype), sems((sub, NB))], (*facts, slots, expo, out0, *late),
        flops=plan.pairs * HD * 2, moved=2 * size, mib=12,
    )
    x = exchange(x.reshape(ways, tiles, 2, TILE, share))
    return call(
        functools.partial(last_kernel, plan), "last",
        jax.ShapeDtypeStruct(queries.shape, dtype), [place], place, [sem], (x,),
        moved=2 * size,
    )


def solution(mesh):
    views, toks = mesh.shape["view"], mesh.shape["tok"]

    def run(queries, keys, values, tile_mask, offsets, branch_slots):
        heads = queries.shape[-1] // HD
        sub = 2 if views % 2 == 0 and heads % (2 * toks) == 0 else 1
        fine = Mesh(mesh.devices.reshape(views // sub, sub, toks), ("plane", "sub", "tok"))
        view = ("plane", "sub")
        shard = P(view, None, "tok", None)
        in_specs = (shard, shard, shard, P(view, None, None, None), P(view, None), P())
        return jax.shard_map(
            local, mesh=fine, in_specs=in_specs, out_specs=shard, check_vma=False
        )(queries, keys, values, tile_mask, offsets, branch_slots)

    return run
```

```python
import functools
import math

import jax
import jax.numpy as jnp
from jax import lax
from jax.experimental import pallas as pl
from jax.experimental.pallas import tpu as pltpu
from jax.sharding import Mesh, PartitionSpec as P

HD = 64
TILE = 128
NB = 2
REACH = 2
MARK_FLOPS = (4 * 10 ** 9, 2 * 10 ** 9, 10 ** 10)
GROUP = ("sub", "tok")

NEG_SCORE = -1e30

SMEM = pl.BlockSpec(memory_space=pltpu.SMEM)
VMEM = pl.BlockSpec(memory_space=pltpu.VMEM)
ANY = pl.BlockSpec(memory_space=pl.ANY)


def from_plane(x, by):
    size = lax.axis_size("plane")
    return lax.ppermute(x, "plane", [((i + by) % size, i) for i in range(size)])


def exchange(x):
    return lax.all_to_all(x, GROUP, split_axis=0, concat_axis=0, tiled=True)


class Move:
    def __init__(self, array, branch, piece, planes=0, row=0, rows=TILE, pitch=TILE, to=0):
        self.array, self.branch, self.piece, self.planes = array, branch, piece, planes
        self.row, self.rows, self.pitch, self.to = row, rows, pitch, to


def slot_of(plan, slots_ref, planes, branch):
    views = slots_ref.shape[1]
    view = (lax.axis_index("plane") + planes) * plan.sub + lax.axis_index("sub") + views
    return slots_ref[branch, lax.rem(view, views)]


def pack_kernel(plan, moves, staged, slots_ref, mark_ref, *refs):
    if staged:
        *ins, out, sem, stage, stage_sem = refs
    else:
        *ins, out, sem = refs
    ways, tiles, _, _, share = out.shape
    sources = []
    for i, move in enumerate(moves):
        slot = slot_of(plan, slots_ref, move.planes, move.branch)
        for m in range(tiles):
            rows = pl.ds(m * move.pitch + move.row, move.rows)
            source = ins[move.array].at[0, slot, rows]
            if staged:
                there = stage.at[i, m, pl.ds(0, move.rows)]
                copy = pltpu.make_async_copy(source, there, stage_sem.at[i, m])
                copy.start()
                sources.append((move, m, there, copy))
            else:
                sources.append((move, m, source, None))
    for move, m, source, copy in sources:
        if copy is not None:
            copy.wait()
        for w in range(ways):
            to, lanes = pl.ds(move.to, move.rows), pl.ds(w * share, share)
            if plan.whole_lanes:
                pltpu.make_async_copy(
                    source.at[:, lanes], out.at[w, m, move.piece, to], sem
                ).start()
            else:
                out[w, m, move.piece, to] = source[:, lanes]
    if plan.whole_lanes:
        first = min(move.piece for move in moves)
        filled = out.at[:, :, first:max(move.piece for move in moves) + 1]
        pltpu.make_async_copy(filled, filled, sem).wait()


def last_kernel(plan, x, out, sem):
    ways, tiles, slots, _, share = x.shape
    for s in range(slots):
        for m in range(tiles):
            for w in range(ways):
                rows, lanes = pl.ds(m * TILE, TILE), pl.ds(w * share, share)
                if plan.whole_lanes:
                    pltpu.make_async_copy(x.at[w, m, s], out.at[0, s, rows, lanes], sem).start()
                else:
                    out[0, s, rows, lanes] = x[w, m, s]
    if plan.whole_lanes:
        pltpu.make_async_copy(out, out, sem).wait()


class Plan:
    def __init__(self, sub, kt, hops, share):
        self.sub, self.kt, self.hops, self.share = sub, kt, hops, share
        self.planes = 2 * hops + 1
        self.heads = share // HD
        self.rows = self.heads * TILE
        self.cols = (1 + NB * kt) * TILE
        self.pairs = sub * kt * self.rows * self.cols
        self.whole_lanes = share % 128 == 0


def fact(plan, facts, g, i):
    own_ref, other_ref = facts
    if plan.sub == 1:
        return own_ref[i]
    return jnp.where(lax.axis_index("sub") == g, own_ref[i], other_ref[i])


def start_far(plan, facts, copies_of):
    for g in range(plan.sub):
        for j in range(NB):
            at = fact(plan, facts, g, NB * plan.kt * plan.kt + j) + (plan.hops * plan.sub + g)
            tiles_at = (at & (plan.sub - 1)) * plan.kt
            for d in range(plan.planes):
                @pl.when((at >> (plan.sub - 1)) == d)
                def _():
                    for copy in copies_of(g, j, d, tiles_at):
                        copy.start()


def mark_kernel(*refs):
    refs[-1][...] = jnp.zeros_like(refs[-1])


def head_of_lane(plan):
    return lax.broadcasted_iota(jnp.int32, (TILE, plan.share), 1) // HD


def split_heads(plan, q):
    if plan.heads == 1:
        return q
    block = head_of_lane(plan)
    return jnp.concatenate([jnp.where(block == h, q, 0) for h in range(plan.heads)], axis=0)


def scores_of(q, k):
    return lax.dot_general(q, k, (((1,), (1,)), ((), ())), preferred_element_type=jnp.float32)


def numerators(plan, facts, g, t, own, far):
    factor = HD ** -0.5 * math.log2(math.e)
    parts = [own]
    for j in range(NB):
        for k in range(plan.kt):
            keep = fact(plan, facts, g, (j * plan.kt + t) * plan.kt + k) == 1
            bias = jnp.where(keep, 0.0, NEG_SCORE)
            parts.append(far[j][:, k * TILE:(k + 1) * TILE] + bias)
    top = functools.reduce(jnp.maximum, parts)
    top = jnp.max(top, axis=1, keepdims=True)
    return [jnp.exp2((part - top) * factor).astype(jnp.bfloat16) for part in parts]


def with_ones(v):
    return jnp.concatenate([v, jnp.ones_like(v)], axis=1)


def weigh(p, v):
    return jnp.dot(p, v, preferred_element_type=jnp.float32)


def finish(plan, total):
    result = total[:TILE]
    block = head_of_lane(plan)
    both = jnp.concatenate([block, block], axis=1)
    for h in range(1, plan.heads):
        result = jnp.where(both == h, total[h * TILE:(h + 1) * TILE], result)
    return (result[:, :plan.share] / result[:, plan.share:]).astype(jnp.bfloat16)


def far_rows(plan, buffer, g, j):
    return buffer[g, j].reshape(plan.kt * TILE, plan.share)


def each_view(plan, wait, one_tile, prepare):
    count = math.gcd(plan.kt, 4)

    def some_tiles(g, t0):
        ready = prepare(g)
        for i in range(count):
            one_tile(g, t0 + i, ready)

    def one_view(g, carry):
        wait(g)
        if count == plan.kt:
            some_tiles(g, 0)
        else:
            def some(i, c):
                some_tiles(g, i * count)
                return c
            lax.fori_loop(0, plan.kt // count, some, 0)
        return carry

    lax.fori_loop(0, plan.sub, one_view, 0)


def first_part_kernel(plan, b, own, other, mixed, *refs):
    n, h = plan.planes, plan.hops
    planes = refs[:n]
    out, k_far, v_far, k_sem, v_sem = refs[-5:]
    facts = (own, other)
    half = TILE // 2
    low, high, mine = pl.ds(0, half), pl.ds(half, half), pl.ds(b * half, half)

    def far_copies(g, j, d, tiles_at):
        tiles = pl.ds(tiles_at, plan.kt)
        found = [
            (mixed.at[tiles, 2 + d, mine], k_far.at[g, j, :, low], k_sem.at[0, g, j]),
            (planes[d].at[tiles, 0, mine], k_far.at[g, j, :, high], k_sem.at[1, g, j]),
        ]
        if b == 0:
            found.append((planes[d].at[tiles, 1], v_far.at[g, j], v_sem.at[g, j]))
        return [pltpu.make_async_copy(*copy) for copy in found]

    start_far(plan, facts, far_copies)

    def wait(g):
        for j in range(NB):
            for part, rows in enumerate((low, high)):
                there = k_far.at[g, j, :, rows]
                pltpu.make_async_copy(there, there, k_sem.at[part, g, j]).wait()
            if b == 0:
                there = v_far.at[g, j]
                pltpu.make_async_copy(there, there, v_sem.at[g, j]).wait()

    def expo_of(g, t, k):
        at = g * plan.kt + t
        q = split_heads(plan, mixed[at, b])
        k_own = jnp.concatenate([mixed[at, 2 + h, mine], planes[h][at, 0, mine]], axis=0)
        return numerators(
            plan, facts, g, t, scores_of(q, k_own), [scores_of(q, k[j]) for j in range(NB)]
        )

    def keys(g):
        return [far_rows(plan, k_far, g, j) for j in range(NB)]

    def attended(g, t, ready):
        k, v = ready
        at = g * plan.kt + t
        expo = expo_of(g, t, k)
        total = weigh(expo[0], with_ones(planes[h][at, 1]))
        for j in range(NB):
            p = jnp.concatenate(expo[1 + j * plan.kt:1 + (j + 1) * plan.kt], axis=1)
            total += weigh(p, v[j])
        out[at, 0] = finish(plan, total)

    def scored(g, t, k):
        for i, part in enumerate(expo_of(g, t, k)):
            out[g * plan.kt + t, :, i * TILE:(i + 1) * TILE] = part

    if b == 0:
        each_view(plan, wait, attended, lambda g: (
            keys(g), [with_ones(far_rows(plan, v_far, g, j)) for j in range(NB)]
        ))
    else:
        each_view(plan, wait, scored, keys)


def weigh_kernel(plan, own, other, slots, expo, done, *refs):
    n, h = plan.planes, plan.hops
    late = refs[:n]
    out, v_far, far_sem = refs[-3:]

    def stored(g, b):
        return slots[b, lax.axis_index("plane") * plan.sub + g]

    def far_copies(g, j, d, tiles_at):
        src = late[d].at[pl.ds(tiles_at, plan.kt), 0]
        return [pltpu.make_async_copy(src, v_far.at[g, j], far_sem.at[g, j])]

    start_far(plan, (own, other), far_copies)
    for g in range(plan.sub):
        for t in range(plan.kt):
            out[g * plan.kt + t, stored(g, 0)] = done[g * plan.kt + t, 0]

    def wait(g):
        for j in range(NB):
            there = v_far.at[g, j]
            pltpu.make_async_copy(there, there, far_sem.at[g, j]).wait()

    def one_tile(g, t, v):
        at = g * plan.kt + t
        wide = plan.kt * TILE
        total = weigh(expo[at, :, :TILE], with_ones(late[h][at, 0]))
        for j in range(NB):
            total += weigh(expo[at, :, TILE + j * wide:TILE + (j + 1) * wide], v[j])
        out[at, stored(g, 1)] = finish(plan, total)

    each_view(
        plan, wait, one_tile,
        lambda g: [with_ones(far_rows(plan, v_far, g, j)) for j in range(NB)],
    )


def call(kernel, name, out_shape, in_specs, out_specs, scratch, args, flops=0, exps=0, moved=0,
         mib=8, aliases={}):
    return pl.pallas_call(
        kernel,
        out_shape=out_shape,
        in_specs=in_specs,
        out_specs=out_specs,
        scratch_shapes=scratch,
        compiler_params=pltpu.CompilerParams(vmem_limit_bytes=mib * 2 ** 20),
        cost_estimate=pl.CostEstimate(flops=flops, bytes_accessed=moved, transcendentals=exps),
        name=name,
        input_output_aliases=aliases,
    )(*args)


def local(queries, keys, values, tile_mask, offsets, branch_slots):
    sub, toks = lax.axis_size("sub"), lax.axis_size("tok")
    ways = sub * toks
    dtype = queries.dtype
    _, _, tokens, width = queries.shape
    tiles, share = tokens // TILE, width // ways
    kt = toks * tiles
    hops = -(-REACH // sub)
    plan = Plan(sub, kt, hops, share)
    shifts = [d for d in range(-hops, hops + 1) if d]
    order = range(-hops, hops + 1)
    half = TILE // 2
    size = queries.size * 2

    slots = branch_slots.T
    own = jnp.concatenate([tile_mask.reshape(-1), offsets.reshape(-1)])
    other = own
    if sub == 2:
        other = lax.ppermute(own, "sub", [(0, 1), (1, 0)])
    facts = (own, other)

    place = ANY if plan.whole_lanes else VMEM
    sem = pltpu.SemaphoreType.DMA(())

    def pack(name, arrays, moves, pieces, staged=False, mark=None, begun=None):
        staged = staged and plan.whole_lanes
        scratch = [sem]
        if staged:
            scratch.append(pltpu.VMEM((len(moves), tiles, TILE, width), dtype))
            scratch.append(pltpu.SemaphoreType.DMA((len(moves), tiles)))
        marks = slots if mark is None else mark
        return call(
            functools.partial(pack_kernel, plan, moves, staged), name,
            jax.ShapeDtypeStruct((ways, tiles, pieces, TILE, share), dtype),
            [SMEM, ANY] + [ANY if staged else VMEM] * len(arrays) + [ANY] * (begun is not None),
            place, scratch,
            (slots, marks, *arrays) + (() if begun is None else (begun,)),
            moved=pieces * size, mib=62 if staged else 8,
            aliases={} if begun is None else {2 + len(arrays): 0},
        )

    def spread(x):
        return exchange(x).reshape(ways * tiles, x.shape[2], TILE, share)

    def around(x):
        return {d: from_plane(x, d) if d else x for d in (0, *shifts)}

    def mark(arrays, flops):
        return call(
            mark_kernel, "mark", jax.ShapeDtypeStruct((8, 128), jnp.float32),
            [ANY] * len(arrays), VMEM, [], arrays, flops=flops, mib=1,
        )

    raw = keys.reshape(1, 2, tiles, TILE, width)[:, :, :, :half].reshape(1, 2, tiles * half, width)
    begun = None
    if plan.whole_lanes:
        begun = pack(
            "queries", [queries], [Move(0, 0, 0), Move(0, 1, 1)], 2 + plan.planes
        )
    found = {0: raw}
    for i, d in enumerate(shifts):
        if i and begun is not None:
            raw, begun, _ = lax.optimization_barrier((raw, begun, found[shifts[i - 1]]))
        elif i:
            raw, _ = lax.optimization_barrier((raw, found[shifts[i - 1]]))
        found[d] = from_plane(raw, d)
    raw = found
    packed = pack(
        "first", [keys, values],
        [Move(0, b, 0, row=half, rows=half, to=b * half) for b in range(2)]
        + [Move(1, b, 1 + b) for b in range(2)], 3, staged=True,
    )
    early = spread(packed)
    arrived = mark([raw[d] for d in shifts], MARK_FLOPS[0])
    early, arrived, facts = lax.optimization_barrier((early, arrived, facts))

    planes = around(early[:, :2])
    leads = mark([planes[shifts[0]]], MARK_FLOPS[1])
    brought = mark([planes[d] for d in shifts[1:]], MARK_FLOPS[2])
    last_values, leads = lax.optimization_barrier((early[:, 2:], leads))
    late = around(last_values)
    moves = [] if plan.whole_lanes else [Move(0, 0, 0), Move(0, 1, 1)]
    for d in order:
        for b in range(2):
            moves.append(Move(
                1 + d + hops, b, 2 + d + hops, planes=d, rows=half, pitch=half, to=b * half
            ))
    packed = pack(
        "second", [queries if begun is None else slots, *[raw[d] for d in order]], moves,
        2 + plan.planes, mark=arrived, begun=begun
    )
    mixed = spread(packed)
    planes[0] = early
    planes = [planes[d] for d in order]
    late = [late[d] for d in order]

    def result(n):
        return jax.ShapeDtypeStruct((ways * tiles, n, TILE, share), dtype)

    sems = pltpu.SemaphoreType.DMA
    far = (sub, NB, kt, TILE, share)
    shapes = result(1), jax.ShapeDtypeStruct((sub * kt, plan.rows, plan.cols), dtype)
    out0, expo = (
        call(
            functools.partial(first_part_kernel, plan, b), ("attend", "scores")[b], shapes[b],
            [SMEM] * 2 + [VMEM] * (1 + plan.planes) + [ANY] * 2, VMEM,
            [pltpu.VMEM(far, dtype), pltpu.VMEM(far, dtype), sems((2, sub, NB)), sems((sub, NB))],
            (*facts, mixed, *planes, leads, brought), flops=plan.pairs * HD * (4 - 2 * b),
            exps=plan.pairs, moved=2 * size, mib=12,
        ) for b in range(2)
    )
    x = call(
        functools.partial(weigh_kernel, plan), "weigh", result(2),
        [SMEM] * 3 + [VMEM] * (2 + plan.planes), VMEM,
        [pltpu.VMEM(far, dtype), sems((sub, NB))], (*facts, slots, expo, out0, *late),
        flops=plan.pairs * HD * 2, moved=2 * size, mib=12,
    )
    x = exchange(x.reshape(ways, tiles, 2, TILE, share))
    return call(
        functools.partial(last_kernel, plan), "last",
        jax.ShapeDtypeStruct(queries.shape, dtype), [place], place, [sem], (x,),
        moved=2 * size,
    )


def solution(mesh):
    views, toks = mesh.shape["view"], mesh.shape["tok"]

    def run(queries, keys, values, tile_mask, offsets, branch_slots):
        heads = queries.shape[-1] // HD
        sub = 2 if views % 2 == 0 and heads % (2 * toks) == 0 else 1
        fine = Mesh(mesh.devices.reshape(views // sub, sub, toks), ("plane", "sub", "tok"))
        view = ("plane", "sub")
        shard = P(view, None, "tok", None)
        in_specs = (shard, shard, shard, P(view, None, None, None), P(view, None), P())
        return jax.shard_map(
            local, mesh=fine, in_specs=in_specs, out_specs=shard, check_vma=False
        )(queries, keys, values, tile_mask, offsets, branch_slots)

    return run
```

```python
import functools
import math

import jax
import jax.numpy as jnp
from jax import lax
from jax.experimental import pallas as pl
from jax.experimental.pallas import tpu as pltpu
from jax.sharding import Mesh, PartitionSpec as P

HD = 64
TILE = 128
NB = 2
REACH = 2
MARK_FLOPS = (4 * 10 ** 9, 2 * 10 ** 9, 10 ** 10)
GROUP = ("sub", "tok")

NEG_SCORE = -1e30

SMEM = pl.BlockSpec(memory_space=pltpu.SMEM)
VMEM = pl.BlockSpec(memory_space=pltpu.VMEM)
ANY = pl.BlockSpec(memory_space=pl.ANY)


def after(x, *others):
    return lax.optimization_barrier((x, others))[0]


def from_plane(x, by):
    size = lax.axis_size("plane")
    return lax.ppermute(x, "plane", [((i + by) % size, i) for i in range(size)])


def exchange(x):
    return lax.all_to_all(x, GROUP, split_axis=0, concat_axis=0, tiled=True)


class Move:
    def __init__(self, array, branch, piece, planes=0, row=0, rows=TILE, pitch=TILE, to=0):
        self.array, self.branch, self.piece, self.planes = array, branch, piece, planes
        self.row, self.rows, self.pitch, self.to = row, rows, pitch, to


def slot_of(plan, slots_ref, planes, branch):
    views = slots_ref.shape[1]
    view = (lax.axis_index("plane") + planes) * plan.sub + lax.axis_index("sub") + views
    return slots_ref[branch, lax.rem(view, views)]


def pack_kernel(plan, moves, staged, slots_ref, mark_ref, *refs):
    if staged:
        *ins, out, sem, stage, stage_sem = refs
    else:
        *ins, out, sem = refs
    ways, tiles, _, _, share = out.shape
    sources = []
    for i, move in enumerate(moves):
        slot = slot_of(plan, slots_ref, move.planes, move.branch)
        for m in range(tiles):
            rows = pl.ds(m * move.pitch + move.row, move.rows)
            source = ins[move.array].at[0, slot, rows]
            if staged:
                there = stage.at[i, m, pl.ds(0, move.rows)]
                copy = pltpu.make_async_copy(source, there, stage_sem.at[i, m])
                copy.start()
                sources.append((move, m, there, copy))
            else:
                sources.append((move, m, source, None))
    for move, m, source, copy in sources:
        if copy is not None:
            copy.wait()
        for w in range(ways):
            to, lanes = pl.ds(move.to, move.rows), pl.ds(w * share, share)
            if plan.whole_lanes:
                pltpu.make_async_copy(
                    source.at[:, lanes], out.at[w, m, move.piece, to], sem
                ).start()
            else:
                out[w, m, move.piece, to] = source[:, lanes]
    if plan.whole_lanes:
        pltpu.make_async_copy(out, out, sem).wait()


def last_kernel(plan, x, out, sem):
    ways, tiles, slots, _, share = x.shape
    for s in range(slots):
        for m in range(tiles):
            for w in range(ways):
                rows, lanes = pl.ds(m * TILE, TILE), pl.ds(w * share, share)
                if plan.whole_lanes:
                    pltpu.make_async_copy(x.at[w, m, s], out.at[0, s, rows, lanes], sem).start()
                else:
                    out[0, s, rows, lanes] = x[w, m, s]
    if plan.whole_lanes:
        pltpu.make_async_copy(out, out, sem).wait()


class Plan:
    def __init__(self, sub, kt, hops, share):
        self.sub, self.kt, self.hops, self.share = sub, kt, hops, share
        self.planes = 2 * hops + 1
        self.heads = share // HD
        self.rows = self.heads * TILE
        self.cols = (1 + NB * kt) * TILE
        self.pairs = sub * kt * self.rows * self.cols
        self.whole_lanes = share % 128 == 0


def fact(plan, facts, g, i):
    own_ref, other_ref = facts
    if plan.sub == 1:
        return own_ref[i]
    return jnp.where(lax.axis_index("sub") == g, own_ref[i], other_ref[i])


def start_far(plan, facts, copies_of):
    for g in range(plan.sub):
        for j in range(NB):
            at = fact(plan, facts, g, NB * plan.kt * plan.kt + j) + (plan.hops * plan.sub + g)
            tiles_at = (at & (plan.sub - 1)) * plan.kt
            for d in range(plan.planes):
                @pl.when((at >> (plan.sub - 1)) == d)
                def _():
                    for copy in copies_of(g, j, d, tiles_at):
                        copy.start()


def mark_kernel(*refs):
    refs[-1][...] = jnp.zeros_like(refs[-1])


def head_of_lane(plan):
    return lax.broadcasted_iota(jnp.int32, (TILE, plan.share), 1) // HD


def split_heads(plan, q):
    if plan.heads == 1:
        return q
    block = head_of_lane(plan)
    return jnp.concatenate([jnp.where(block == h, q, 0) for h in range(plan.heads)], axis=0)


def scores_of(q, k):
    return lax.dot_general(q, k, (((1,), (1,)), ((), ())), preferred_element_type=jnp.float32)


def numerators(plan, facts, g, t, own, far):
    factor = HD ** -0.5 * math.log2(math.e)
    parts = [own]
    for j in range(NB):
        for k in range(plan.kt):
            keep = fact(plan, facts, g, (j * plan.kt + t) * plan.kt + k) == 1
            bias = jnp.where(keep, 0.0, NEG_SCORE)
            parts.append(far[j][:, k * TILE:(k + 1) * TILE] + bias)
    top = functools.reduce(jnp.maximum, parts)
    top = jnp.max(top, axis=1, keepdims=True)
    return [jnp.exp2((part - top) * factor).astype(jnp.bfloat16) for part in parts]


def with_ones(v):
    return jnp.concatenate([v, jnp.ones_like(v)], axis=1)


def weigh(p, v):
    return jnp.dot(p, v, preferred_element_type=jnp.float32)


def finish(plan, total):
    result = total[:TILE]
    block = head_of_lane(plan)
    both = jnp.concatenate([block, block], axis=1)
    for h in range(1, plan.heads):
        result = jnp.where(both == h, total[h * TILE:(h + 1) * TILE], result)
    return (result[:, :plan.share] / result[:, plan.share:]).astype(jnp.bfloat16)


def far_rows(plan, buffer, g, j):
    return buffer[g, j].reshape(plan.kt * TILE, plan.share)


def each_view(plan, wait, one_tile, prepare):
    count = math.gcd(plan.kt, 4)

    def some_tiles(g, t0):
        ready = prepare(g)
        for i in range(count):
            one_tile(g, t0 + i, ready)

    def one_view(g, carry):
        wait(g)
        if count == plan.kt:
            some_tiles(g, 0)
        else:
            def some(i, c):
                some_tiles(g, i * count)
                return c
            lax.fori_loop(0, plan.kt // count, some, 0)
        return carry

    lax.fori_loop(0, plan.sub, one_view, 0)


def core_kernel(plan, own, other, mixed, *refs):
    n, h = plan.planes, plan.hops
    planes = refs[:n]
    out, expo_ref, k_far, v_far, k_sem, v_sem = refs[-6:]
    facts = (own, other)
    half = TILE // 2
    low, high = pl.ds(0, half), pl.ds(half, half)
    mine = [pl.ds(b * half, half) for b in range(2)]

    def far_copies(g, j, d, tiles_at):
        tiles = pl.ds(tiles_at, plan.kt)
        found = []
        for b in range(2):
            found.append((mixed.at[tiles, 2 + d, mine[b]], k_far.at[b, g, j, :, low], k_sem.at[0, b, g, j]))
            found.append((planes[d].at[tiles, 0, mine[b]], k_far.at[b, g, j, :, high], k_sem.at[1, b, g, j]))
            if b == 0:
                found.append((planes[d].at[tiles, 1], v_far.at[g, j], v_sem.at[g, j]))
        return [pltpu.make_async_copy(*copy) for copy in found]

    start_far(plan, facts, far_copies)

    def wait(b, g):
        for j in range(NB):
            for part, rows in enumerate((low, high)):
                there = k_far.at[b, g, j, :, rows]
                pltpu.make_async_copy(there, there, k_sem.at[part, b, g, j]).wait()
            if b == 0:
                there = v_far.at[g, j]
                pltpu.make_async_copy(there, there, v_sem.at[g, j]).wait()

    def expo_of(b, g, t, k):
        at = g * plan.kt + t
        q = split_heads(plan, mixed[at, b])
        k_own = jnp.concatenate([mixed[at, 2 + h, mine[b]], planes[h][at, 0, mine[b]]], axis=0)
        return numerators(
            plan, facts, g, t, scores_of(q, k_own), [scores_of(q, k[j]) for j in range(NB)]
        )

    def keys(b, g):
        return [far_rows(plan, k_far.at[b], g, j) for j in range(NB)]

    def attended(g, t, ready):
        k, v = ready
        at = g * plan.kt + t
        expo = expo_of(0, g, t, k)
        total = weigh(expo[0], with_ones(planes[h][at, 1]))
        for j in range(NB):
            p = jnp.concatenate(expo[1 + j * plan.kt:1 + (j + 1) * plan.kt], axis=1)
            total += weigh(p, v[j])
        out[at, 0] = finish(plan, total)

    def scored(g, t, k):
        for i, part in enumerate(expo_of(1, g, t, k)):
            expo_ref[g * plan.kt + t, :, i * TILE:(i + 1) * TILE] = part

    each_view(
        plan, functools.partial(wait, 0), attended,
        lambda g: (keys(0, g), [with_ones(far_rows(plan, v_far, g, j)) for j in range(NB)]),
    )
    each_view(plan, functools.partial(wait, 1), scored, functools.partial(keys, 1))


def weigh_kernel(plan, own, other, slots, expo, done, *refs):
    n, h = plan.planes, plan.hops
    late = refs[:n]
    out, v_far, far_sem = refs[-3:]

    def stored(g, b):
        return slots[b, lax.axis_index("plane") * plan.sub + g]

    def far_copies(g, j, d, tiles_at):
        src = late[d].at[pl.ds(tiles_at, plan.kt), 0]
        return [pltpu.make_async_copy(src, v_far.at[g, j], far_sem.at[g, j])]

    start_far(plan, (own, other), far_copies)
    for g in range(plan.sub):
        for t in range(plan.kt):
            out[g * plan.kt + t, stored(g, 0)] = done[g * plan.kt + t, 0]

    def wait(g):
        for j in range(NB):
            there = v_far.at[g, j]
            pltpu.make_async_copy(there, there, far_sem.at[g, j]).wait()

    def one_tile(g, t, v):
        at = g * plan.kt + t
        wide = plan.kt * TILE
        total = weigh(expo[at, :, :TILE], with_ones(late[h][at, 0]))
        for j in range(NB):
            total += weigh(expo[at, :, TILE + j * wide:TILE + (j + 1) * wide], v[j])
        out[at, stored(g, 1)] = finish(plan, total)

    each_view(
        plan, wait, one_tile,
        lambda g: [with_ones(far_rows(plan, v_far, g, j)) for j in range(NB)],
    )


def call(kernel, name, out_shape, in_specs, out_specs, scratch, args, flops=0, exps=0, moved=0,
         mib=8):
    return pl.pallas_call(
        kernel,
        out_shape=out_shape,
        in_specs=in_specs,
        out_specs=out_specs,
        scratch_shapes=scratch,
        compiler_params=pltpu.CompilerParams(vmem_limit_bytes=mib * 2 ** 20),
        cost_estimate=pl.CostEstimate(flops=flops, bytes_accessed=moved, transcendentals=exps),
        name=name,
    )(*args)


def local(queries, keys, values, tile_mask, offsets, branch_slots):
    sub, toks = lax.axis_size("sub"), lax.axis_size("tok")
    ways = sub * toks
    dtype = queries.dtype
    _, _, tokens, width = queries.shape
    tiles, share = tokens // TILE, width // ways
    kt = toks * tiles
    hops = -(-REACH // sub)
    plan = Plan(sub, kt, hops, share)
    shifts = [d for d in range(-hops, hops + 1) if d]
    order = range(-hops, hops + 1)
    half = TILE // 2
    size = queries.size * 2

    slots = branch_slots.T
    own = jnp.concatenate([tile_mask.reshape(-1), offsets.reshape(-1)])
    other = own
    if sub == 2:
        other = lax.ppermute(own, "sub", [(0, 1), (1, 0)])
    facts = (own, other)

    place = ANY if plan.whole_lanes else VMEM
    sem = pltpu.SemaphoreType.DMA(())

    def pack(name, arrays, moves, pieces, staged=False, mark=None):
        staged = staged and plan.whole_lanes
        scratch = [sem]
        if staged:
            scratch.append(pltpu.VMEM((len(moves), tiles, TILE, width), dtype))
            scratch.append(pltpu.SemaphoreType.DMA((len(moves), tiles)))
        return call(
            functools.partial(pack_kernel, plan, moves, staged), name,
            jax.ShapeDtypeStruct((ways, tiles, pieces, TILE, share), dtype),
            [SMEM, ANY] + [ANY if staged else VMEM] * len(arrays), place, scratch,
            (slots, slots if mark is None else mark, *arrays), moved=pieces * size,
            mib=62 if staged else 8,
        )

    def spread(x):
        return exchange(x).reshape(ways * tiles, x.shape[2], TILE, share)

    def around(x, chain=False):
        found, last = {0: x}, ()
        for d in shifts:
            found[d] = from_plane(after(x, last), d)
            last = found[d] if chain else ()
        return found

    def mark(arrays, flops):
        return call(
            mark_kernel, "mark", jax.ShapeDtypeStruct((8, 128), jnp.float32),
            [ANY] * len(arrays), VMEM, [], arrays, flops=flops, mib=1,
        )

    raw = keys.reshape(1, 2, tiles, TILE, width)[:, :, :, :half].reshape(1, 2, tiles * half, width)
    raw = around(raw, chain=True)
    packed = pack(
        "first", [keys, values],
        [Move(0, b, 0, row=half, rows=half, to=b * half) for b in range(2)]
        + [Move(1, b, 1 + b) for b in range(2)], 3, staged=True,
    )
    early = spread(packed)
    arrived = mark([raw[d] for d in shifts], MARK_FLOPS[0])
    early, arrived, facts = lax.optimization_barrier((early, arrived, facts))

    planes = around(early[:, :2])
    leads = mark([planes[shifts[0]]], MARK_FLOPS[1])
    brought = mark([planes[d] for d in shifts[1:]], MARK_FLOPS[2])
    last_values, leads = lax.optimization_barrier((early[:, 2:], leads))
    late = around(last_values)
    moves = [Move(0, 0, 0), Move(0, 1, 1)]
    for d in order:
        for b in range(2):
            moves.append(Move(
                1 + d + hops, b, 2 + d + hops, planes=d, rows=half, pitch=half, to=b * half
            ))
    packed = pack(
        "second", [queries, *[raw[d] for d in order]], moves, 2 + plan.planes, mark=arrived
    )
    mixed = spread(packed)
    planes[0] = early
    planes = [planes[d] for d in order]
    late = [late[d] for d in order]

    def result(n):
        return jax.ShapeDtypeStruct((ways * tiles, n, TILE, share), dtype)

    sems = pltpu.SemaphoreType.DMA
    far = (sub, NB, kt, TILE, share)
    expo = jax.ShapeDtypeStruct((sub * kt, plan.rows, plan.cols), dtype)
    out0, expo = call(
        functools.partial(core_kernel, plan), "core", (result(1), expo),
        [SMEM] * 2 + [VMEM] * (1 + plan.planes) + [ANY] * 2, (VMEM, VMEM),
        [pltpu.VMEM((2, *far), dtype), pltpu.VMEM(far, dtype), sems((2, 2, sub, NB)),
         sems((sub, NB))],
        (*facts, mixed, *planes, leads, brought), flops=plan.pairs * HD * 6,
        exps=2 * plan.pairs, moved=2 * size, mib=12,
    )
    x = call(
        functools.partial(weigh_kernel, plan), "weigh", result(2),
        [SMEM] * 3 + [VMEM] * 2 + [ANY if d else VMEM for d in order], VMEM,
        [pltpu.VMEM(far, dtype), sems((sub, NB))], (*facts, slots, expo, out0, *late),
        flops=plan.pairs * HD * 2, moved=2 * size, mib=12,
    )
    x = exchange(x.reshape(ways, tiles, 2, TILE, share))
    return call(
        functools.partial(last_kernel, plan), "last",
        jax.ShapeDtypeStruct(queries.shape, dtype), [place], place, [sem], (x,),
        moved=2 * size,
    )


def solution(mesh):
    views, toks = mesh.shape["view"], mesh.shape["tok"]

    def run(queries, keys, values, tile_mask, offsets, branch_slots):
        heads = queries.shape[-1] // HD
        sub = 2 if views % 2 == 0 and heads % (2 * toks) == 0 else 1
        fine = Mesh(mesh.devices.reshape(views // sub, sub, toks), ("plane", "sub", "tok"))
        view = ("plane", "sub")
        shard = P(view, None, "tok", None)
        in_specs = (shard, shard, shard, P(view, None, None, None), P(view, None), P())
        return jax.shard_map(
            local, mesh=fine, in_specs=in_specs, out_specs=shard, check_vma=False
        )(queries, keys, values, tile_mask, offsets, branch_slots)

    return run
```

```python
import functools
import math

import jax
import jax.numpy as jnp
from jax import lax
from jax.experimental import pallas as pl
from jax.experimental.pallas import tpu as pltpu
from jax.sharding import Mesh, PartitionSpec as P

HD = 64
TILE = 128
NB = 2
REACH = 2
MARK_FLOPS = (4 * 10 ** 9, 2 * 10 ** 9, 10 ** 10)
GROUP = ("sub", "tok")

NEG_SCORE = -1e30

SMEM = pl.BlockSpec(memory_space=pltpu.SMEM)
VMEM = pl.BlockSpec(memory_space=pltpu.VMEM)
ANY = pl.BlockSpec(memory_space=pl.ANY)


def after(x, *others):
    return lax.optimization_barrier((x, others))[0]


def from_plane(x, by):
    size = lax.axis_size("plane")
    return lax.ppermute(x, "plane", [((i + by) % size, i) for i in range(size)])


def exchange(x):
    return lax.all_to_all(x, GROUP, split_axis=0, concat_axis=0, tiled=True)


class Move:
    def __init__(self, array, branch, piece, planes=0, row=0, rows=TILE, pitch=TILE, to=0):
        self.array, self.branch, self.piece, self.planes = array, branch, piece, planes
        self.row, self.rows, self.pitch, self.to = row, rows, pitch, to


def slot_of(plan, slots_ref, planes, branch):
    views = slots_ref.shape[1]
    view = (lax.axis_index("plane") + planes) * plan.sub + lax.axis_index("sub") + views
    return slots_ref[branch, lax.rem(view, views)]


def pack_kernel(plan, moves, staged, slots_ref, mark_ref, *refs):
    if staged:
        *ins, out, sem, stage, stage_sem = refs
    else:
        *ins, out, sem = refs
    ways, tiles, _, _, share = out.shape
    sources = []
    for i, move in enumerate(moves):
        slot = slot_of(plan, slots_ref, move.planes, move.branch)
        for m in range(tiles):
            rows = pl.ds(m * move.pitch + move.row, move.rows)
            source = ins[move.array].at[0, slot, rows]
            if staged:
                there = stage.at[i, m, pl.ds(0, move.rows)]
                copy = pltpu.make_async_copy(source, there, stage_sem.at[i, m])
                copy.start()
                sources.append((move, m, there, copy))
            else:
                sources.append((move, m, source, None))
    for move, m, source, copy in sources:
        if copy is not None:
            copy.wait()
        for w in range(ways):
            to, lanes = pl.ds(move.to, move.rows), pl.ds(w * share, share)
            if plan.whole_lanes:
                pltpu.make_async_copy(
                    source.at[:, lanes], out.at[w, m, move.piece, to], sem
                ).start()
            else:
                out[w, m, move.piece, to] = source[:, lanes]
    if plan.whole_lanes:
        pltpu.make_async_copy(out, out, sem).wait()


def first_kernel(plan, slots_ref, keys, values, out, stage, slots, stage_sem, slots_sem, sem):
    ways, tiles, _, _, share = out.shape
    half = TILE // 2
    ask = pltpu.make_async_copy(slots_ref, slots, slots_sem)
    ask.start()
    fetched = []
    for i, (src, row, rows) in enumerate(((keys, half, half), (values, 0, TILE))):
        for s in range(2):
            for m in range(tiles):
                there = stage.at[2 * i + s, m, pl.ds(0, rows)]
                copy = pltpu.make_async_copy(
                    src.at[0, s, pl.ds(m * TILE + row, rows)], there, stage_sem.at[2 * i + s, m]
                )
                copy.start()
                fetched.append((i, s, m, there, copy))
    ask.wait()
    view = lax.axis_index("plane") * plan.sub + lax.axis_index("sub")
    lead = slots[0, view]
    for i, s, m, there, copy in fetched:
        branch = jnp.where(lead == s, 0, 1)
        copy.wait()
        for w in range(ways):
            if i == 0:
                to = out.at[w, m, 0, pl.ds(pl.multiple_of(branch * half, half), half)]
            else:
                to = out.at[w, m, 1 + branch]
            pltpu.make_async_copy(there.at[:, pl.ds(w * share, share)], to, sem).start()
    pltpu.make_async_copy(out, out, sem).wait()


def split_kernel(x, head, tail):
    pieces = head.shape[1]
    head[...] = x[:, :pieces]
    tail[...] = x[:, pieces:]


def last_kernel(plan, x, out, sem):
    ways, tiles, slots, _, share = x.shape
    for s in range(slots):
        for m in range(tiles):
            for w in range(ways):
                rows, lanes = pl.ds(m * TILE, TILE), pl.ds(w * share, share)
                if plan.whole_lanes:
                    pltpu.make_async_copy(x.at[w, m, s], out.at[0, s, rows, lanes], sem).start()
                else:
                    out[0, s, rows, lanes] = x[w, m, s]
    if plan.whole_lanes:
        pltpu.make_async_copy(out, out, sem).wait()


class Plan:
    def __init__(self, sub, kt, hops, share):
        self.sub, self.kt, self.hops, self.share = sub, kt, hops, share
        self.planes = 2 * hops + 1
        self.heads = share // HD
        self.rows = self.heads * TILE
        self.cols = (1 + NB * kt) * TILE
        self.pairs = sub * kt * self.rows * self.cols
        self.whole_lanes = share % 128 == 0


def fact(plan, facts, g, i):
    own_ref, other_ref = facts
    if plan.sub == 1:
        return own_ref[i]
    return jnp.where(lax.axis_index("sub") == g, own_ref[i], other_ref[i])


def start_far(plan, facts, copies_of):
    for g in range(plan.sub):
        for j in range(NB):
            at = fact(plan, facts, g, NB * plan.kt * plan.kt + j) + (plan.hops * plan.sub + g)
            tiles_at = (at & (plan.sub - 1)) * plan.kt
            for d in range(plan.planes):
                @pl.when((at >> (plan.sub - 1)) == d)
                def _():
                    for copy in copies_of(g, j, d, tiles_at):
                        copy.start()


def mark_kernel(*refs):
    refs[-1][...] = jnp.zeros_like(refs[-1])


def head_of_lane(plan):
    return lax.broadcasted_iota(jnp.int32, (TILE, plan.share), 1) // HD


def split_heads(plan, q):
    if plan.heads == 1:
        return q
    block = head_of_lane(plan)
    return jnp.concatenate([jnp.where(block == h, q, 0) for h in range(plan.heads)], axis=0)


def scores_of(q, k):
    return lax.dot_general(q, k, (((1,), (1,)), ((), ())), preferred_element_type=jnp.float32)


def numerators(plan, facts, g, t, own, far):
    factor = HD ** -0.5 * math.log2(math.e)
    parts = [own]
    for j in range(NB):
        for k in range(plan.kt):
            keep = fact(plan, facts, g, (j * plan.kt + t) * plan.kt + k) == 1
            bias = jnp.where(keep, 0.0, NEG_SCORE)
            parts.append(far[j][:, k * TILE:(k + 1) * TILE] + bias)
    top = functools.reduce(jnp.maximum, parts)
    top = jnp.max(top, axis=1, keepdims=True)
    return [jnp.exp2((part - top) * factor).astype(jnp.bfloat16) for part in parts]


def with_ones(v):
    return jnp.concatenate([v, jnp.ones_like(v)], axis=1)


def weigh(p, v):
    return jnp.dot(p, v, preferred_element_type=jnp.float32)


def finish(plan, total):
    result = total[:TILE]
    block = head_of_lane(plan)
    both = jnp.concatenate([block, block], axis=1)
    for h in range(1, plan.heads):
        result = jnp.where(both == h, total[h * TILE:(h + 1) * TILE], result)
    return (result[:, :plan.share] / result[:, plan.share:]).astype(jnp.bfloat16)


def far_rows(plan, buffer, g, j):
    return buffer[g, j].reshape(plan.kt * TILE, plan.share)


def each_view(plan, wait, one_tile, prepare):
    count = math.gcd(plan.kt, 4)

    def some_tiles(g, t0):
        ready = prepare(g)
        for i in range(count):
            one_tile(g, t0 + i, ready)

    def one_view(g, carry):
        wait(g)
        if count == plan.kt:
            some_tiles(g, 0)
        else:
            def some(i, c):
                some_tiles(g, i * count)
                return c
            lax.fori_loop(0, plan.kt // count, some, 0)
        return carry

    lax.fori_loop(0, plan.sub, one_view, 0)


def core_kernel(plan, own, other, mixed, *refs):
    n, h = plan.planes, plan.hops
    planes = refs[:n]
    out, expo_ref, k_far, v_far, k_sem, v_sem = refs[-6:]
    facts = (own, other)
    half = TILE // 2
    low, high = pl.ds(0, half), pl.ds(half, half)
    mine = [pl.ds(b * half, half) for b in range(2)]

    def far_copies(g, j, d, tiles_at):
        tiles = pl.ds(tiles_at, plan.kt)
        found = []
        for b in range(2):
            found.append((mixed.at[tiles, 2 + d, mine[b]], k_far.at[b, g, j, :, low], k_sem.at[0, b, g, j]))
            found.append((planes[d].at[tiles, 0, mine[b]], k_far.at[b, g, j, :, high], k_sem.at[1, b, g, j]))
            if b == 0:
                found.append((planes[d].at[tiles, 1], v_far.at[g, j], v_sem.at[g, j]))
        return [pltpu.make_async_copy(*copy) for copy in found]

    start_far(plan, facts, far_copies)

    def wait(b, g):
        for j in range(NB):
            for part, rows in enumerate((low, high)):
                there = k_far.at[b, g, j, :, rows]
                pltpu.make_async_copy(there, there, k_sem.at[part, b, g, j]).wait()
            if b == 0:
                there = v_far.at[g, j]
                pltpu.make_async_copy(there, there, v_sem.at[g, j]).wait()

    def expo_of(b, g, t, k):
        at = g * plan.kt + t
        q = split_heads(plan, mixed[at, b])
        k_own = jnp.concatenate([mixed[at, 2 + h, mine[b]], planes[h][at, 0, mine[b]]], axis=0)
        return numerators(
            plan, facts, g, t, scores_of(q, k_own), [scores_of(q, k[j]) for j in range(NB)]
        )

    def keys(b, g):
        return [far_rows(plan, k_far.at[b], g, j) for j in range(NB)]

    def attended(g, t, ready):
        k, v = ready
        at = g * plan.kt + t
        expo = expo_of(0, g, t, k)
        total = weigh(expo[0], with_ones(planes[h][at, 1]))
        for j in range(NB):
            p = jnp.concatenate(expo[1 + j * plan.kt:1 + (j + 1) * plan.kt], axis=1)
            total += weigh(p, v[j])
        out[at, 0] = finish(plan, total)

    def scored(g, t, k):
        for i, part in enumerate(expo_of(1, g, t, k)):
            expo_ref[g * plan.kt + t, :, i * TILE:(i + 1) * TILE] = part

    def wait_both(g):
        wait(0, g)
        wait(1, g)

    def prepare(g):
        v = [with_ones(far_rows(plan, v_far, g, j)) for j in range(NB)]
        return (keys(0, g), v), keys(1, g)

    def both(g, t, ready):
        attended(g, t, ready[0])
        scored(g, t, ready[1])

    each_view(plan, wait_both, both, prepare)


def weigh_kernel(plan, own, other, slots, expo, done, *refs):
    n, h = plan.planes, plan.hops
    late = refs[:n]
    out, v_far, far_sem = refs[-3:]

    def stored(g, b):
        return slots[b, lax.axis_index("plane") * plan.sub + g]

    def far_copies(g, j, d, tiles_at):
        src = late[d].at[pl.ds(tiles_at, plan.kt), 0]
        return [pltpu.make_async_copy(src, v_far.at[g, j], far_sem.at[g, j])]

    start_far(plan, (own, other), far_copies)
    for g in range(plan.sub):
        for t in range(plan.kt):
            out[g * plan.kt + t, stored(g, 0)] = done[g * plan.kt + t, 0]

    def wait(g):
        for j in range(NB):
            there = v_far.at[g, j]
            pltpu.make_async_copy(there, there, far_sem.at[g, j]).wait()

    def one_tile(g, t, v):
        at = g * plan.kt + t
        wide = plan.kt * TILE
        total = weigh(expo[at, :, :TILE], with_ones(late[h][at, 0]))
        for j in range(NB):
            total += weigh(expo[at, :, TILE + j * wide:TILE + (j + 1) * wide], v[j])
        out[at, stored(g, 1)] = finish(plan, total)

    each_view(
        plan, wait, one_tile,
        lambda g: [with_ones(far_rows(plan, v_far, g, j)) for j in range(NB)],
    )


def call(kernel, name, out_shape, in_specs, out_specs, scratch, args, flops=0, exps=0, moved=0,
         mib=8):
    return pl.pallas_call(
        kernel,
        out_shape=out_shape,
        in_specs=in_specs,
        out_specs=out_specs,
        scratch_shapes=scratch,
        compiler_params=pltpu.CompilerParams(vmem_limit_bytes=mib * 2 ** 20),
        cost_estimate=pl.CostEstimate(flops=flops, bytes_accessed=moved, transcendentals=exps),
        name=name,
    )(*args)


def local(queries, keys, values, tile_mask, offsets, branch_slots):
    sub, toks = lax.axis_size("sub"), lax.axis_size("tok")
    ways = sub * toks
    dtype = queries.dtype
    _, _, tokens, width = queries.shape
    tiles, share = tokens // TILE, width // ways
    kt = toks * tiles
    hops = -(-REACH // sub)
    plan = Plan(sub, kt, hops, share)
    shifts = [d for d in range(-hops, hops + 1) if d]
    order = range(-hops, hops + 1)
    half = TILE // 2
    size = queries.size * 2

    slots = branch_slots.T
    own = jnp.concatenate([tile_mask.reshape(-1), offsets.reshape(-1)])
    other = own
    if sub == 2:
        other = lax.ppermute(own, "sub", [(0, 1), (1, 0)])
    facts = (own, other)

    place = ANY if plan.whole_lanes else VMEM
    sem = pltpu.SemaphoreType.DMA(())

    def pack(name, arrays, moves, pieces, staged=False, mark=None):
        staged = staged and plan.whole_lanes
        scratch = [sem]
        if staged:
            scratch.append(pltpu.VMEM((len(moves), tiles, TILE, width), dtype))
            scratch.append(pltpu.SemaphoreType.DMA((len(moves), tiles)))
        return call(
            functools.partial(pack_kernel, plan, moves, staged), name,
            jax.ShapeDtypeStruct((ways, tiles, pieces, TILE, share), dtype),
            [SMEM, ANY] + [ANY if staged else VMEM] * len(arrays), place, scratch,
            (slots, slots if mark is None else mark, *arrays), moved=pieces * size,
            mib=62 if staged else 8,
        )

    def spread(x):
        return exchange(x).reshape(ways * tiles, x.shape[2], TILE, share)

    def around(x, chain=False):
        found, last = {0: x}, ()
        for d in shifts:
            found[d] = from_plane(after(x, last), d)
            last = found[d] if chain else ()
        return found

    def mark(arrays, flops):
        return call(
            mark_kernel, "mark", jax.ShapeDtypeStruct((8, 128), jnp.float32),
            [ANY] * len(arrays), VMEM, [], arrays, flops=flops, mib=1,
        )

    raw = keys.reshape(1, 2, tiles, TILE, width)[:, :, :, :half].reshape(1, 2, tiles * half, width)
    raw = around(raw, chain=True)
    if plan.whole_lanes:
        packed = call(
            functools.partial(first_kernel, plan), "first",
            jax.ShapeDtypeStruct((ways, tiles, 3, TILE, share), dtype), [ANY] * 3, ANY,
            [pltpu.VMEM((4, tiles, TILE, width), dtype), pltpu.SMEM(slots.shape, jnp.int32),
             pltpu.SemaphoreType.DMA((4, tiles)), sem, sem],
            (slots, keys, values), moved=3 * size, mib=62,
        )
    else:
        packed = pack(
            "first", [keys, values],
            [Move(0, b, 0, row=half, rows=half, to=b * half) for b in range(2)]
            + [Move(1, b, 1 + b) for b in range(2)], 3,
        )
    early = spread(packed)
    arrived = mark([raw[d] for d in shifts], MARK_FLOPS[0])
    early, arrived, facts = lax.optimization_barrier((early, arrived, facts))

    heads, last_values = call(
        split_kernel, "split",
        tuple(jax.ShapeDtypeStruct((ways * tiles, n, TILE, share), dtype) for n in (2, 1)),
        [VMEM], (VMEM, VMEM), [], (early,), moved=size,
    )
    planes = around(heads)
    leads = mark([planes[shifts[0]]], MARK_FLOPS[1])
    brought = mark([planes[d] for d in shifts[1:]], MARK_FLOPS[2])
    last_values, leads = lax.optimization_barrier((last_values, leads))
    late = around(last_values)
    moves = [Move(0, 0, 0), Move(0, 1, 1)]
    for d in order:
        for b in range(2):
            moves.append(Move(
                1 + d + hops, b, 2 + d + hops, planes=d, rows=half, pitch=half, to=b * half
            ))
    packed = pack(
        "second", [queries, *[raw[d] for d in order]], moves, 2 + plan.planes, mark=arrived
    )
    mixed = spread(packed)
    planes[0] = early
    planes = [planes[d] for d in order]
    late = [late[d] for d in order]

    def result(n):
        return jax.ShapeDtypeStruct((ways * tiles, n, TILE, share), dtype)

    sems = pltpu.SemaphoreType.DMA
    far = (sub, NB, kt, TILE, share)
    expo = jax.ShapeDtypeStruct((sub * kt, plan.rows, plan.cols), dtype)
    out0, expo = call(
        functools.partial(core_kernel, plan), "core", (result(1), expo),
        [SMEM] * 2 + [VMEM] * (1 + plan.planes) + [ANY] * 2, (VMEM, VMEM),
        [pltpu.VMEM((2, *far), dtype), pltpu.VMEM(far, dtype), sems((2, 2, sub, NB)),
         sems((sub, NB))],
        (*facts, mixed, *planes, leads, brought), flops=plan.pairs * HD * 6,
        exps=2 * plan.pairs, moved=2 * size, mib=12 if kt <= 4 else 32,
    )
    x = call(
        functools.partial(weigh_kernel, plan), "weigh", result(2),
        [SMEM] * 3 + [VMEM] * 2 + [ANY if d else VMEM for d in order], VMEM,
        [pltpu.VMEM(far, dtype), sems((sub, NB))], (*facts, slots, expo, out0, *late),
        flops=plan.pairs * HD * 2, moved=2 * size, mib=12,
    )
    x = exchange(x.reshape(ways, tiles, 2, TILE, share))
    return call(
        functools.partial(last_kernel, plan), "last",
        jax.ShapeDtypeStruct(queries.shape, dtype), [place], place, [sem], (x,),
        moved=2 * size,
    )


def solution(mesh):
    views, toks = mesh.shape["view"], mesh.shape["tok"]

    def run(queries, keys, values, tile_mask, offsets, branch_slots):
        heads = queries.shape[-1] // HD
        sub = 2 if views % 2 == 0 and heads % (2 * toks) == 0 else 1
        fine = Mesh(mesh.devices.reshape(views // sub, sub, toks), ("plane", "sub", "tok"))
        view = ("plane", "sub")
        shard = P(view, None, "tok", None)
        in_specs = (shard, shard, shard, P(view, None, None, None), P(view, None), P())
        return jax.shard_map(
            local, mesh=fine, in_specs=in_specs, out_specs=shard, check_vma=False
        )(queries, keys, values, tile_mask, offsets, branch_slots)

    return run
```

```python
import functools
import math

import jax
import jax.numpy as jnp
from jax import lax
from jax.experimental import pallas as pl
from jax.experimental.pallas import tpu as pltpu
from jax.sharding import Mesh, PartitionSpec as P

HD = 64
TILE = 128
NB = 2
REACH = 2
MARK_FLOPS = (4 * 10 ** 9, 2 * 10 ** 9, 10 ** 10)
GROUP = ("sub", "tok")

NEG_SCORE = -1e30

SMEM = pl.BlockSpec(memory_space=pltpu.SMEM)
VMEM = pl.BlockSpec(memory_space=pltpu.VMEM)
ANY = pl.BlockSpec(memory_space=pl.ANY)


def after(x, *others):
    return lax.optimization_barrier((x, others))[0]


def from_plane(x, by):
    size = lax.axis_size("plane")
    return lax.ppermute(x, "plane", [((i + by) % size, i) for i in range(size)])


def exchange(x):
    return lax.all_to_all(x, GROUP, split_axis=0, concat_axis=0, tiled=True)


class Move:
    def __init__(self, array, branch, piece, planes=0, row=0, rows=TILE, pitch=TILE, to=0):
        self.array, self.branch, self.piece, self.planes = array, branch, piece, planes
        self.row, self.rows, self.pitch, self.to = row, rows, pitch, to


def slot_of(plan, slots_ref, planes, branch):
    views = slots_ref.shape[1]
    view = (lax.axis_index("plane") + planes) * plan.sub + lax.axis_index("sub") + views
    return slots_ref[branch, lax.rem(view, views)]


def pack_kernel(plan, moves, staged, slots_ref, mark_ref, *refs):
    if staged:
        *ins, out, sem, stage, stage_sem = refs
    else:
        *ins, out, sem = refs
    ways, tiles, _, _, share = out.shape
    sources = []
    for i, move in enumerate(moves):
        slot = slot_of(plan, slots_ref, move.planes, move.branch)
        for m in range(tiles):
            rows = pl.ds(m * move.pitch + move.row, move.rows)
            source = ins[move.array].at[0, slot, rows]
            if staged:
                there = stage.at[i, m, pl.ds(0, move.rows)]
                copy = pltpu.make_async_copy(source, there, stage_sem.at[i, m])
                copy.start()
                sources.append((move, m, there, copy))
            else:
                sources.append((move, m, source, None))
    for move, m, source, copy in sources:
        if copy is not None:
            copy.wait()
        for w in range(ways):
            to, lanes = pl.ds(move.to, move.rows), pl.ds(w * share, share)
            if plan.whole_lanes:
                pltpu.make_async_copy(
                    source.at[:, lanes], out.at[w, m, move.piece, to], sem
                ).start()
            else:
                out[w, m, move.piece, to] = source[:, lanes]
    if plan.whole_lanes:
        pltpu.make_async_copy(out, out, sem).wait()


def first_kernel(plan, slots_ref, keys, values, out, stage, slots, stage_sem, slots_sem, sem):
    ways, tiles, _, _, share = out.shape
    half = TILE // 2
    ask = pltpu.make_async_copy(slots_ref, slots, slots_sem)
    ask.start()
    fetched = []
    for i, (src, row, rows) in enumerate(((keys, half, half), (values, 0, TILE))):
        for s in range(2):
            for m in range(tiles):
                there = stage.at[2 * i + s, m, pl.ds(0, rows)]
                copy = pltpu.make_async_copy(
                    src.at[0, s, pl.ds(m * TILE + row, rows)], there, stage_sem.at[2 * i + s, m]
                )
                copy.start()
                fetched.append((i, s, m, there, copy))
    ask.wait()
    view = lax.axis_index("plane") * plan.sub + lax.axis_index("sub")
    lead = slots[0, view]
    for i, s, m, there, copy in fetched:
        branch = jnp.where(lead == s, 0, 1)
        copy.wait()
        for w in range(ways):
            if i == 0:
                to = out.at[w, m, 0, pl.ds(pl.multiple_of(branch * half, half), half)]
            else:
                to = out.at[w, m, 1 + branch]
            pltpu.make_async_copy(there.at[:, pl.ds(w * share, share)], to, sem).start()
    pltpu.make_async_copy(out, out, sem).wait()


def split_kernel(x, head, tail):
    pieces = head.shape[1]
    head[...] = x[:, :pieces]
    tail[...] = x[:, pieces:]


def last_kernel(plan, x, out, sem):
    ways, tiles, slots, _, share = x.shape
    for s in range(slots):
        for m in range(tiles):
            for w in range(ways):
                rows, lanes = pl.ds(m * TILE, TILE), pl.ds(w * share, share)
                if plan.whole_lanes:
                    pltpu.make_async_copy(x.at[w, m, s], out.at[0, s, rows, lanes], sem).start()
                else:
                    out[0, s, rows, lanes] = x[w, m, s]
    if plan.whole_lanes:
        pltpu.make_async_copy(out, out, sem).wait()


class Plan:
    def __init__(self, sub, kt, hops, share):
        self.sub, self.kt, self.hops, self.share = sub, kt, hops, share
        self.planes = 2 * hops + 1
        self.heads = share // HD
        self.rows = self.heads * TILE
        self.cols = (1 + NB * kt) * TILE
        self.pairs = sub * kt * self.rows * self.cols
        self.whole_lanes = share % 128 == 0


def fact(plan, facts, g, i):
    own_ref, other_ref = facts
    if plan.sub == 1:
        return own_ref[i]
    return jnp.where(lax.axis_index("sub") == g, own_ref[i], other_ref[i])


def start_far(plan, facts, copies_of):
    for g in range(plan.sub):
        for j in range(NB):
            at = fact(plan, facts, g, NB * plan.kt * plan.kt + j) + (plan.hops * plan.sub + g)
            tiles_at = (at & (plan.sub - 1)) * plan.kt
            for d in range(plan.planes):
                @pl.when((at >> (plan.sub - 1)) == d)
                def _():
                    for copy in copies_of(g, j, d, tiles_at):
                        copy.start()


def mark_kernel(*refs):
    refs[-1][...] = jnp.zeros_like(refs[-1])


def head_of_lane(plan):
    return lax.broadcasted_iota(jnp.int32, (TILE, plan.share), 1) // HD


def split_heads(plan, q):
    if plan.heads == 1:
        return q
    block = head_of_lane(plan)
    return jnp.concatenate([jnp.where(block == h, q, 0) for h in range(plan.heads)], axis=0)


def scores_of(q, k):
    return lax.dot_general(q, k, (((1,), (1,)), ((), ())), preferred_element_type=jnp.float32)


def numerators(plan, facts, g, t, own, far):
    factor = HD ** -0.5 * math.log2(math.e)
    parts = [own]
    for j in range(NB):
        for k in range(plan.kt):
            keep = fact(plan, facts, g, (j * plan.kt + t) * plan.kt + k) == 1
            bias = jnp.where(keep, 0.0, NEG_SCORE)
            parts.append(far[j][:, k * TILE:(k + 1) * TILE] + bias)
    top = functools.reduce(jnp.maximum, parts)
    top = jnp.max(top, axis=1, keepdims=True)
    return [jnp.exp2((part - top) * factor).astype(jnp.bfloat16) for part in parts]


def with_ones(v):
    return jnp.concatenate([v, jnp.ones_like(v)], axis=1)


def weigh(p, v):
    return jnp.dot(p, v, preferred_element_type=jnp.float32)


def finish(plan, total):
    result = total[:TILE]
    block = head_of_lane(plan)
    both = jnp.concatenate([block, block], axis=1)
    for h in range(1, plan.heads):
        result = jnp.where(both == h, total[h * TILE:(h + 1) * TILE], result)
    return (result[:, :plan.share] / result[:, plan.share:]).astype(jnp.bfloat16)


def far_rows(plan, buffer, g, j):
    return buffer[g, j].reshape(plan.kt * TILE, plan.share)


def each_view(plan, wait, one_tile, prepare):
    count = math.gcd(plan.kt, 4)

    def some_tiles(g, t0):
        ready = prepare(g)
        for i in range(count):
            one_tile(g, t0 + i, ready)

    def one_view(g, carry):
        wait(g)
        if count == plan.kt:
            some_tiles(g, 0)
        else:
            def some(i, c):
                some_tiles(g, i * count)
                return c
            lax.fori_loop(0, plan.kt // count, some, 0)
        return carry

    lax.fori_loop(0, plan.sub, one_view, 0)


def core_kernel(plan, own, other, mixed, *refs):
    n, h = plan.planes, plan.hops
    planes = refs[:n]
    out, expo_ref, k_far, v_far, k_sem, v_sem = refs[-6:]
    facts = (own, other)
    half = TILE // 2
    low, high = pl.ds(0, half), pl.ds(half, half)
    mine = [pl.ds(b * half, half) for b in range(2)]

    def far_copies(g, j, d, tiles_at):
        tiles = pl.ds(tiles_at, plan.kt)
        found = []
        for b in range(2):
            found.append((mixed.at[tiles, 2 + d, mine[b]], k_far.at[b, g, j, :, low], k_sem.at[0, b, g, j]))
            found.append((planes[d].at[tiles, 0, mine[b]], k_far.at[b, g, j, :, high], k_sem.at[1, b, g, j]))
            if b == 0:
                found.append((planes[d].at[tiles, 1], v_far.at[g, j], v_sem.at[g, j]))
        return [pltpu.make_async_copy(*copy) for copy in found]

    start_far(plan, facts, far_copies)

    def wait(b, g):
        for j in range(NB):
            for part, rows in enumerate((low, high)):
                there = k_far.at[b, g, j, :, rows]
                pltpu.make_async_copy(there, there, k_sem.at[part, b, g, j]).wait()
            if b == 0:
                there = v_far.at[g, j]
                pltpu.make_async_copy(there, there, v_sem.at[g, j]).wait()

    def expo_of(b, g, t, k):
        at = g * plan.kt + t
        q = split_heads(plan, mixed[at, b])
        k_own = jnp.concatenate([mixed[at, 2 + h, mine[b]], planes[h][at, 0, mine[b]]], axis=0)
        return numerators(
            plan, facts, g, t, scores_of(q, k_own), [scores_of(q, k[j]) for j in range(NB)]
        )

    def keys(b, g):
        return [far_rows(plan, k_far.at[b], g, j) for j in range(NB)]

    def attended(g, t, ready):
        k, v = ready
        at = g * plan.kt + t
        expo = expo_of(0, g, t, k)
        total = weigh(expo[0], with_ones(planes[h][at, 1]))
        for j in range(NB):
            p = jnp.concatenate(expo[1 + j * plan.kt:1 + (j + 1) * plan.kt], axis=1)
            total += weigh(p, v[j])
        out[at, 0] = finish(plan, total)

    def scored(g, t, k):
        for i, part in enumerate(expo_of(1, g, t, k)):
            expo_ref[g * plan.kt + t, :, i * TILE:(i + 1) * TILE] = part

    each_view(
        plan, functools.partial(wait, 0), attended,
        lambda g: (keys(0, g), [with_ones(far_rows(plan, v_far, g, j)) for j in range(NB)]),
    )
    each_view(plan, functools.partial(wait, 1), scored, functools.partial(keys, 1))


def weigh_kernel(plan, own, other, slots, expo, done, *refs):
    n, h = plan.planes, plan.hops
    late = refs[:n]
    out, v_far, far_sem = refs[-3:]

    def stored(g, b):
        return slots[b, lax.axis_index("plane") * plan.sub + g]

    def far_copies(g, j, d, tiles_at):
        src = late[d].at[pl.ds(tiles_at, plan.kt), 0]
        return [pltpu.make_async_copy(src, v_far.at[g, j], far_sem.at[g, j])]

    start_far(plan, (own, other), far_copies)
    for g in range(plan.sub):
        for t in range(plan.kt):
            out[g * plan.kt + t, stored(g, 0)] = done[g * plan.kt + t, 0]

    def wait(g):
        for j in range(NB):
            there = v_far.at[g, j]
            pltpu.make_async_copy(there, there, far_sem.at[g, j]).wait()

    def one_tile(g, t, v):
        at = g * plan.kt + t
        wide = plan.kt * TILE
        total = weigh(expo[at, :, :TILE], with_ones(late[h][at, 0]))
        for j in range(NB):
            total += weigh(expo[at, :, TILE + j * wide:TILE + (j + 1) * wide], v[j])
        out[at, stored(g, 1)] = finish(plan, total)

    each_view(
        plan, wait, one_tile,
        lambda g: [with_ones(far_rows(plan, v_far, g, j)) for j in range(NB)],
    )


def call(kernel, name, out_shape, in_specs, out_specs, scratch, args, flops=0, exps=0, moved=0,
         mib=8):
    return pl.pallas_call(
        kernel,
        out_shape=out_shape,
        in_specs=in_specs,
        out_specs=out_specs,
        scratch_shapes=scratch,
        compiler_params=pltpu.CompilerParams(vmem_limit_bytes=mib * 2 ** 20),
        cost_estimate=pl.CostEstimate(flops=flops, bytes_accessed=moved, transcendentals=exps),
        name=name,
    )(*args)


def local(queries, keys, values, tile_mask, offsets, branch_slots):
    sub, toks = lax.axis_size("sub"), lax.axis_size("tok")
    ways = sub * toks
    dtype = queries.dtype
    _, _, tokens, width = queries.shape
    tiles, share = tokens // TILE, width // ways
    kt = toks * tiles
    hops = -(-REACH // sub)
    plan = Plan(sub, kt, hops, share)
    shifts = [d for d in range(-hops, hops + 1) if d]
    order = range(-hops, hops + 1)
    half = TILE // 2
    size = queries.size * 2

    slots = branch_slots.T
    own = jnp.concatenate([tile_mask.reshape(-1), offsets.reshape(-1)])
    other = own
    if sub == 2:
        other = lax.ppermute(own, "sub", [(0, 1), (1, 0)])
    facts = (own, other)

    place = ANY if plan.whole_lanes else VMEM
    sem = pltpu.SemaphoreType.DMA(())

    def pack(name, arrays, moves, pieces, staged=False, mark=None):
        staged = staged and plan.whole_lanes
        scratch = [sem]
        if staged:
            scratch.append(pltpu.VMEM((len(moves), tiles, TILE, width), dtype))
            scratch.append(pltpu.SemaphoreType.DMA((len(moves), tiles)))
        return call(
            functools.partial(pack_kernel, plan, moves, staged), name,
            jax.ShapeDtypeStruct((ways, tiles, pieces, TILE, share), dtype),
            [SMEM, ANY] + [ANY if staged else VMEM] * len(arrays), place, scratch,
            (slots, slots if mark is None else mark, *arrays), moved=pieces * size,
            mib=62 if staged else 8,
        )

    def spread(x):
        return exchange(x).reshape(ways * tiles, x.shape[2], TILE, share)

    def around(x, chain=False):
        found, last = {0: x}, ()
        for d in shifts:
            found[d] = from_plane(after(x, last), d)
            last = found[d] if chain else ()
        return found

    def mark(arrays, flops):
        return call(
            mark_kernel, "mark", jax.ShapeDtypeStruct((8, 128), jnp.float32),
            [ANY] * len(arrays), VMEM, [], arrays, flops=flops, mib=1,
        )

    raw = keys.reshape(1, 2, tiles, TILE, width)[:, :, :, :half].reshape(1, 2, tiles * half, width)
    raw = around(raw, chain=True)
    if plan.whole_lanes:
        packed = call(
            functools.partial(first_kernel, plan), "first",
            jax.ShapeDtypeStruct((ways, tiles, 3, TILE, share), dtype), [ANY] * 3, ANY,
            [pltpu.VMEM((4, tiles, TILE, width), dtype), pltpu.SMEM(slots.shape, jnp.int32),
             pltpu.SemaphoreType.DMA((4, tiles)), sem, sem],
            (slots, keys, values), moved=3 * size, mib=62,
        )
    else:
        packed = pack(
            "first", [keys, values],
            [Move(0, b, 0, row=half, rows=half, to=b * half) for b in range(2)]
            + [Move(1, b, 1 + b) for b in range(2)], 3,
        )
    early = spread(packed)
    arrived = mark([raw[d] for d in shifts], MARK_FLOPS[0])
    early, arrived, facts = lax.optimization_barrier((early, arrived, facts))

    heads, last_values = call(
        split_kernel, "split",
        tuple(jax.ShapeDtypeStruct((ways * tiles, n, TILE, share), dtype) for n in (2, 1)),
        [VMEM], (VMEM, VMEM), [], (early,), moved=size,
    )
    planes = around(heads)
    leads = mark([planes[shifts[0]]], MARK_FLOPS[1])
    brought = mark([planes[d] for d in shifts[1:]], MARK_FLOPS[2])
    last_values, leads = lax.optimization_barrier((last_values, leads))
    late = around(last_values)
    moves = [Move(0, 0, 0), Move(0, 1, 1)]
    for d in order:
        for b in range(2):
            moves.append(Move(
                1 + d + hops, b, 2 + d + hops, planes=d, rows=half, pitch=half, to=b * half
            ))
    packed = pack(
        "second", [queries, *[raw[d] for d in order]], moves, 2 + plan.planes, mark=arrived
    )
    mixed = spread(packed)
    planes = [planes[d] for d in order]
    late = [late[d] for d in order]

    def result(n):
        return jax.ShapeDtypeStruct((ways * tiles, n, TILE, share), dtype)

    sems = pltpu.SemaphoreType.DMA
    far = (sub, NB, kt, TILE, share)
    expo = jax.ShapeDtypeStruct((sub * kt, plan.rows, plan.cols), dtype)
    out0, expo = call(
        functools.partial(core_kernel, plan), "core", (result(1), expo),
        [SMEM] * 2 + [VMEM] + [ANY if d else VMEM for d in order] + [ANY] * 2, (VMEM, VMEM),
        [pltpu.VMEM((2, *far), dtype), pltpu.VMEM(far, dtype), sems((2, 2, sub, NB)),
         sems((sub, NB))],
        (*facts, mixed, *planes, leads, brought), flops=plan.pairs * HD * 6,
        exps=2 * plan.pairs, moved=2 * size, mib=12 if kt <= 4 else 32,
    )
    x = call(
        functools.partial(weigh_kernel, plan), "weigh", result(2),
        [SMEM] * 3 + [VMEM] * 2 + [ANY if d else VMEM for d in order], VMEM,
        [pltpu.VMEM(far, dtype), sems((sub, NB))], (*facts, slots, expo, out0, *late),
        flops=plan.pairs * HD * 2, moved=2 * size, mib=12,
    )
    x = exchange(x.reshape(ways, tiles, 2, TILE, share))
    return call(
        functools.partial(last_kernel, plan), "last",
        jax.ShapeDtypeStruct(queries.shape, dtype), [place], place, [sem], (x,),
        moved=2 * size,
    )


def solution(mesh):
    views, toks = mesh.shape["view"], mesh.shape["tok"]

    def run(queries, keys, values, tile_mask, offsets, branch_slots):
        heads = queries.shape[-1] // HD
        sub = 2 if views % 2 == 0 and heads % (2 * toks) == 0 else 1
        fine = Mesh(mesh.devices.reshape(views // sub, sub, toks), ("plane", "sub", "tok"))
        view = ("plane", "sub")
        shard = P(view, None, "tok", None)
        in_specs = (shard, shard, shard, P(view, None, None, None), P(view, None), P())
        return jax.shard_map(
            local, mesh=fine, in_specs=in_specs, out_specs=shard, check_vma=False
        )(queries, keys, values, tile_mask, offsets, branch_slots)

    return run
```

```python
import functools
import math

import jax
import jax.numpy as jnp
from jax import lax
from jax.experimental import pallas as pl
from jax.experimental.pallas import tpu as pltpu
from jax.sharding import Mesh, PartitionSpec as P

HD = 64
TILE = 128
NB = 2
REACH = 2
MARK_FLOPS = (4 * 10 ** 9, 2 * 10 ** 9, 10 ** 10)
GROUP = ("sub", "tok")

NEG_SCORE = -1e30

SMEM = pl.BlockSpec(memory_space=pltpu.SMEM)
VMEM = pl.BlockSpec(memory_space=pltpu.VMEM)
ANY = pl.BlockSpec(memory_space=pl.ANY)


def after(x, *others):
    return lax.optimization_barrier((x, others))[0]


def from_plane(x, by):
    size = lax.axis_size("plane")
    return lax.ppermute(x, "plane", [((i + by) % size, i) for i in range(size)])


def exchange(x):
    return lax.all_to_all(x, GROUP, split_axis=0, concat_axis=0, tiled=True)


class Move:
    def __init__(self, array, branch, piece, planes=0, row=0, rows=TILE, pitch=TILE, to=0):
        self.array, self.branch, self.piece, self.planes = array, branch, piece, planes
        self.row, self.rows, self.pitch, self.to = row, rows, pitch, to


def slot_of(plan, slots_ref, planes, branch):
    views = slots_ref.shape[1]
    view = (lax.axis_index("plane") + planes) * plan.sub + lax.axis_index("sub") + views
    return slots_ref[branch, lax.rem(view, views)]


def pack_kernel(plan, moves, staged, slots_ref, mark_ref, *refs):
    if staged:
        *ins, out, sem, stage, stage_sem = refs
    else:
        *ins, out, sem = refs
    ways, tiles, _, _, share = out.shape
    sources = []
    for i, move in enumerate(moves):
        slot = slot_of(plan, slots_ref, move.planes, move.branch)
        for m in range(tiles):
            rows = pl.ds(m * move.pitch + move.row, move.rows)
            source = ins[move.array].at[0, slot, rows]
            if staged:
                there = stage.at[i, m, pl.ds(0, move.rows)]
                copy = pltpu.make_async_copy(source, there, stage_sem.at[i, m])
                copy.start()
                sources.append((move, m, there, copy))
            else:
                sources.append((move, m, source, None))
    for move, m, source, copy in sources:
        if copy is not None:
            copy.wait()
        for w in range(ways):
            to, lanes = pl.ds(move.to, move.rows), pl.ds(w * share, share)
            if plan.whole_lanes:
                pltpu.make_async_copy(
                    source.at[:, lanes], out.at[w, m, move.piece, to], sem
                ).start()
            else:
                out[w, m, move.piece, to] = source[:, lanes]
    if plan.whole_lanes:
        pltpu.make_async_copy(out, out, sem).wait()


def first_kernel(plan, slots_ref, keys, values, out, stage, slots, stage_sem, slots_sem, sem):
    ways, tiles, _, _, share = out.shape
    half = TILE // 2
    ask = pltpu.make_async_copy(slots_ref, slots, slots_sem)
    ask.start()
    fetched = []
    for i, (src, row, rows) in enumerate(((keys, half, half), (values, 0, TILE))):
        for s in range(2):
            for m in range(tiles):
                there = stage.at[2 * i + s, m, pl.ds(0, rows)]
                copy = pltpu.make_async_copy(
                    src.at[0, s, pl.ds(m * TILE + row, rows)], there, stage_sem.at[2 * i + s, m]
                )
                copy.start()
                fetched.append((i, s, m, there, copy))
    ask.wait()
    view = lax.axis_index("plane") * plan.sub + lax.axis_index("sub")
    lead = slots[0, view]
    for i, s, m, there, copy in fetched:
        branch = jnp.where(lead == s, 0, 1)
        copy.wait()
        for w in range(ways):
            if i == 0:
                to = out.at[w, m, 0, pl.ds(pl.multiple_of(branch * half, half), half)]
            else:
                to = out.at[w, m, 1 + branch]
            pltpu.make_async_copy(there.at[:, pl.ds(w * share, share)], to, sem).start()
    pltpu.make_async_copy(out, out, sem).wait()


def raw_kernel(keys, out, sem):
    half = TILE // 2
    for s in range(2):
        for m in range(keys.shape[2] // TILE):
            for i in range(2):
                rows = half // 2
                pltpu.make_async_copy(
                    keys.at[0, s, pl.ds(m * TILE + i * rows, rows)],
                    out.at[0, s, pl.ds(m * half + i * rows, rows)], sem,
                ).start()
    pltpu.make_async_copy(out, out, sem).wait()


def split_kernel(x, head, tail):
    pieces = head.shape[1]
    head[...] = x[:, :pieces]
    tail[...] = x[:, pieces:]


def last_kernel(plan, x, out, sem):
    ways, tiles, slots, _, share = x.shape
    for s in range(slots):
        for m in range(tiles):
            for w in range(ways):
                rows, lanes = pl.ds(m * TILE, TILE), pl.ds(w * share, share)
                if plan.whole_lanes:
                    pltpu.make_async_copy(x.at[w, m, s], out.at[0, s, rows, lanes], sem).start()
                else:
                    out[0, s, rows, lanes] = x[w, m, s]
    if plan.whole_lanes:
        pltpu.make_async_copy(out, out, sem).wait()


class Plan:
    def __init__(self, sub, kt, hops, share):
        self.sub, self.kt, self.hops, self.share = sub, kt, hops, share
        self.planes = 2 * hops + 1
        self.heads = share // HD
        self.rows = self.heads * TILE
        self.cols = (1 + NB * kt) * TILE
        self.pairs = sub * kt * self.rows * self.cols
        self.whole_lanes = share % 128 == 0


def fact(plan, facts, g, i):
    own_ref, other_ref = facts
    if plan.sub == 1:
        return own_ref[i]
    return jnp.where(lax.axis_index("sub") == g, own_ref[i], other_ref[i])


def start_far(plan, facts, copies_of):
    for g in range(plan.sub):
        for j in range(NB):
            at = fact(plan, facts, g, NB * plan.kt * plan.kt + j) + (plan.hops * plan.sub + g)
            tiles_at = (at & (plan.sub - 1)) * plan.kt
            for d in range(plan.planes):
                @pl.when((at >> (plan.sub - 1)) == d)
                def _():
                    for copy in copies_of(g, j, d, tiles_at):
                        copy.start()


def mark_kernel(*refs):
    refs[-1][...] = jnp.zeros_like(refs[-1])


def head_of_lane(plan):
    return lax.broadcasted_iota(jnp.int32, (TILE, plan.share), 1) // HD


def split_heads(plan, q):
    if plan.heads == 1:
        return q
    block = head_of_lane(plan)
    return jnp.concatenate([jnp.where(block == h, q, 0) for h in range(plan.heads)], axis=0)


def scores_of(q, k):
    return lax.dot_general(q, k, (((1,), (1,)), ((), ())), preferred_element_type=jnp.float32)


def numerators(plan, facts, g, t, own, far):
    factor = HD ** -0.5 * math.log2(math.e)
    parts = [own]
    for j in range(NB):
        for k in range(plan.kt):
            keep = fact(plan, facts, g, (j * plan.kt + t) * plan.kt + k) == 1
            bias = jnp.where(keep, 0.0, NEG_SCORE)
            parts.append(far[j][:, k * TILE:(k + 1) * TILE] + bias)
    top = functools.reduce(jnp.maximum, parts)
    top = jnp.max(top, axis=1, keepdims=True)
    return [jnp.exp2((part - top) * factor).astype(jnp.bfloat16) for part in parts]


def with_ones(v):
    return jnp.concatenate([v, jnp.ones_like(v)], axis=1)


def weigh(p, v):
    return jnp.dot(p, v, preferred_element_type=jnp.float32)


def finish(plan, total):
    result = total[:TILE]
    block = head_of_lane(plan)
    both = jnp.concatenate([block, block], axis=1)
    for h in range(1, plan.heads):
        result = jnp.where(both == h, total[h * TILE:(h + 1) * TILE], result)
    return (result[:, :plan.share] / result[:, plan.share:]).astype(jnp.bfloat16)


def far_rows(plan, buffer, g, j):
    return buffer[g, j].reshape(plan.kt * TILE, plan.share)


def each_view(plan, wait, one_tile, prepare):
    count = math.gcd(plan.kt, 4)

    def some_tiles(g, t0):
        ready = prepare(g)
        for i in range(count):
            one_tile(g, t0 + i, ready)

    def one_view(g, carry):
        wait(g)
        if count == plan.kt:
            some_tiles(g, 0)
        else:
            def some(i, c):
                some_tiles(g, i * count)
                return c
            lax.fori_loop(0, plan.kt // count, some, 0)
        return carry

    lax.fori_loop(0, plan.sub, one_view, 0)


def core_kernel(plan, own, other, mixed, *refs):
    n, h = plan.planes, plan.hops
    planes = refs[:n]
    out, expo_ref, k_far, v_far, k_sem, v_sem = refs[-6:]
    facts = (own, other)
    half = TILE // 2
    low, high = pl.ds(0, half), pl.ds(half, half)
    mine = [pl.ds(b * half, half) for b in range(2)]

    def far_copies(b, g, j, d, tiles_at):
        tiles = pl.ds(tiles_at, plan.kt)
        to, sem = k_far.at[b, g, j], k_sem.at[:, b, g, j]
        found = [
            (mixed.at[tiles, 2 + d, mine[b]], to.at[:, low], sem.at[0]),
            (planes[d].at[tiles, 0, mine[b]], to.at[:, high], sem.at[1]),
        ]
        if b == 0:
            found.append((planes[d].at[tiles, 1], v_far.at[g, j], v_sem.at[g, j]))
        return [pltpu.make_async_copy(*copy) for copy in found]

    for b in range(2):
        start_far(plan, facts, functools.partial(far_copies, b))

    def wait(b, g):
        for j in range(NB):
            for part, rows in enumerate((low, high)):
                there = k_far.at[b, g, j, :, rows]
                pltpu.make_async_copy(there, there, k_sem.at[part, b, g, j]).wait()
            if b == 0:
                there = v_far.at[g, j]
                pltpu.make_async_copy(there, there, v_sem.at[g, j]).wait()

    def expo_of(b, g, t, k):
        at = g * plan.kt + t
        q = split_heads(plan, mixed[at, b])
        k_own = jnp.concatenate([mixed[at, 2 + h, mine[b]], planes[h][at, 0, mine[b]]], axis=0)
        return numerators(
            plan, facts, g, t, scores_of(q, k_own), [scores_of(q, k[j]) for j in range(NB)]
        )

    def keys(b, g):
        return [far_rows(plan, k_far.at[b], g, j) for j in range(NB)]

    def attended(g, t, ready):
        k, v = ready
        at = g * plan.kt + t
        expo = expo_of(0, g, t, k)
        total = weigh(expo[0], with_ones(planes[h][at, 1]))
        for j in range(NB):
            p = jnp.concatenate(expo[1 + j * plan.kt:1 + (j + 1) * plan.kt], axis=1)
            total += weigh(p, v[j])
        out[at, 0] = finish(plan, total)

    def scored(g, t, k):
        for i, part in enumerate(expo_of(1, g, t, k)):
            expo_ref[g * plan.kt + t, :, i * TILE:(i + 1) * TILE] = part

    each_view(
        plan, functools.partial(wait, 0), attended,
        lambda g: (keys(0, g), [with_ones(far_rows(plan, v_far, g, j)) for j in range(NB)]),
    )
    each_view(plan, functools.partial(wait, 1), scored, functools.partial(keys, 1))


def weigh_kernel(plan, own, other, slots, expo, done, *refs):
    n, h = plan.planes, plan.hops
    late = refs[:n]
    out, v_far, far_sem = refs[-3:]

    def stored(g, b):
        return slots[b, lax.axis_index("plane") * plan.sub + g]

    def far_copies(g, j, d, tiles_at):
        src = late[d].at[pl.ds(tiles_at, plan.kt), 0]
        return [pltpu.make_async_copy(src, v_far.at[g, j], far_sem.at[g, j])]

    start_far(plan, (own, other), far_copies)
    for g in range(plan.sub):
        for t in range(plan.kt):
            out[g * plan.kt + t, stored(g, 0)] = done[g * plan.kt + t, 0]

    def wait(g):
        for j in range(NB):
            there = v_far.at[g, j]
            pltpu.make_async_copy(there, there, far_sem.at[g, j]).wait()

    def one_tile(g, t, v):
        at = g * plan.kt + t
        wide = plan.kt * TILE
        total = weigh(expo[at, :, :TILE], with_ones(late[h][at, 0]))
        for j in range(NB):
            total += weigh(expo[at, :, TILE + j * wide:TILE + (j + 1) * wide], v[j])
        out[at, stored(g, 1)] = finish(plan, total)

    each_view(
        plan, wait, one_tile,
        lambda g: [with_ones(far_rows(plan, v_far, g, j)) for j in range(NB)],
    )


def call(kernel, name, out_shape, in_specs, out_specs, scratch, args, flops=0, exps=0, moved=0,
         mib=8):
    return pl.pallas_call(
        kernel,
        out_shape=out_shape,
        in_specs=in_specs,
        out_specs=out_specs,
        scratch_shapes=scratch,
        compiler_params=pltpu.CompilerParams(vmem_limit_bytes=mib * 2 ** 20),
        cost_estimate=pl.CostEstimate(flops=flops, bytes_accessed=moved, transcendentals=exps),
        name=name,
    )(*args)


def local(queries, keys, values, tile_mask, offsets, branch_slots):
    sub, toks = lax.axis_size("sub"), lax.axis_size("tok")
    ways = sub * toks
    dtype = queries.dtype
    _, _, tokens, width = queries.shape
    tiles, share = tokens // TILE, width // ways
    kt = toks * tiles
    hops = -(-REACH // sub)
    plan = Plan(sub, kt, hops, share)
    shifts = [d for d in range(-hops, hops + 1) if d]
    order = range(-hops, hops + 1)
    half = TILE // 2
    size = queries.size * 2

    slots = branch_slots.T
    own = jnp.concatenate([tile_mask.reshape(-1), offsets.reshape(-1)])
    other = own
    if sub == 2:
        other = lax.ppermute(own, "sub", [(0, 1), (1, 0)])
    facts = (own, other)

    place = ANY if plan.whole_lanes else VMEM
    sem = pltpu.SemaphoreType.DMA(())

    def pack(name, arrays, moves, pieces, staged=False, mark=None):
        staged = staged and plan.whole_lanes
        scratch = [sem]
        if staged:
            scratch.append(pltpu.VMEM((len(moves), tiles, TILE, width), dtype))
            scratch.append(pltpu.SemaphoreType.DMA((len(moves), tiles)))
        return call(
            functools.partial(pack_kernel, plan, moves, staged), name,
            jax.ShapeDtypeStruct((ways, tiles, pieces, TILE, share), dtype),
            [SMEM, ANY] + [ANY if staged else VMEM] * len(arrays), place, scratch,
            (slots, slots if mark is None else mark, *arrays), moved=pieces * size,
            mib=62 if staged else 8,
        )

    def spread(x):
        return exchange(x).reshape(ways * tiles, x.shape[2], TILE, share)

    def around(x, chain=False):
        found, last = {0: x}, ()
        for d in shifts:
            found[d] = from_plane(after(x, last), d)
            last = found[d] if chain else ()
        return found

    def mark(arrays, flops):
        return call(
            mark_kernel, "mark", jax.ShapeDtypeStruct((8, 128), jnp.float32),
            [ANY] * len(arrays), VMEM, [], arrays, flops=flops, mib=1,
        )

    raw = call(
        raw_kernel, "raw", jax.ShapeDtypeStruct((1, 2, tiles * half, width), dtype), [ANY], ANY,
        [sem], (keys,), moved=size, mib=1,
    )
    raw = around(raw, chain=True)
    if plan.whole_lanes:
        packed = call(
            functools.partial(first_kernel, plan), "first",
            jax.ShapeDtypeStruct((ways, tiles, 3, TILE, share), dtype), [ANY] * 3, ANY,
            [pltpu.VMEM((4, tiles, TILE, width), dtype), pltpu.SMEM(slots.shape, jnp.int32),
             pltpu.SemaphoreType.DMA((4, tiles)), sem, sem],
            (slots, keys, values), moved=3 * size, mib=62,
        )
    else:
        packed = pack(
            "first", [keys, values],
            [Move(0, b, 0, row=half, rows=half, to=b * half) for b in range(2)]
            + [Move(1, b, 1 + b) for b in range(2)], 3,
        )
    early = spread(packed)
    arrived = mark([raw[d] for d in shifts], MARK_FLOPS[0])
    early, arrived, facts = lax.optimization_barrier((early, arrived, facts))

    heads, last_values = call(
        split_kernel, "split",
        tuple(jax.ShapeDtypeStruct((ways * tiles, n, TILE, share), dtype) for n in (2, 1)),
        [VMEM], (VMEM, VMEM), [], (early,), moved=size,
    )
    planes = around(heads)
    leads = mark([planes[shifts[0]]], MARK_FLOPS[1])
    brought = mark([planes[d] for d in shifts[1:]], MARK_FLOPS[2])
    last_values, leads = lax.optimization_barrier((last_values, leads))
    late = around(last_values)
    moves = [Move(0, 0, 0), Move(0, 1, 1)]
    for d in order:
        for b in range(2):
            moves.append(Move(
                1 + d + hops, b, 2 + d + hops, planes=d, rows=half, pitch=half, to=b * half
            ))
    packed = pack(
        "second", [queries, *[raw[d] for d in order]], moves, 2 + plan.planes, mark=arrived
    )
    mixed = spread(packed)
    planes = [planes[d] for d in order]
    late = [late[d] for d in order]

    def result(n):
        return jax.ShapeDtypeStruct((ways * tiles, n, TILE, share), dtype)

    sems = pltpu.SemaphoreType.DMA
    far = (sub, NB, kt, TILE, share)
    expo = jax.ShapeDtypeStruct((sub * kt, plan.rows, plan.cols), dtype)
    out0, expo = call(
        functools.partial(core_kernel, plan), "core", (result(1), expo),
        [SMEM] * 2 + [VMEM] + [ANY if d else VMEM for d in order] + [ANY] * 2, (VMEM, VMEM),
        [pltpu.VMEM((2, *far), dtype), pltpu.VMEM(far, dtype), sems((2, 2, sub, NB)),
         sems((sub, NB))],
        (*facts, mixed, *planes, leads, brought), flops=plan.pairs * HD * 6,
        exps=2 * plan.pairs, moved=2 * size, mib=12 if kt <= 4 else 32,
    )
    x = call(
        functools.partial(weigh_kernel, plan), "weigh", result(2),
        [SMEM] * 3 + [VMEM] * 2 + [ANY if d else VMEM for d in order], VMEM,
        [pltpu.VMEM(far, dtype), sems((sub, NB))], (*facts, slots, expo, out0, *late),
        flops=plan.pairs * HD * 2, moved=2 * size, mib=12,
    )
    x = exchange(x.reshape(ways, tiles, 2, TILE, share))
    return call(
        functools.partial(last_kernel, plan), "last",
        jax.ShapeDtypeStruct(queries.shape, dtype), [place], place, [sem], (x,),
        moved=2 * size,
    )


def solution(mesh):
    views, toks = mesh.shape["view"], mesh.shape["tok"]

    def run(queries, keys, values, tile_mask, offsets, branch_slots):
        heads = queries.shape[-1] // HD
        sub = 2 if views % 2 == 0 and heads % (2 * toks) == 0 else 1
        fine = Mesh(mesh.devices.reshape(views // sub, sub, toks), ("plane", "sub", "tok"))
        view = ("plane", "sub")
        shard = P(view, None, "tok", None)
        in_specs = (shard, shard, shard, P(view, None, None, None), P(view, None), P())
        return jax.shard_map(
            local, mesh=fine, in_specs=in_specs, out_specs=shard, check_vma=False
        )(queries, keys, values, tile_mask, offsets, branch_slots)

    return run
```

```python
import functools
import math

import jax
import jax.numpy as jnp
from jax import lax
from jax.experimental import pallas as pl
from jax.experimental.pallas import tpu as pltpu
from jax.sharding import Mesh, PartitionSpec as P

HD = 64
TILE = 128
NB = 2
REACH = 2
MARK_FLOPS = (4 * 10 ** 9, 2 * 10 ** 9, 10 ** 10)
GROUP = ("sub", "tok")

NEG_SCORE = -1e30

SMEM = pl.BlockSpec(memory_space=pltpu.SMEM)
VMEM = pl.BlockSpec(memory_space=pltpu.VMEM)
ANY = pl.BlockSpec(memory_space=pl.ANY)


def after(x, *others):
    return lax.optimization_barrier((x, others))[0]


def from_plane(x, by):
    size = lax.axis_size("plane")
    return lax.ppermute(x, "plane", [((i + by) % size, i) for i in range(size)])


def exchange(x):
    return lax.all_to_all(x, GROUP, split_axis=0, concat_axis=0, tiled=True)


class Move:
    def __init__(self, array, branch, piece, planes=0, row=0, rows=TILE, pitch=TILE, to=0):
        self.array, self.branch, self.piece, self.planes = array, branch, piece, planes
        self.row, self.rows, self.pitch, self.to = row, rows, pitch, to


def slot_of(plan, slots_ref, planes, branch):
    views = slots_ref.shape[1]
    view = (lax.axis_index("plane") + planes) * plan.sub + lax.axis_index("sub") + views
    return slots_ref[branch, lax.rem(view, views)]


def pack_kernel(plan, moves, staged, slots_ref, mark_ref, *refs):
    if staged:
        *ins, out, sem, stage, stage_sem = refs
    else:
        *ins, out, sem = refs
    ways, tiles, _, _, share = out.shape
    sources = []
    for i, move in enumerate(moves):
        slot = slot_of(plan, slots_ref, move.planes, move.branch)
        for m in range(tiles):
            rows = pl.ds(m * move.pitch + move.row, move.rows)
            source = ins[move.array].at[0, slot, rows]
            if staged:
                there = stage.at[i, m, pl.ds(0, move.rows)]
                copy = pltpu.make_async_copy(source, there, stage_sem.at[i, m])
                copy.start()
                sources.append((move, m, there, copy))
            else:
                sources.append((move, m, source, None))
    for move, m, source, copy in sources:
        if copy is not None:
            copy.wait()
        for w in range(ways):
            to, lanes = pl.ds(move.to, move.rows), pl.ds(w * share, share)
            if plan.whole_lanes:
                pltpu.make_async_copy(
                    source.at[:, lanes], out.at[w, m, move.piece, to], sem
                ).start()
            else:
                out[w, m, move.piece, to] = source[:, lanes]
    if plan.whole_lanes:
        pltpu.make_async_copy(out, out, sem).wait()


def first_kernel(plan, slots_ref, keys, values, out, stage, slots, stage_sem, slots_sem, sem):
    ways, tiles, _, _, share = out.shape
    half = TILE // 2
    ask = pltpu.make_async_copy(slots_ref, slots, slots_sem)
    ask.start()
    fetched = []
    for i, (src, row, rows) in enumerate(((keys, half, half), (values, 0, TILE))):
        for s in range(2):
            for m in range(tiles):
                there = stage.at[2 * i + s, m, pl.ds(0, rows)]
                copy = pltpu.make_async_copy(
                    src.at[0, s, pl.ds(m * TILE + row, rows)], there, stage_sem.at[2 * i + s, m]
                )
                copy.start()
                fetched.append((i, s, m, there, copy))
    ask.wait()
    view = lax.axis_index("plane") * plan.sub + lax.axis_index("sub")
    lead = slots[0, view]
    for i, s, m, there, copy in fetched:
        branch = jnp.where(lead == s, 0, 1)
        copy.wait()
        for w in range(ways):
            if i == 0:
                to = out.at[w, m, 0, pl.ds(pl.multiple_of(branch * half, half), half)]
            else:
                to = out.at[w, m, 1 + branch]
            pltpu.make_async_copy(there.at[:, pl.ds(w * share, share)], to, sem).start()
    pltpu.make_async_copy(out, out, sem).wait()


def split_kernel(x, head, tail):
    pieces = head.shape[1]
    head[...] = x[:, :pieces]
    tail[...] = x[:, pieces:]


def last_kernel(plan, x, out, sem):
    ways, tiles, slots, _, share = x.shape
    for s in range(slots):
        for m in range(tiles):
            for w in range(ways):
                rows, lanes = pl.ds(m * TILE, TILE), pl.ds(w * share, share)
                if plan.whole_lanes:
                    pltpu.make_async_copy(x.at[w, m, s], out.at[0, s, rows, lanes], sem).start()
                else:
                    out[0, s, rows, lanes] = x[w, m, s]
    if plan.whole_lanes:
        pltpu.make_async_copy(out, out, sem).wait()


class Plan:
    def __init__(self, sub, kt, hops, share):
        self.sub, self.kt, self.hops, self.share = sub, kt, hops, share
        self.planes = 2 * hops + 1
        self.heads = share // HD
        self.rows = self.heads * TILE
        self.cols = (1 + NB * kt) * TILE
        self.pairs = sub * kt * self.rows * self.cols
        self.whole_lanes = share % 128 == 0


def fact(plan, facts, g, i):
    own_ref, other_ref = facts
    if plan.sub == 1:
        return own_ref[i]
    return jnp.where(lax.axis_index("sub") == g, own_ref[i], other_ref[i])


def start_far(plan, facts, copies_of):
    for g in range(plan.sub):
        for j in range(NB):
            at = fact(plan, facts, g, NB * plan.kt * plan.kt + j) + (plan.hops * plan.sub + g)
            tiles_at = (at & (plan.sub - 1)) * plan.kt
            for d in range(plan.planes):
                @pl.when((at >> (plan.sub - 1)) == d)
                def _():
                    for copy in copies_of(g, j, d, tiles_at):
                        copy.start()


def mark_kernel(*refs):
    refs[-1][...] = jnp.zeros_like(refs[-1])


def head_of_lane(plan):
    return lax.broadcasted_iota(jnp.int32, (TILE, plan.share), 1) // HD


def split_heads(plan, q):
    if plan.heads == 1:
        return q
    block = head_of_lane(plan)
    return jnp.concatenate([jnp.where(block == h, q, 0) for h in range(plan.heads)], axis=0)


def scores_of(q, k):
    return lax.dot_general(q, k, (((1,), (1,)), ((), ())), preferred_element_type=jnp.float32)


def numerators(plan, facts, g, t, own, far):
    factor = HD ** -0.5 * math.log2(math.e)
    parts = [own]
    for j in range(NB):
        for k in range(plan.kt):
            keep = fact(plan, facts, g, (j * plan.kt + t) * plan.kt + k) == 1
            bias = jnp.where(keep, 0.0, NEG_SCORE)
            parts.append(far[j][:, k * TILE:(k + 1) * TILE] + bias)
    top = functools.reduce(jnp.maximum, parts)
    top = jnp.max(top, axis=1, keepdims=True) * factor
    return [jnp.exp2(part * factor - top).astype(jnp.bfloat16) for part in parts]


def with_ones(v):
    return jnp.concatenate([v, jnp.ones_like(v)], axis=1)


def weigh(p, v):
    return jnp.dot(p, v, preferred_element_type=jnp.float32)


def finish(plan, total):
    result = total[:TILE]
    block = head_of_lane(plan)
    both = jnp.concatenate([block, block], axis=1)
    for h in range(1, plan.heads):
        result = jnp.where(both == h, total[h * TILE:(h + 1) * TILE], result)
    return (result[:, :plan.share] / result[:, plan.share:]).astype(jnp.bfloat16)


def far_rows(plan, buffer, g, j):
    return buffer[g, j].reshape(plan.kt * TILE, plan.share)


def each_view(plan, wait, one_tile, prepare):
    count = math.gcd(plan.kt, 4)

    def some_tiles(g, t0):
        ready = prepare(g)
        for i in range(count):
            one_tile(g, t0 + i, ready)

    def one_view(g, carry):
        wait(g)
        if count == plan.kt:
            some_tiles(g, 0)
        else:
            def some(i, c):
                some_tiles(g, i * count)
                return c
            lax.fori_loop(0, plan.kt // count, some, 0)
        return carry

    lax.fori_loop(0, plan.sub, one_view, 0)


def core_kernel(plan, own, other, mixed, *refs):
    n, h = plan.planes, plan.hops
    planes = refs[:n]
    out, expo_ref, k_far, v_far, k_sem, v_sem = refs[-6:]
    facts = (own, other)
    half = TILE // 2
    low, high = pl.ds(0, half), pl.ds(half, half)
    mine = [pl.ds(b * half, half) for b in range(2)]

    def far_copies(b, g, j, d, tiles_at):
        tiles = pl.ds(tiles_at, plan.kt)
        to, sem = k_far.at[b, g, j], k_sem.at[:, b, g, j]
        found = [
            (mixed.at[tiles, 2 + d, mine[b]], to.at[:, low], sem.at[0]),
            (planes[d].at[tiles, 0, mine[b]], to.at[:, high], sem.at[1]),
        ]
        if b == 0:
            found.append((planes[d].at[tiles, 1], v_far.at[g, j], v_sem.at[g, j]))
        return [pltpu.make_async_copy(*copy) for copy in found]

    for b in range(2):
        start_far(plan, facts, functools.partial(far_copies, b))

    def wait(b, g):
        for j in range(NB):
            for part, rows in enumerate((low, high)):
                there = k_far.at[b, g, j, :, rows]
                pltpu.make_async_copy(there, there, k_sem.at[part, b, g, j]).wait()
            if b == 0:
                there = v_far.at[g, j]
                pltpu.make_async_copy(there, there, v_sem.at[g, j]).wait()

    def expo_of(b, g, t, k):
        at = g * plan.kt + t
        q = split_heads(plan, mixed[at, b])
        k_own = jnp.concatenate([mixed[at, 2 + h, mine[b]], planes[h][at, 0, mine[b]]], axis=0)
        return numerators(
            plan, facts, g, t, scores_of(q, k_own), [scores_of(q, k[j]) for j in range(NB)]
        )

    def keys(b, g):
        return [far_rows(plan, k_far.at[b], g, j) for j in range(NB)]

    def attended(g, t, ready):
        k, v = ready
        at = g * plan.kt + t
        expo = expo_of(0, g, t, k)
        total = weigh(expo[0], with_ones(planes[h][at, 1]))
        for j in range(NB):
            p = jnp.concatenate(expo[1 + j * plan.kt:1 + (j + 1) * plan.kt], axis=1)
            total += weigh(p, v[j])
        out[at, 0] = finish(plan, total)

    def scored(g, t, k):
        for i, part in enumerate(expo_of(1, g, t, k)):
            expo_ref[g * plan.kt + t, :, i * TILE:(i + 1) * TILE] = part

    each_view(
        plan, functools.partial(wait, 0), attended,
        lambda g: (keys(0, g), [with_ones(far_rows(plan, v_far, g, j)) for j in range(NB)]),
    )
    each_view(plan, functools.partial(wait, 1), scored, functools.partial(keys, 1))


def weigh_kernel(plan, own, other, slots, expo, done, *refs):
    n, h = plan.planes, plan.hops
    late = refs[:n]
    out, v_far, far_sem = refs[-3:]

    def stored(g, b):
        return slots[b, lax.axis_index("plane") * plan.sub + g]

    def far_copies(g, j, d, tiles_at):
        src = late[d].at[pl.ds(tiles_at, plan.kt), 0]
        return [pltpu.make_async_copy(src, v_far.at[g, j], far_sem.at[g, j])]

    start_far(plan, (own, other), far_copies)
    for g in range(plan.sub):
        for t in range(plan.kt):
            out[g * plan.kt + t, stored(g, 0)] = done[g * plan.kt + t, 0]

    def wait(g):
        for j in range(NB):
            there = v_far.at[g, j]
            pltpu.make_async_copy(there, there, far_sem.at[g, j]).wait()

    def one_tile(g, t, v):
        at = g * plan.kt + t
        wide = plan.kt * TILE
        total = weigh(expo[at, :, :TILE], with_ones(late[h][at, 0]))
        for j in range(NB):
            total += weigh(expo[at, :, TILE + j * wide:TILE + (j + 1) * wide], v[j])
        out[at, stored(g, 1)] = finish(plan, total)

    each_view(
        plan, wait, one_tile,
        lambda g: [with_ones(far_rows(plan, v_far, g, j)) for j in range(NB)],
    )


def call(kernel, name, out_shape, in_specs, out_specs, scratch, args, flops=0, exps=0, moved=0,
         mib=8):
    return pl.pallas_call(
        kernel,
        out_shape=out_shape,
        in_specs=in_specs,
        out_specs=out_specs,
        scratch_shapes=scratch,
        compiler_params=pltpu.CompilerParams(vmem_limit_bytes=mib * 2 ** 20),
        cost_estimate=pl.CostEstimate(flops=flops, bytes_accessed=moved, transcendentals=exps),
        name=name,
    )(*args)


def local(queries, keys, values, tile_mask, offsets, branch_slots):
    sub, toks = lax.axis_size("sub"), lax.axis_size("tok")
    ways = sub * toks
    dtype = queries.dtype
    _, _, tokens, width = queries.shape
    tiles, share = tokens // TILE, width // ways
    kt = toks * tiles
    hops = -(-REACH // sub)
    plan = Plan(sub, kt, hops, share)
    shifts = [d for d in range(-hops, hops + 1) if d]
    order = range(-hops, hops + 1)
    half = TILE // 2
    size = queries.size * 2

    slots = branch_slots.T
    own = jnp.concatenate([tile_mask.reshape(-1), offsets.reshape(-1)])
    other = own
    if sub == 2:
        other = lax.ppermute(own, "sub", [(0, 1), (1, 0)])
    facts = (own, other)

    place = ANY if plan.whole_lanes else VMEM
    sem = pltpu.SemaphoreType.DMA(())

    def pack(name, arrays, moves, pieces, staged=False, mark=None):
        staged = staged and plan.whole_lanes
        scratch = [sem]
        if staged:
            scratch.append(pltpu.VMEM((len(moves), tiles, TILE, width), dtype))
            scratch.append(pltpu.SemaphoreType.DMA((len(moves), tiles)))
        return call(
            functools.partial(pack_kernel, plan, moves, staged), name,
            jax.ShapeDtypeStruct((ways, tiles, pieces, TILE, share), dtype),
            [SMEM, ANY] + [ANY if staged else VMEM] * len(arrays), place, scratch,
            (slots, slots if mark is None else mark, *arrays), moved=pieces * size,
            mib=62 if staged else 8,
        )

    def spread(x):
        return exchange(x).reshape(ways * tiles, x.shape[2], TILE, share)

    def around(x, chain=False):
        found, last = {0: x}, ()
        for d in shifts:
            found[d] = from_plane(after(x, last), d)
            last = found[d] if chain else ()
        return found

    def mark(arrays, flops):
        return call(
            mark_kernel, "mark", jax.ShapeDtypeStruct((8, 128), jnp.float32),
            [ANY] * len(arrays), VMEM, [], arrays, flops=flops, mib=1,
        )

    raw = keys.reshape(1, 2, tiles, TILE, width)[:, :, :, :half].reshape(1, 2, tiles * half, width)
    raw = around(raw, chain=True)
    if plan.whole_lanes:
        packed = call(
            functools.partial(first_kernel, plan), "first",
            jax.ShapeDtypeStruct((ways, tiles, 3, TILE, share), dtype), [ANY] * 3, ANY,
            [pltpu.VMEM((4, tiles, TILE, width), dtype), pltpu.SMEM(slots.shape, jnp.int32),
             pltpu.SemaphoreType.DMA((4, tiles)), sem, sem],
            (slots, keys, values), moved=3 * size, mib=62,
        )
    else:
        packed = pack(
            "first", [keys, values],
            [Move(0, b, 0, row=half, rows=half, to=b * half) for b in range(2)]
            + [Move(1, b, 1 + b) for b in range(2)], 3,
        )
    early = spread(packed)
    arrived = mark([raw[d] for d in shifts], MARK_FLOPS[0])
    early, arrived, facts = lax.optimization_barrier((early, arrived, facts))

    heads, last_values = call(
        split_kernel, "split",
        tuple(jax.ShapeDtypeStruct((ways * tiles, n, TILE, share), dtype) for n in (2, 1)),
        [VMEM], (VMEM, VMEM), [], (early,), moved=size,
    )
    planes = around(heads)
    leads = mark([planes[shifts[0]]], MARK_FLOPS[1])
    brought = mark([planes[d] for d in shifts[1:]], MARK_FLOPS[2])
    last_values, leads = lax.optimization_barrier((last_values, leads))
    late = around(last_values)
    moves = [Move(0, 0, 0), Move(0, 1, 1)]
    for d in order:
        for b in range(2):
            moves.append(Move(
                1 + d + hops, b, 2 + d + hops, planes=d, rows=half, pitch=half, to=b * half
            ))
    packed = pack(
        "second", [queries, *[raw[d] for d in order]], moves, 2 + plan.planes, mark=arrived
    )
    mixed = spread(packed)
    planes = [planes[d] for d in order]
    late = [late[d] for d in order]

    def result(n):
        return jax.ShapeDtypeStruct((ways * tiles, n, TILE, share), dtype)

    sems = pltpu.SemaphoreType.DMA
    far = (sub, NB, kt, TILE, share)
    expo = jax.ShapeDtypeStruct((sub * kt, plan.rows, plan.cols), dtype)
    out0, expo = call(
        functools.partial(core_kernel, plan), "core", (result(1), expo),
        [SMEM] * 2 + [VMEM] + [ANY if d else VMEM for d in order] + [ANY] * 2, (VMEM, VMEM),
        [pltpu.VMEM((2, *far), dtype), pltpu.VMEM(far, dtype), sems((2, 2, sub, NB)),
         sems((sub, NB))],
        (*facts, mixed, *planes, leads, brought), flops=plan.pairs * HD * 6,
        exps=2 * plan.pairs, moved=2 * size, mib=12 if kt <= 4 else 32,
    )
    x = call(
        functools.partial(weigh_kernel, plan), "weigh", result(2),
        [SMEM] * 3 + [VMEM] * 2 + [ANY if d else VMEM for d in order], VMEM,
        [pltpu.VMEM(far, dtype), sems((sub, NB))], (*facts, slots, expo, out0, *late),
        flops=plan.pairs * HD * 2, moved=2 * size, mib=12,
    )
    x = exchange(x.reshape(ways, tiles, 2, TILE, share))
    return call(
        functools.partial(last_kernel, plan), "last",
        jax.ShapeDtypeStruct(queries.shape, dtype), [place], place, [sem], (x,),
        moved=2 * size,
    )


def solution(mesh):
    views, toks = mesh.shape["view"], mesh.shape["tok"]

    def run(queries, keys, values, tile_mask, offsets, branch_slots):
        heads = queries.shape[-1] // HD
        sub = 2 if views % 2 == 0 and heads % (2 * toks) == 0 else 1
        fine = Mesh(mesh.devices.reshape(views // sub, sub, toks), ("plane", "sub", "tok"))
        view = ("plane", "sub")
        shard = P(view, None, "tok", None)
        in_specs = (shard, shard, shard, P(view, None, None, None), P(view, None), P())
        return jax.shard_map(
            local, mesh=fine, in_specs=in_specs, out_specs=shard, check_vma=False
        )(queries, keys, values, tile_mask, offsets, branch_slots)

    return run
```

```python
import functools
import math

import jax
import jax.numpy as jnp
from jax import lax
from jax.experimental import pallas as pl
from jax.experimental.pallas import tpu as pltpu
from jax.sharding import Mesh, PartitionSpec as P

HD = 64
TILE = 128
NB = 2
REACH = 2
MARK_FLOPS = (4 * 10 ** 9, 2 * 10 ** 9, 10 ** 10)
GROUP = ("sub", "tok")

NEG_SCORE = -1e30

SMEM = pl.BlockSpec(memory_space=pltpu.SMEM)
VMEM = pl.BlockSpec(memory_space=pltpu.VMEM)
ANY = pl.BlockSpec(memory_space=pl.ANY)


def after(x, *others):
    return lax.optimization_barrier((x, others))[0]


def from_plane(x, by):
    size = lax.axis_size("plane")
    return lax.ppermute(x, "plane", [((i + by) % size, i) for i in range(size)])


def exchange(x):
    return lax.all_to_all(x, GROUP, split_axis=0, concat_axis=0, tiled=True)


class Move:
    def __init__(self, array, branch, piece, planes=0, row=0, rows=TILE, pitch=TILE, to=0):
        self.array, self.branch, self.piece, self.planes = array, branch, piece, planes
        self.row, self.rows, self.pitch, self.to = row, rows, pitch, to


def slot_of(plan, slots_ref, planes, branch):
    views = slots_ref.shape[1]
    view = (lax.axis_index("plane") + planes) * plan.sub + lax.axis_index("sub") + views
    return slots_ref[branch, lax.rem(view, views)]


def pack_kernel(plan, moves, staged, slots_ref, mark_ref, *refs):
    if staged:
        *ins, out, sem, stage, stage_sem = refs
    else:
        *ins, out, sem = refs
    ways, tiles, _, _, share = out.shape
    sources = []
    for i, move in enumerate(moves):
        slot = slot_of(plan, slots_ref, move.planes, move.branch)
        for m in range(tiles):
            rows = pl.ds(m * move.pitch + move.row, move.rows)
            source = ins[move.array].at[0, slot, rows]
            if staged:
                there = stage.at[i, m, pl.ds(0, move.rows)]
                copy = pltpu.make_async_copy(source, there, stage_sem.at[i, m])
                copy.start()
                sources.append((move, m, there, copy))
            else:
                sources.append((move, m, source, None))
    for move, m, source, copy in sources:
        if copy is not None:
            copy.wait()
        for w in range(ways):
            to, lanes = pl.ds(move.to, move.rows), pl.ds(w * share, share)
            if plan.whole_lanes:
                pltpu.make_async_copy(
                    source.at[:, lanes], out.at[w, m, move.piece, to], sem
                ).start()
            else:
                out[w, m, move.piece, to] = source[:, lanes]
    if plan.whole_lanes:
        pltpu.make_async_copy(out, out, sem).wait()


def first_kernel(plan, slots_ref, keys, values, out, stage, slots, stage_sem, slots_sem, sem):
    ways, tiles, _, _, share = out.shape
    half = TILE // 2
    ask = pltpu.make_async_copy(slots_ref, slots, slots_sem)
    ask.start()
    fetched = []
    for i, (src, row, rows) in enumerate(((keys, half, half), (values, 0, TILE))):
        for s in range(2):
            for m in range(tiles):
                there = stage.at[2 * i + s, m, pl.ds(0, rows)]
                copy = pltpu.make_async_copy(
                    src.at[0, s, pl.ds(m * TILE + row, rows)], there, stage_sem.at[2 * i + s, m]
                )
                copy.start()
                fetched.append((i, s, m, there, copy))
    ask.wait()
    view = lax.axis_index("plane") * plan.sub + lax.axis_index("sub")
    lead = slots[0, view]
    for i, s, m, there, copy in fetched:
        branch = jnp.where(lead == s, 0, 1)
        copy.wait()
        for w in range(ways):
            if i == 0:
                to = out.at[w, m, 0, pl.ds(pl.multiple_of(branch * half, half), half)]
            else:
                to = out.at[w, m, 1 + branch]
            pltpu.make_async_copy(there.at[:, pl.ds(w * share, share)], to, sem).start()
    pltpu.make_async_copy(out, out, sem).wait()


def split_kernel(x, head, tail):
    pieces = head.shape[1]
    head[...] = x[:, :pieces]
    tail[...] = x[:, pieces:]


def last_kernel(plan, x, out, sem):
    ways, tiles, slots, _, share = x.shape
    for s in range(slots):
        for m in range(tiles):
            for w in range(ways):
                rows, lanes = pl.ds(m * TILE, TILE), pl.ds(w * share, share)
                if plan.whole_lanes:
                    pltpu.make_async_copy(x.at[w, m, s], out.at[0, s, rows, lanes], sem).start()
                else:
                    out[0, s, rows, lanes] = x[w, m, s]
    if plan.whole_lanes:
        pltpu.make_async_copy(out, out, sem).wait()


class Plan:
    def __init__(self, sub, kt, hops, share):
        self.sub, self.kt, self.hops, self.share = sub, kt, hops, share
        self.planes = 2 * hops + 1
        self.heads = share // HD
        self.rows = self.heads * TILE
        self.cols = (1 + NB * kt) * TILE
        self.pairs = sub * kt * self.rows * self.cols
        self.whole_lanes = share % 128 == 0


def fact(plan, facts, g, i):
    own_ref, other_ref = facts
    if plan.sub == 1:
        return own_ref[i]
    return jnp.where(lax.axis_index("sub") == g, own_ref[i], other_ref[i])


def start_far(plan, facts, copies_of):
    for g in range(plan.sub):
        for j in range(NB):
            at = fact(plan, facts, g, NB * plan.kt * plan.kt + j) + (plan.hops * plan.sub + g)
            tiles_at = (at & (plan.sub - 1)) * plan.kt
            for d in range(plan.planes):
                @pl.when((at >> (plan.sub - 1)) == d)
                def _():
                    for copy in copies_of(g, j, d, tiles_at):
                        copy.start()


def mark_kernel(*refs):
    refs[-1][...] = jnp.zeros_like(refs[-1])


def head_of_lane(plan):
    return lax.broadcasted_iota(jnp.int32, (TILE, plan.share), 1) // HD


def split_heads(plan, q):
    if plan.heads == 1:
        return q
    block = head_of_lane(plan)
    return jnp.concatenate([jnp.where(block == h, q, 0) for h in range(plan.heads)], axis=0)


def scores_of(q, k):
    return lax.dot_general(q, k, (((1,), (1,)), ((), ())), preferred_element_type=jnp.float32)


def numerators(plan, facts, g, t, own, far):
    factor = HD ** -0.5 * math.log2(math.e)
    parts = [own]
    for j in range(NB):
        for k in range(plan.kt):
            keep = fact(plan, facts, g, (j * plan.kt + t) * plan.kt + k) == 1
            bias = jnp.where(keep, 0.0, NEG_SCORE)
            parts.append(far[j][:, k * TILE:(k + 1) * TILE] + bias)
    top = functools.reduce(jnp.maximum, parts)
    top = jnp.max(top, axis=1, keepdims=True) * factor
    return [jnp.exp2(part * factor - top).astype(jnp.bfloat16) for part in parts]


def with_ones(v):
    return jnp.concatenate([v, jnp.ones_like(v)], axis=1)


def weigh(p, v):
    return jnp.dot(p, v, preferred_element_type=jnp.float32)


def finish(plan, total):
    result = total[:TILE]
    block = head_of_lane(plan)
    both = jnp.concatenate([block, block], axis=1)
    for h in range(1, plan.heads):
        result = jnp.where(both == h, total[h * TILE:(h + 1) * TILE], result)
    return (result[:, :plan.share] / result[:, plan.share:]).astype(jnp.bfloat16)


def far_rows(plan, buffer, g, j):
    return buffer[g, j].reshape(plan.kt * TILE, plan.share)


def each_view(plan, wait, one_tile, prepare):
    count = math.gcd(plan.kt, 4)

    def some_tiles(g, t0):
        ready = prepare(g)
        for i in range(count):
            one_tile(g, t0 + i, ready)

    def one_view(g, carry):
        wait(g)
        if count == plan.kt:
            some_tiles(g, 0)
        else:
            def some(i, c):
                some_tiles(g, i * count)
                return c
            lax.fori_loop(0, plan.kt // count, some, 0)
        return carry

    for g in range(plan.sub):
        one_view(g, 0)


def core_kernel(plan, own, other, mixed, *refs):
    n, h = plan.planes, plan.hops
    planes = refs[:n]
    out, expo_ref, k_far, v_far, k_sem, v_sem = refs[-6:]
    facts = (own, other)
    half = TILE // 2
    low, high = pl.ds(0, half), pl.ds(half, half)
    mine = [pl.ds(b * half, half) for b in range(2)]

    def far_copies(b, g, j, d, tiles_at):
        tiles = pl.ds(tiles_at, plan.kt)
        to, sem = k_far.at[b, g, j], k_sem.at[:, b, g, j]
        found = [
            (mixed.at[tiles, 2 + d, mine[b]], to.at[:, low], sem.at[0]),
            (planes[d].at[tiles, 0, mine[b]], to.at[:, high], sem.at[1]),
        ]
        if b == 0:
            found.append((planes[d].at[tiles, 1], v_far.at[g, j], v_sem.at[g, j]))
        return [pltpu.make_async_copy(*copy) for copy in found]

    for b in range(2):
        start_far(plan, facts, functools.partial(far_copies, b))

    def wait(b, g):
        for j in range(NB):
            for part, rows in enumerate((low, high)):
                there = k_far.at[b, g, j, :, rows]
                pltpu.make_async_copy(there, there, k_sem.at[part, b, g, j]).wait()
            if b == 0:
                there = v_far.at[g, j]
                pltpu.make_async_copy(there, there, v_sem.at[g, j]).wait()

    def expo_of(b, g, t, k):
        at = g * plan.kt + t
        q = split_heads(plan, mixed[at, b])
        k_own = jnp.concatenate([mixed[at, 2 + h, mine[b]], planes[h][at, 0, mine[b]]], axis=0)
        return numerators(
            plan, facts, g, t, scores_of(q, k_own), [scores_of(q, k[j]) for j in range(NB)]
        )

    def keys(b, g):
        return [far_rows(plan, k_far.at[b], g, j) for j in range(NB)]

    def attended(g, t, ready):
        k, v = ready
        at = g * plan.kt + t
        expo = expo_of(0, g, t, k)
        total = weigh(expo[0], with_ones(planes[h][at, 1]))
        for j in range(NB):
            p = jnp.concatenate(expo[1 + j * plan.kt:1 + (j + 1) * plan.kt], axis=1)
            total += weigh(p, v[j])
        out[at, 0] = finish(plan, total)

    def scored(g, t, k):
        for i, part in enumerate(expo_of(1, g, t, k)):
            expo_ref[g * plan.kt + t, :, i * TILE:(i + 1) * TILE] = part

    each_view(
        plan, functools.partial(wait, 0), attended,
        lambda g: (keys(0, g), [with_ones(far_rows(plan, v_far, g, j)) for j in range(NB)]),
    )
    each_view(plan, functools.partial(wait, 1), scored, functools.partial(keys, 1))


def weigh_kernel(plan, own, other, slots, expo, done, *refs):
    n, h = plan.planes, plan.hops
    late = refs[:n]
    out, v_far, far_sem = refs[-3:]

    def stored(g, b):
        return slots[b, lax.axis_index("plane") * plan.sub + g]

    def far_copies(g, j, d, tiles_at):
        src = late[d].at[pl.ds(tiles_at, plan.kt), 0]
        return [pltpu.make_async_copy(src, v_far.at[g, j], far_sem.at[g, j])]

    start_far(plan, (own, other), far_copies)
    for g in range(plan.sub):
        for t in range(plan.kt):
            out[g * plan.kt + t, stored(g, 0)] = done[g * plan.kt + t, 0]

    def wait(g):
        for j in range(NB):
            there = v_far.at[g, j]
            pltpu.make_async_copy(there, there, far_sem.at[g, j]).wait()

    def one_tile(g, t, v):
        at = g * plan.kt + t
        wide = plan.kt * TILE
        total = weigh(expo[at, :, :TILE], with_ones(late[h][at, 0]))
        for j in range(NB):
            total += weigh(expo[at, :, TILE + j * wide:TILE + (j + 1) * wide], v[j])
        out[at, stored(g, 1)] = finish(plan, total)

    each_view(
        plan, wait, one_tile,
        lambda g: [with_ones(far_rows(plan, v_far, g, j)) for j in range(NB)],
    )


def call(kernel, name, out_shape, in_specs, out_specs, scratch, args, flops=0, exps=0, moved=0,
         mib=8):
    return pl.pallas_call(
        kernel,
        out_shape=out_shape,
        in_specs=in_specs,
        out_specs=out_specs,
        scratch_shapes=scratch,
        compiler_params=pltpu.CompilerParams(vmem_limit_bytes=mib * 2 ** 20),
        cost_estimate=pl.CostEstimate(flops=flops, bytes_accessed=moved, transcendentals=exps),
        name=name,
    )(*args)


def local(queries, keys, values, tile_mask, offsets, branch_slots):
    sub, toks = lax.axis_size("sub"), lax.axis_size("tok")
    ways = sub * toks
    dtype = queries.dtype
    _, _, tokens, width = queries.shape
    tiles, share = tokens // TILE, width // ways
    kt = toks * tiles
    hops = -(-REACH // sub)
    plan = Plan(sub, kt, hops, share)
    shifts = [d for d in range(-hops, hops + 1) if d]
    order = range(-hops, hops + 1)
    half = TILE // 2
    size = queries.size * 2

    slots = branch_slots.T
    own = jnp.concatenate([tile_mask.reshape(-1), offsets.reshape(-1)])
    other = own
    if sub == 2:
        other = lax.ppermute(own, "sub", [(0, 1), (1, 0)])
    facts = (own, other)

    place = ANY if plan.whole_lanes else VMEM
    sem = pltpu.SemaphoreType.DMA(())

    def pack(name, arrays, moves, pieces, staged=False, mark=None):
        staged = staged and plan.whole_lanes
        scratch = [sem]
        if staged:
            scratch.append(pltpu.VMEM((len(moves), tiles, TILE, width), dtype))
            scratch.append(pltpu.SemaphoreType.DMA((len(moves), tiles)))
        return call(
            functools.partial(pack_kernel, plan, moves, staged), name,
            jax.ShapeDtypeStruct((ways, tiles, pieces, TILE, share), dtype),
            [SMEM, ANY] + [ANY if staged else VMEM] * len(arrays), place, scratch,
            (slots, slots if mark is None else mark, *arrays), moved=pieces * size,
            mib=62 if staged else 8,
        )

    def spread(x):
        return exchange(x).reshape(ways * tiles, x.shape[2], TILE, share)

    def around(x, chain=False):
        found, last = {0: x}, ()
        for d in shifts:
            found[d] = from_plane(after(x, last), d)
            last = found[d] if chain else ()
        return found

    def mark(arrays, flops):
        return call(
            mark_kernel, "mark", jax.ShapeDtypeStruct((8, 128), jnp.float32),
            [ANY] * len(arrays), VMEM, [], arrays, flops=flops, mib=1,
        )

    raw = keys.reshape(1, 2, tiles, TILE, width)[:, :, :, :half].reshape(1, 2, tiles * half, width)
    raw = around(raw, chain=True)
    if plan.whole_lanes:
        packed = call(
            functools.partial(first_kernel, plan), "first",
            jax.ShapeDtypeStruct((ways, tiles, 3, TILE, share), dtype), [ANY] * 3, ANY,
            [pltpu.VMEM((4, tiles, TILE, width), dtype), pltpu.SMEM(slots.shape, jnp.int32),
             pltpu.SemaphoreType.DMA((4, tiles)), sem, sem],
            (slots, keys, values), moved=3 * size, mib=62,
        )
    else:
        packed = pack(
            "first", [keys, values],
            [Move(0, b, 0, row=half, rows=half, to=b * half) for b in range(2)]
            + [Move(1, b, 1 + b) for b in range(2)], 3,
        )
    early = spread(packed)
    arrived = mark([raw[d] for d in shifts], MARK_FLOPS[0])
    early, arrived, facts = lax.optimization_barrier((early, arrived, facts))

    heads, last_values = call(
        split_kernel, "split",
        tuple(jax.ShapeDtypeStruct((ways * tiles, n, TILE, share), dtype) for n in (2, 1)),
        [VMEM], (VMEM, VMEM), [], (early,), moved=size,
    )
    planes = around(heads)
    leads = mark([planes[shifts[0]]], MARK_FLOPS[1])
    brought = mark([planes[d] for d in shifts[1:]], MARK_FLOPS[2])
    last_values, leads = lax.optimization_barrier((last_values, leads))
    late = around(last_values)
    moves = [Move(0, 0, 0), Move(0, 1, 1)]
    for d in order:
        for b in range(2):
            moves.append(Move(
                1 + d + hops, b, 2 + d + hops, planes=d, rows=half, pitch=half, to=b * half
            ))
    packed = pack(
        "second", [queries, *[raw[d] for d in order]], moves, 2 + plan.planes, mark=arrived
    )
    mixed = spread(packed)
    planes = [planes[d] for d in order]
    late = [late[d] for d in order]

    def result(n):
        return jax.ShapeDtypeStruct((ways * tiles, n, TILE, share), dtype)

    sems = pltpu.SemaphoreType.DMA
    far = (sub, NB, kt, TILE, share)
    expo = jax.ShapeDtypeStruct((sub * kt, plan.rows, plan.cols), dtype)
    out0, expo = call(
        functools.partial(core_kernel, plan), "core", (result(1), expo),
        [SMEM] * 2 + [VMEM] + [ANY if d else VMEM for d in order] + [ANY] * 2, (VMEM, VMEM),
        [pltpu.VMEM((2, *far), dtype), pltpu.VMEM(far, dtype), sems((2, 2, sub, NB)),
         sems((sub, NB))],
        (*facts, mixed, *planes, leads, brought), flops=plan.pairs * HD * 6,
        exps=2 * plan.pairs, moved=2 * size, mib=12 if kt <= 4 else 32,
    )
    x = call(
        functools.partial(weigh_kernel, plan), "weigh", result(2),
        [SMEM] * 3 + [VMEM] * 2 + [ANY if d else VMEM for d in order], VMEM,
        [pltpu.VMEM(far, dtype), sems((sub, NB))], (*facts, slots, expo, out0, *late),
        flops=plan.pairs * HD * 2, moved=2 * size, mib=12,
    )
    x = exchange(x.reshape(ways, tiles, 2, TILE, share))
    return call(
        functools.partial(last_kernel, plan), "last",
        jax.ShapeDtypeStruct(queries.shape, dtype), [place], place, [sem], (x,),
        moved=2 * size,
    )


def solution(mesh):
    views, toks = mesh.shape["view"], mesh.shape["tok"]

    def run(queries, keys, values, tile_mask, offsets, branch_slots):
        heads = queries.shape[-1] // HD
        sub = 2 if views % 2 == 0 and heads % (2 * toks) == 0 else 1
        fine = Mesh(mesh.devices.reshape(views // sub, sub, toks), ("plane", "sub", "tok"))
        view = ("plane", "sub")
        shard = P(view, None, "tok", None)
        in_specs = (shard, shard, shard, P(view, None, None, None), P(view, None), P())
        return jax.shard_map(
            local, mesh=fine, in_specs=in_specs, out_specs=shard, check_vma=False
        )(queries, keys, values, tile_mask, offsets, branch_slots)

    return run
```

```python
import functools
import math

import jax
import jax.numpy as jnp
from jax import lax
from jax.experimental import pallas as pl
from jax.experimental.pallas import tpu as pltpu
from jax.sharding import Mesh, PartitionSpec as P

HD = 64
TILE = 128
NB = 2
REACH = 2
MARK_FLOPS = (4 * 10 ** 9, 2 * 10 ** 9, 10 ** 10)
GROUP = ("sub", "tok")

NEG_SCORE = -1e30

SMEM = pl.BlockSpec(memory_space=pltpu.SMEM)
VMEM = pl.BlockSpec(memory_space=pltpu.VMEM)
ANY = pl.BlockSpec(memory_space=pl.ANY)


def after(x, *others):
    return lax.optimization_barrier((x, others))[0]


def from_plane(x, by):
    size = lax.axis_size("plane")
    return lax.ppermute(x, "plane", [((i + by) % size, i) for i in range(size)])


def exchange(x):
    return lax.all_to_all(x, GROUP, split_axis=0, concat_axis=0, tiled=True)


class Move:
    def __init__(self, array, branch, piece, planes=0, row=0, rows=TILE, pitch=TILE, to=0):
        self.array, self.branch, self.piece, self.planes = array, branch, piece, planes
        self.row, self.rows, self.pitch, self.to = row, rows, pitch, to


def slot_of(plan, slots_ref, planes, branch):
    views = slots_ref.shape[1]
    view = (lax.axis_index("plane") + planes) * plan.sub + lax.axis_index("sub") + views
    return slots_ref[branch, lax.rem(view, views)]


def pack_kernel(plan, moves, staged, slots_ref, mark_ref, *refs):
    if staged:
        *ins, out, sem, stage, stage_sem = refs
    else:
        *ins, out, sem = refs
    ways, tiles, _, _, share = out.shape
    sources = []
    for i, move in enumerate(moves):
        slot = slot_of(plan, slots_ref, move.planes, move.branch)
        for m in range(tiles):
            rows = pl.ds(m * move.pitch + move.row, move.rows)
            source = ins[move.array].at[0, slot, rows]
            if staged:
                there = stage.at[i, m, pl.ds(0, move.rows)]
                copy = pltpu.make_async_copy(source, there, stage_sem.at[i, m])
                copy.start()
                sources.append((move, m, there, copy))
            else:
                sources.append((move, m, source, None))
    for move, m, source, copy in sources:
        if copy is not None:
            copy.wait()
        for w in range(ways):
            to, lanes = pl.ds(move.to, move.rows), pl.ds(w * share, share)
            if plan.whole_lanes:
                pltpu.make_async_copy(
                    source.at[:, lanes], out.at[w, m, move.piece, to], sem
                ).start()
            else:
                out[w, m, move.piece, to] = source[:, lanes]
    if plan.whole_lanes:
        pltpu.make_async_copy(out, out, sem).wait()


def first_kernel(plan, slots_ref, keys, values, out, stage, slots, stage_sem, slots_sem, sem):
    ways, tiles, _, _, share = out.shape
    half = TILE // 2
    ask = pltpu.make_async_copy(slots_ref, slots, slots_sem)
    ask.start()
    fetched = []
    for i, (src, row, rows) in enumerate(((keys, half, half), (values, 0, TILE))):
        for s in range(2):
            for m in range(tiles):
                there = stage.at[2 * i + s, m, pl.ds(0, rows)]
                copies = [
                    pltpu.make_async_copy(
                        src.at[0, s, pl.ds(m * TILE + row + at, rows // 2)],
                        there.at[pl.ds(at, rows // 2)], stage_sem.at[2 * i + s, m, k],
                    ) for k, at in enumerate((0, rows // 2))
                ]
                for copy in copies:
                    copy.start()
                fetched.append((i, s, m, there, copies))
    ask.wait()
    view = lax.axis_index("plane") * plan.sub + lax.axis_index("sub")
    lead = slots[0, view]
    for i, s, m, there, copies in fetched:
        branch = jnp.where(lead == s, 0, 1)
        for copy in copies:
            copy.wait()
        for w in range(ways):
            if i == 0:
                to = out.at[w, m, 0, pl.ds(pl.multiple_of(branch * half, half), half)]
            else:
                to = out.at[w, m, 1 + branch]
            pltpu.make_async_copy(there.at[:, pl.ds(w * share, share)], to, sem).start()
    pltpu.make_async_copy(out, out, sem).wait()


def split_kernel(x, head, tail):
    pieces = head.shape[1]
    head[...] = x[:, :pieces]
    tail[...] = x[:, pieces:]


def last_kernel(plan, x, out, sem):
    ways, tiles, slots, _, share = x.shape
    for s in range(slots):
        for m in range(tiles):
            for w in range(ways):
                rows, lanes = pl.ds(m * TILE, TILE), pl.ds(w * share, share)
                if plan.whole_lanes:
                    pltpu.make_async_copy(x.at[w, m, s], out.at[0, s, rows, lanes], sem).start()
                else:
                    out[0, s, rows, lanes] = x[w, m, s]
    if plan.whole_lanes:
        pltpu.make_async_copy(out, out, sem).wait()


class Plan:
    def __init__(self, sub, kt, hops, share):
        self.sub, self.kt, self.hops, self.share = sub, kt, hops, share
        self.planes = 2 * hops + 1
        self.heads = share // HD
        self.rows = self.heads * TILE
        self.cols = (1 + NB * kt) * TILE
        self.pairs = sub * kt * self.rows * self.cols
        self.whole_lanes = share % 128 == 0


def fact(plan, facts, g, i):
    own_ref, other_ref = facts
    if plan.sub == 1:
        return own_ref[i]
    return jnp.where(lax.axis_index("sub") == g, own_ref[i], other_ref[i])


def start_far(plan, facts, copies_of):
    for g in range(plan.sub):
        for j in range(NB):
            at = fact(plan, facts, g, NB * plan.kt * plan.kt + j) + (plan.hops * plan.sub + g)
            tiles_at = (at & (plan.sub - 1)) * plan.kt
            for d in range(plan.planes):
                @pl.when((at >> (plan.sub - 1)) == d)
                def _():
                    for copy in copies_of(g, j, d, tiles_at):
                        copy.start()


def mark_kernel(*refs):
    refs[-1][...] = jnp.zeros_like(refs[-1])


def head_of_lane(plan):
    return lax.broadcasted_iota(jnp.int32, (TILE, plan.share), 1) // HD


def split_heads(plan, q):
    if plan.heads == 1:
        return q
    block = head_of_lane(plan)
    return jnp.concatenate([jnp.where(block == h, q, 0) for h in range(plan.heads)], axis=0)


def scores_of(q, k):
    return lax.dot_general(q, k, (((1,), (1,)), ((), ())), preferred_element_type=jnp.float32)


def numerators(plan, facts, g, t, own, far):
    factor = HD ** -0.5 * math.log2(math.e)
    parts = [own]
    for j in range(NB):
        for k in range(plan.kt):
            keep = fact(plan, facts, g, (j * plan.kt + t) * plan.kt + k) == 1
            bias = jnp.where(keep, 0.0, NEG_SCORE)
            parts.append(far[j][:, k * TILE:(k + 1) * TILE] + bias)
    top = functools.reduce(jnp.maximum, parts)
    top = jnp.max(top, axis=1, keepdims=True) * factor
    return [jnp.exp2(part * factor - top).astype(jnp.bfloat16) for part in parts]


def with_ones(v):
    return jnp.concatenate([v, jnp.ones_like(v)], axis=1)


def weigh(p, v):
    return jnp.dot(p, v, preferred_element_type=jnp.float32)


def finish(plan, total):
    result = total[:TILE]
    block = head_of_lane(plan)
    both = jnp.concatenate([block, block], axis=1)
    for h in range(1, plan.heads):
        result = jnp.where(both == h, total[h * TILE:(h + 1) * TILE], result)
    return (result[:, :plan.share] / result[:, plan.share:]).astype(jnp.bfloat16)


def far_rows(plan, buffer, g, j):
    return buffer[g, j].reshape(plan.kt * TILE, plan.share)


def each_view(plan, wait, one_tile, prepare):
    count = math.gcd(plan.kt, 4)

    def some_tiles(g, t0):
        ready = prepare(g)
        for i in range(count):
            one_tile(g, t0 + i, ready)

    def one_view(g, carry):
        wait(g)
        if count == plan.kt:
            some_tiles(g, 0)
        else:
            def some(i, c):
                some_tiles(g, i * count)
                return c
            lax.fori_loop(0, plan.kt // count, some, 0)
        return carry

    lax.fori_loop(0, plan.sub, one_view, 0)


def core_kernel(plan, own, other, mixed, *refs):
    n, h = plan.planes, plan.hops
    planes = refs[:n]
    out, expo_ref, k_far, v_far, k_sem, v_sem = refs[-6:]
    facts = (own, other)
    half = TILE // 2
    low, high = pl.ds(0, half), pl.ds(half, half)
    mine = [pl.ds(b * half, half) for b in range(2)]

    def far_copies(b, g, j, d, tiles_at):
        tiles = pl.ds(tiles_at, plan.kt)
        to, sem = k_far.at[b, g, j], k_sem.at[:, b, g, j]
        found = [
            (mixed.at[tiles, 2 + d, mine[b]], to.at[:, low], sem.at[0]),
            (planes[d].at[tiles, 0, mine[b]], to.at[:, high], sem.at[1]),
        ]
        if b == 0:
            found.append((planes[d].at[tiles, 1], v_far.at[g, j], v_sem.at[g, j]))
        return [pltpu.make_async_copy(*copy) for copy in found]

    for b in range(2):
        start_far(plan, facts, functools.partial(far_copies, b))

    def wait(b, g):
        for j in range(NB):
            for part, rows in enumerate((low, high)):
                there = k_far.at[b, g, j, :, rows]
                pltpu.make_async_copy(there, there, k_sem.at[part, b, g, j]).wait()
            if b == 0:
                there = v_far.at[g, j]
                pltpu.make_async_copy(there, there, v_sem.at[g, j]).wait()

    def expo_of(b, g, t, k):
        at = g * plan.kt + t
        q = split_heads(plan, mixed[at, b])
        k_own = jnp.concatenate([mixed[at, 2 + h, mine[b]], planes[h][at, 0, mine[b]]], axis=0)
        return numerators(
            plan, facts, g, t, scores_of(q, k_own), [scores_of(q, k[j]) for j in range(NB)]
        )

    def keys(b, g):
        return [far_rows(plan, k_far.at[b], g, j) for j in range(NB)]

    def attended(g, t, ready):
        k, v = ready
        at = g * plan.kt + t
        expo = expo_of(0, g, t, k)
        total = weigh(expo[0], with_ones(planes[h][at, 1]))
        for j in range(NB):
            p = jnp.concatenate(expo[1 + j * plan.kt:1 + (j + 1) * plan.kt], axis=1)
            total += weigh(p, v[j])
        out[at, 0] = finish(plan, total)

    def scored(g, t, k):
        for i, part in enumerate(expo_of(1, g, t, k)):
            expo_ref[g * plan.kt + t, :, i * TILE:(i + 1) * TILE] = part

    each_view(
        plan, functools.partial(wait, 0), attended,
        lambda g: (keys(0, g), [with_ones(far_rows(plan, v_far, g, j)) for j in range(NB)]),
    )
    each_view(plan, functools.partial(wait, 1), scored, functools.partial(keys, 1))


def weigh_kernel(plan, own, other, slots, expo, done, *refs):
    n, h = plan.planes, plan.hops
    late = refs[:n]
    out, v_far, far_sem = refs[-3:]

    def stored(g, b):
        return slots[b, lax.axis_index("plane") * plan.sub + g]

    def far_copies(g, j, d, tiles_at):
        src = late[d].at[pl.ds(tiles_at, plan.kt), 0]
        return [pltpu.make_async_copy(src, v_far.at[g, j], far_sem.at[g, j])]

    start_far(plan, (own, other), far_copies)
    for g in range(plan.sub):
        for t in range(plan.kt):
            out[g * plan.kt + t, stored(g, 0)] = done[g * plan.kt + t, 0]

    def wait(g):
        for j in range(NB):
            there = v_far.at[g, j]
            pltpu.make_async_copy(there, there, far_sem.at[g, j]).wait()

    def one_tile(g, t, v):
        at = g * plan.kt + t
        wide = plan.kt * TILE
        total = weigh(expo[at, :, :TILE], with_ones(late[h][at, 0]))
        for j in range(NB):
            total += weigh(expo[at, :, TILE + j * wide:TILE + (j + 1) * wide], v[j])
        out[at, stored(g, 1)] = finish(plan, total)

    each_view(
        plan, wait, one_tile,
        lambda g: [with_ones(far_rows(plan, v_far, g, j)) for j in range(NB)],
    )


def call(kernel, name, out_shape, in_specs, out_specs, scratch, args, flops=0, exps=0, moved=0,
         mib=8):
    return pl.pallas_call(
        kernel,
        out_shape=out_shape,
        in_specs=in_specs,
        out_specs=out_specs,
        scratch_shapes=scratch,
        compiler_params=pltpu.CompilerParams(vmem_limit_bytes=mib * 2 ** 20),
        cost_estimate=pl.CostEstimate(flops=flops, bytes_accessed=moved, transcendentals=exps),
        name=name,
    )(*args)


def local(queries, keys, values, tile_mask, offsets, branch_slots):
    sub, toks = lax.axis_size("sub"), lax.axis_size("tok")
    ways = sub * toks
    dtype = queries.dtype
    _, _, tokens, width = queries.shape
    tiles, share = tokens // TILE, width // ways
    kt = toks * tiles
    hops = -(-REACH // sub)
    plan = Plan(sub, kt, hops, share)
    shifts = [d for d in range(-hops, hops + 1) if d]
    order = range(-hops, hops + 1)
    half = TILE // 2
    size = queries.size * 2

    slots = branch_slots.T
    own = jnp.concatenate([tile_mask.reshape(-1), offsets.reshape(-1)])
    other = own
    if sub == 2:
        other = lax.ppermute(own, "sub", [(0, 1), (1, 0)])
    facts = (own, other)

    place = ANY if plan.whole_lanes else VMEM
    sem = pltpu.SemaphoreType.DMA(())

    def pack(name, arrays, moves, pieces, staged=False, mark=None):
        staged = staged and plan.whole_lanes
        scratch = [sem]
        if staged:
            scratch.append(pltpu.VMEM((len(moves), tiles, TILE, width), dtype))
            scratch.append(pltpu.SemaphoreType.DMA((len(moves), tiles)))
        return call(
            functools.partial(pack_kernel, plan, moves, staged), name,
            jax.ShapeDtypeStruct((ways, tiles, pieces, TILE, share), dtype),
            [SMEM, ANY] + [ANY if staged else VMEM] * len(arrays), place, scratch,
            (slots, slots if mark is None else mark, *arrays), moved=pieces * size,
            mib=62 if staged else 8,
        )

    def spread(x):
        return exchange(x).reshape(ways * tiles, x.shape[2], TILE, share)

    def around(x, chain=False):
        found, last = {0: x}, ()
        for d in shifts:
            found[d] = from_plane(after(x, last), d)
            last = found[d] if chain else ()
        return found

    def mark(arrays, flops):
        return call(
            mark_kernel, "mark", jax.ShapeDtypeStruct((8, 128), jnp.float32),
            [ANY] * len(arrays), VMEM, [], arrays, flops=flops, mib=1,
        )

    raw = keys.reshape(1, 2, tiles, TILE, width)[:, :, :, :half].reshape(1, 2, tiles * half, width)
    raw = around(raw, chain=True)
    if plan.whole_lanes:
        packed = call(
            functools.partial(first_kernel, plan), "first",
            jax.ShapeDtypeStruct((ways, tiles, 3, TILE, share), dtype), [ANY] * 3, ANY,
            [pltpu.VMEM((4, tiles, TILE, width), dtype), pltpu.SMEM(slots.shape, jnp.int32),
             pltpu.SemaphoreType.DMA((4, tiles, 2)), sem, sem],
            (slots, keys, values), moved=3 * size, mib=62,
        )
    else:
        packed = pack(
            "first", [keys, values],
            [Move(0, b, 0, row=half, rows=half, to=b * half) for b in range(2)]
            + [Move(1, b, 1 + b) for b in range(2)], 3,
        )
    early = spread(packed)
    arrived = mark([raw[d] for d in shifts], MARK_FLOPS[0])
    early, arrived, facts = lax.optimization_barrier((early, arrived, facts))

    heads, last_values = call(
        split_kernel, "split",
        tuple(jax.ShapeDtypeStruct((ways * tiles, n, TILE, share), dtype) for n in (2, 1)),
        [VMEM], (VMEM, VMEM), [], (early,), moved=size,
    )
    planes = around(heads)
    leads = mark([planes[shifts[0]]], MARK_FLOPS[1])
    brought = mark([planes[d] for d in shifts[1:]], MARK_FLOPS[2])
    last_values, leads = lax.optimization_barrier((last_values, leads))
    late = around(last_values)
    moves = [Move(0, 0, 0), Move(0, 1, 1)]
    for d in order:
        for b in range(2):
            moves.append(Move(
                1 + d + hops, b, 2 + d + hops, planes=d, rows=half, pitch=half, to=b * half
            ))
    packed = pack(
        "second", [queries, *[raw[d] for d in order]], moves, 2 + plan.planes, mark=arrived
    )
    mixed = spread(packed)
    planes = [planes[d] for d in order]
    late = [late[d] for d in order]

    def result(n):
        return jax.ShapeDtypeStruct((ways * tiles, n, TILE, share), dtype)

    sems = pltpu.SemaphoreType.DMA
    far = (sub, NB, kt, TILE, share)
    expo = jax.ShapeDtypeStruct((sub * kt, plan.rows, plan.cols), dtype)
    out0, expo = call(
        functools.partial(core_kernel, plan), "core", (result(1), expo),
        [SMEM] * 2 + [VMEM] + [ANY if d else VMEM for d in order] + [ANY] * 2, (VMEM, VMEM),
        [pltpu.VMEM((2, *far), dtype), pltpu.VMEM(far, dtype), sems((2, 2, sub, NB)),
         sems((sub, NB))],
        (*facts, mixed, *planes, leads, brought), flops=plan.pairs * HD * 6,
        exps=2 * plan.pairs, moved=2 * size, mib=12 if kt <= 4 else 32,
    )
    x = call(
        functools.partial(weigh_kernel, plan), "weigh", result(2),
        [SMEM] * 3 + [VMEM] * 2 + [ANY if d else VMEM for d in order], VMEM,
        [pltpu.VMEM(far, dtype), sems((sub, NB))], (*facts, slots, expo, out0, *late),
        flops=plan.pairs * HD * 2, moved=2 * size, mib=12,
    )
    x = exchange(x.reshape(ways, tiles, 2, TILE, share))
    return call(
        functools.partial(last_kernel, plan), "last",
        jax.ShapeDtypeStruct(queries.shape, dtype), [place], place, [sem], (x,),
        moved=2 * size,
    )


def solution(mesh):
    views, toks = mesh.shape["view"], mesh.shape["tok"]

    def run(queries, keys, values, tile_mask, offsets, branch_slots):
        heads = queries.shape[-1] // HD
        sub = 2 if views % 2 == 0 and heads % (2 * toks) == 0 else 1
        fine = Mesh(mesh.devices.reshape(views // sub, sub, toks), ("plane", "sub", "tok"))
        view = ("plane", "sub")
        shard = P(view, None, "tok", None)
        in_specs = (shard, shard, shard, P(view, None, None, None), P(view, None), P())
        return jax.shard_map(
            local, mesh=fine, in_specs=in_specs, out_specs=shard, check_vma=False
        )(queries, keys, values, tile_mask, offsets, branch_slots)

    return run
```
